256 devices in a mesh: ctx: 32 (over x, z), tp: 8 (over y, core).
Axes of the slice: x: 4, y: 4, z: 8, core: 2. Of those that a mesh axis runs over, the one named last changes fastest.
Arguments:
- tokens: bfloat16 [16384, 4096], P(('ctx', 'tp')), may hold values from -6 to 6
- in_x: bfloat16 [4096, 4096], P(None, 'tp'), may hold values from -0.09375 to 0.09375
- in_bc: bfloat16 [4096, 256], replicated, may hold values from -0.09375 to 0.09375
- in_dt: bfloat16 [4096, 64], P(None, 'tp'), may hold values from -0.09375 to 0.09375
- conv_x: float32 [4, 4096], P(None, 'tp'), may hold values from -3 to 3
- conv_bc: float32 [4, 256], replicated, may hold values from -3 to 3
- dt_bias: float32 [64], P('tp'), may hold values from -7.5 to -3.5
- a_log: float32 [64], P('tp'), may hold values from -4.61 to 0.41
- skip_d: float32 [64], P('tp'), may hold values from 0.5 to 1.5
- norm_gain: float32 [4096], P('tp'), may hold values from 0.1 to 1.9
- out_w: bfloat16 [4096, 4096], P('tp'), may hold values from -0.09375 to 0.09375
Outputs:
- mixed: bfloat16 [16384, 4096], P(('ctx', 'tp'))
The draws below stay inside these ranges and needn't reach their ends.
All inputs are finite; a program needn't handle non-finite values.
Results may differ from the reference program's by a relative error of at most 0.019.
Values may be sent and summed in bfloat16 or wider, within the bound.
No kernel may reach another device: no remote copies, remote signals or barrier semaphores. Data moves between devices by JAX's collectives and lax.ppermute only.
A program may use at most 64 MiB of HBM per device.

```python
import math
import jax
import jax.numpy as jnp
from jax import lax

D = 4096
HEADS = 64
HEAD_DIM = 64
STATE = 128
CONV = 4
BLOCK = 256
INNER = 4096
TOKENS = 16384


def head_kinds(key):
    pick_key = jax.random.fold_in(key, 11)
    share = 0.5
    return jax.random.uniform(pick_key, (HEADS,), jnp.float32) < share


def draw_a_log(key, part):
    fast = head_kinds(key)
    fast_key = jax.random.fold_in(key, 12)
    slow_key = jax.random.fold_in(key, 13)
    fast_vals = jax.random.uniform(fast_key, (HEADS,), jnp.float32, math.log(0.5), math.log(1.5))
    slow_vals = jax.random.uniform(slow_key, (HEADS,), jnp.float32, math.log(0.01), math.log(0.03))
    return jnp.where(fast, fast_vals, slow_vals).astype(jnp.float32)


def draw_dt_bias(key, part):
    fast = head_kinds(key)
    fast_key = jax.random.fold_in(key, 14)
    slow_key = jax.random.fold_in(key, 15)
    fast_vals = jax.random.uniform(fast_key, (HEADS,), jnp.float32, -4.5, -3.5)
    slow_vals = jax.random.uniform(slow_key, (HEADS,), jnp.float32, -7.5, -6.9)
    return jnp.where(fast, fast_vals, slow_vals).astype(jnp.float32)


def level_of(rng, dims, cuts, least, largest):
    def one(axis_at, parts):
        steps = jax.random.uniform(jax.random.fold_in(jax.random.fold_in(rng, 6), axis_at), (parts,), jnp.float32, least / len(cuts), largest / len(cuts))
        return jnp.repeat(jnp.exp(steps), dims[axis_at] // parts).reshape((-1,) + (1,) * (len(dims) - axis_at - 1))

    gain = one(*cuts[0])
    for cut in cuts[1:]:
        gain = gain * one(*cut)
    return gain


def bell_draw(stream_key, extent, deviation, most, shards=(), dtype=jnp.bfloat16):
    array = jax.random.normal(stream_key, extent, jnp.float32) * deviation
    if len(shards) > 0:
        array = level_of(stream_key, extent, shards, -0.22, 0.18) * array
    return jnp.clip(array, min=-most, max=most).astype(dtype)


def setup_inputs(seed: int = 0) -> dict:
    seeds = jax.random.split(jax.random.key(seed), 12)
    return {
        "tokens": bell_draw(seeds[0], (TOKENS, D), 1.0, 6.0, ((0, 256),)),
        "in_x": bell_draw(seeds[1], (D, INNER), D ** -0.5, 0.09375, ((1, 8),)),
        "in_bc": bell_draw(seeds[2], (D, 2 * STATE), D ** -0.5, 0.09375),
        "in_dt": bell_draw(seeds[3], (D, HEADS), D ** -0.5, 0.09375, ((1, 8),)),
        "conv_x": bell_draw(seeds[4], (CONV, INNER), CONV ** -0.5, 3.0, ((1, 8),), jnp.float32),
        "conv_bc": bell_draw(seeds[5], (CONV, 2 * STATE), CONV ** -0.5, 3.0, (), jnp.float32),
        "dt_bias": draw_dt_bias(jax.random.fold_in(seeds[11], 71), 0),
        "a_log": draw_a_log(jax.random.fold_in(seeds[11], 71), 0),
        "skip_d": jnp.clip(0.5 + 1.0 * jax.random.uniform(seeds[8], (HEADS,), jnp.float32) ** level_of(seeds[8], (HEADS,), ((0, 8),), -0.2, 0.2), 0.5, 1.5),
        "norm_gain": jnp.clip(1.0 + 0.18 * jax.random.normal(seeds[9], (INNER,), jnp.float32), 0.1, 1.9),
        "out_w": bell_draw(seeds[10], (INNER, D), INNER ** -0.5, 0.09375, ((0, 8),)),
    }


def causal_conv(prev, cur, kernel):
    ext = jnp.concatenate([prev, cur], 0).astype(jnp.float32)
    rows = cur.shape[0]
    taps = kernel.shape[0]
    total = kernel[0][None, :] * ext[0:rows]
    for k in range(1, taps):
        total = total + kernel[k][None, :] * ext[k:k + rows]
    return jax.nn.silu(total)

def ssd_block(state, xb, bb, cb, lab, dtb):
    hi = lax.Precision.HIGHEST
    length = lab.shape[0]
    cs = jnp.cumsum(lab, axis=0)
    scores = jnp.dot(cb, bb.T, precision=hi)
    diff = cs[:, None, :] - cs[None, :, :]
    later = lax.broadcasted_iota(jnp.int32, (length, length), 0)
    earlier = lax.broadcasted_iota(jnp.int32, (length, length), 1)
    tri = (later >= earlier)[:, :, None]
    decay = jnp.exp(jnp.where(tri, diff, -jnp.inf))
    xdt = xb * dtb[:, :, None]
    weighted = scores[:, :, None] * decay
    y_in = jnp.einsum('tsh,shp->thp', weighted, xdt, precision=hi)
    y_st = jnp.exp(cs)[:, :, None] * jnp.einsum('tn,hpn->thp', cb, state, precision=hi)
    tail = jnp.exp(cs[-1][None, :] - cs)
    fresh = jnp.einsum('shp,sn->hpn', xdt * tail[:, :, None], bb, precision=hi)
    new_state = jnp.exp(cs[-1])[:, None, None] * state + fresh
    return (new_state, y_in + y_st)

def reference(tokens, in_x, in_bc, in_dt, conv_x, conv_bc, dt_bias, a_log, skip_d, norm_gain, out_w):
    x_raw = jnp.dot(tokens, in_x, preferred_element_type=jnp.float32).astype(jnp.bfloat16)
    bc_raw = jnp.dot(tokens, in_bc, preferred_element_type=jnp.float32).astype(jnp.bfloat16)
    dt_raw = jnp.dot(tokens, in_dt, preferred_element_type=jnp.float32)
    x_conv = causal_conv(jnp.zeros((CONV - 1, INNER), jnp.bfloat16), x_raw, conv_x)
    bc_conv = causal_conv(jnp.zeros((CONV - 1, 2 * STATE), jnp.bfloat16), bc_raw, conv_bc)
    b_all = bc_conv[:, :STATE]
    c_all = bc_conv[:, STATE:]
    step_dt = jax.nn.softplus(dt_raw + dt_bias[None, :])
    log_decay = -jnp.exp(a_log)[None, :] * step_dt
    blocks = TOKENS // BLOCK
    x_heads = x_conv.reshape(blocks, BLOCK, HEADS, HEAD_DIM)

    def scan_step(state, inputs):
        xb, bb, cb, lab, dtb = inputs
        return ssd_block(state, xb, bb, cb, lab, dtb)
    start = jnp.zeros((HEADS, HEAD_DIM, STATE), jnp.float32)
    final, y_blocks = lax.scan(scan_step, start, (x_heads, b_all.reshape(blocks, BLOCK, STATE), c_all.reshape(blocks, BLOCK, STATE), log_decay.reshape(blocks, BLOCK, HEADS), step_dt.reshape(blocks, BLOCK, HEADS)))
    x_flat = x_conv.reshape(TOKENS, HEADS, HEAD_DIM)
    y_all = y_blocks.reshape(TOKENS, HEADS, HEAD_DIM) + skip_d[None, :, None] * x_flat
    mean_sq = lax.optimization_barrier(jnp.mean(y_all * y_all, axis=-1, keepdims=True))
    normed = (y_all * lax.rsqrt(mean_sq + 1e-05) * norm_gain.reshape(HEADS, HEAD_DIM)[None]).reshape(TOKENS, INNER).astype(jnp.bfloat16)
    return jnp.dot(normed, out_w, preferred_element_type=jnp.float32).astype(jnp.bfloat16)
```

```python
import functools

import jax
import jax.numpy as jnp
from jax import lax
from jax.experimental import pallas as pl
from jax.experimental.pallas import tpu as pltpu
from jax.sharding import PartitionSpec as P

BF = jnp.bfloat16
F32 = jnp.float32
VMEM = pl.BlockSpec(memory_space=pltpu.VMEM)
SMEM = pl.BlockSpec(memory_space=pltpu.SMEM)
LIMIT = 56 * 1024 * 1024

Q = 128
NQ = 4
HH = 8
HD = 64
NS = 128
CH = 512
BCW = 256


def params():
    return pltpu.CompilerParams(vmem_limit_bytes=LIMIT)


def dot_tn(a, b):
    return lax.dot_general(a, b, (((0,), (0,)), ((), ())), preferred_element_type=F32)


def dot_nt(a, b):
    return lax.dot_general(a, b, (((1,), (1,)), ((), ())), preferred_element_type=F32)


def two_parts(v):
    hi = v.astype(BF)
    return hi, (v - hi.astype(F32)).astype(BF)


def head_spread():
    row = lax.broadcasted_iota(jnp.int32, (2 * HH, CH), 0)
    lane = lax.broadcasted_iota(jnp.int32, (2 * HH, CH), 1)
    return jnp.where(lane // HD == row % HH, 1.0, 0.0).astype(BF)


def spread(v, ones):
    hi, lo = two_parts(v)
    both = jnp.concatenate([hi.astype(F32), lo.astype(F32)], 0).astype(BF)
    return dot_tn(both, ones)


def project_kernel(n_own, idx, *refs):
    own, other = refs[:n_own], refs[n_own : 2 * n_own]
    wx, wbc, wdt, xo, bco, dto, tok = refs[2 * n_own :]
    core = idx[1]
    for group, half in ((own, core), (other, 1 - core)):
        at = half * 64
        step = 64 // n_own
        for j, r in enumerate(group):
            tok[pl.ds(pl.multiple_of(at + j * step, step), step), :] = r[...]
    rows = tok[...]
    xo[...] = jnp.dot(rows, wx[...], preferred_element_type=F32).astype(BF)
    bco[...] = jnp.dot(rows, wbc[...], preferred_element_type=F32).astype(BF)
    dt = jnp.dot(rows, wdt[...], preferred_element_type=F32)
    dto[...] = dt.T


def project(idx, own, other, in_x, in_bc, in_dt, name):
    n_own = len(own)
    return pl.pallas_call(
        functools.partial(project_kernel, n_own),
        out_shape=(
            jax.ShapeDtypeStruct((Q, CH), BF),
            jax.ShapeDtypeStruct((Q, BCW), BF),
            jax.ShapeDtypeStruct((HH, Q), F32),
        ),
        in_specs=[SMEM] + [VMEM] * (2 * n_own + 3),
        out_specs=(VMEM, VMEM, VMEM),
        scratch_shapes=[pltpu.VMEM((Q, 4096), BF)],
        compiler_params=params(),
        name=name,
    )(idx, *own, *other, in_x, in_bc, in_dt)


def silu(v):
    return v / (1.0 + jnp.exp(-v))


def softplus(v):
    return jnp.maximum(v, 0.0) + jnp.log1p(jnp.exp(-jnp.abs(v)))


OFFS = (0, 3, 1, 2)


def local_kernel(idx, *refs):
    xs, bcs, dts = refs[0:4], refs[4:8], refs[8:12]
    (hx, hbc, kx, kbc, bias, alog) = refs[12:18]
    (xo, bo, co, cso, dto, eo, do, send) = refs[18:26]
    ext, extb, dtr = refs[26:29]
    y = idx[0]
    keep = idx[2].astype(F32)
    ext[0:8, :] = hx[...].astype(F32) * keep
    extb[0:8, :] = hbc[...].astype(F32) * keep
    for k in range(4):
        a = lax.rem(y + OFFS[k], NQ)
        at = pl.multiple_of(a * Q + 8, 8)
        ext[pl.ds(at, Q), :] = xs[k][...].astype(F32)
        extb[pl.ds(at, Q), :] = bcs[k][...].astype(F32)
        dtr[a] = dts[k][...]
    ones = head_spread()
    lane = lax.broadcasted_iota(jnp.int32, (HH, Q), 1)
    decay = -jnp.exp(alog[...])
    total = jnp.zeros((HH, Q), F32)
    state = jnp.zeros((NS, CH), F32)
    for a in range(NQ):
        dt = softplus(dtr[a] + bias[...])
        cs = decay * dt
        for s in (1, 2, 4, 8, 16, 32, 64):
            cs = cs + jnp.where(lane >= s, pltpu.roll(cs, s, 1), 0.0)
        end = jnp.broadcast_to(cs[:, Q - 1 : Q], (HH, Q))
        dto[a] = dt
        cso[a] = cs
        total = total + end
        v = kbc[0:1, :] * extb[a * Q + 5 : a * Q + 5 + Q, :]
        for j in range(1, 4):
            v = v + kbc[j : j + 1, :] * extb[a * Q + 5 + j : a * Q + 5 + j + Q, :]
        bc = silu(v).astype(BF)
        b = bc[:, :NS]
        bo[a] = b
        co[a] = bc[:, NS:]
        v = kx[0:1, :] * ext[a * Q + 5 : a * Q + 5 + Q, :]
        for j in range(1, 4):
            v = v + kx[j : j + 1, :] * ext[a * Q + 5 + j : a * Q + 5 + j + Q, :]
        x = silu(v)
        xo[a] = x.astype(BF)
        w = spread(dt * jnp.exp(end - cs), ones)
        e = dot_tn(b, (x * w).astype(BF))
        eo[a] = e
        d = spread(jnp.exp(end), ones)[0:8, :]
        do[a] = d
        state = state * d[0:1, :] + e
    st = state.T
    dec = jnp.exp(total)
    hi = dec.astype(BF).astype(F32)
    mid = (dec - hi).astype(BF).astype(F32)
    low = dec - hi - mid
    row = lax.broadcasted_iota(jnp.int32, (HH, Q), 0)
    for h in range(HH):
        p = lambda t: jnp.broadcast_to(t[h : h + 1, :], (8, Q))
        tail = jnp.where(row == 0, p(hi), jnp.where(row == 1, p(mid), jnp.where(row == 2, p(low), 0.0)))
        for q in range(4):
            d = h * 4 + q
            send[d] = jnp.concatenate([st[16 * d : 16 * d + 16, :], tail], 0).astype(BF)


def local_part(idx, xs, bcs, dts, hx, hbc, kx, kbc, bias, alog):
    s = jax.ShapeDtypeStruct
    return pl.pallas_call(
        local_kernel,
        out_shape=(
            s((NQ, Q, CH), BF),
            s((NQ, Q, NS), BF),
            s((NQ, Q, NS), BF),
            s((NQ, HH, Q), F32),
            s((NQ, HH, Q), F32),
            s((NQ, NS, CH), F32),
            s((NQ, 8, CH), F32),
            s((32, 24, 128), BF),
        ),
        in_specs=[SMEM] + [VMEM] * 18,
        out_specs=(VMEM,) * 8,
        scratch_shapes=[
            pltpu.VMEM((8 + NQ * Q, CH), F32),
            pltpu.VMEM((8 + NQ * Q, BCW), F32),
            pltpu.VMEM((NQ, HH, Q), F32),
        ],
        compiler_params=params(),
        name="local_part",
    )(idx, *xs, *bcs, *dts, hx, hbc, kx, kbc, bias, alog)


def prefix_kernel(r, o):
    s = jnp.zeros((16, 128), F32)
    for j in range(32):
        o[j] = s.astype(BF)
        v = r[j].astype(F32)
        s = s * (v[16:17] + v[17:18] + v[18:19]) + v[0:16]


def prefix(r):
    return pl.pallas_call(
        prefix_kernel,
        out_shape=jax.ShapeDtypeStruct((32, 16, 128), BF),
        in_specs=[VMEM],
        out_specs=VMEM,
        compiler_params=params(),
        name="prefix",
    )(r)


def diag_kernel(x, b, c, cs, dt, skip, y):
    t = lax.broadcasted_iota(jnp.int32, (Q, Q), 0)
    u = lax.broadcasted_iota(jnp.int32, (Q, Q), 1)
    tri = t >= u
    left = u < HD
    for a in range(NQ):
        scores = dot_nt(c[a], b[a])
        csr = cs[a]
        csc = csr.T
        dtr = dt[a]
        for p in range(HH // 2):
            xp = x[a, :, 128 * p : 128 * p + 128]
            ms = []
            for h in (2 * p, 2 * p + 1):
                diff = csc[:, h : h + 1] - csr[h : h + 1, :]
                m = scores * jnp.exp(jnp.where(tri, diff, -jnp.inf)) * dtr[h : h + 1, :]
                ms.append(m.astype(BF))
            xf = xp.astype(F32)
            xx = jnp.concatenate([jnp.where(left, xf, 0.0), jnp.where(left, 0.0, xf)], 0).astype(BF)
            yy = jnp.dot(jnp.concatenate(ms, 1), xx, preferred_element_type=F32)
            y[a, :, 128 * p : 128 * p + 128] = yy + skip[0:1, 128 * p : 128 * p + 128] * xf


def diag_part(x, b, c, cs, dt, skip):
    return pl.pallas_call(
        diag_kernel,
        out_shape=jax.ShapeDtypeStruct((NQ, Q, CH), F32),
        in_specs=[VMEM] * 6,
        out_specs=VMEM,
        compiler_params=params(),
        name="diag_part",
    )(x, b, c, cs, dt, skip)


def norm_kernel(idx, s_in, e, d, c, cs, ydiag, gain, n2, n1, nm, n0, nb):
    y = idx[0]
    core = idx[1]
    ones = head_spread()
    r = lax.broadcasted_iota(jnp.int32, (Q, Q), 0) // HD
    l = lax.broadcasted_iota(jnp.int32, (Q, Q), 1) // HD
    mean = jnp.where(r == l, 1.0 / HD, 0.0).astype(BF)
    state = s_in[...].astype(F32).T
    for a in range(NQ):
        yst = jnp.dot(c[a], state.astype(BF), preferred_element_type=F32)
        g = spread(jnp.exp(cs[a]), ones)
        v = ydiag[a] + g * yst
        if a < NQ - 1:
            state = state * d[a][0:1, :] + e[a]
        hi, lo = two_parts(v * v)
        for p in range(HH // 2):
            at = slice(128 * p, 128 * p + 128)
            ms = jnp.dot(hi[:, at], mean, preferred_element_type=F32)
            ms = ms + jnp.dot(lo[:, at], mean, preferred_element_type=F32)
            nb[a, :, at] = (v[:, at] * lax.rsqrt(ms + 1e-05) * gain[0:1, at]).astype(BF)
    for k, o in ((2, n2), (1, n1), (3, nm), (0, n0)):
        a = lax.rem(y + k, NQ)
        o[0:64, :] = nb[a, pl.ds(pl.multiple_of((1 - core) * 64, 64), 64), :]
        o[64:128, :] = nb[a, pl.ds(pl.multiple_of(core * 64, 64), 64), :]


def norm_part(idx, s_in, e, d, c, cs, ydiag, gain):
    s = jax.ShapeDtypeStruct
    return pl.pallas_call(
        norm_kernel,
        out_shape=(s((Q, CH), BF),) * 4,
        in_specs=[SMEM] + [VMEM] * 7,
        out_specs=(VMEM,) * 4,
        scratch_shapes=[pltpu.VMEM((NQ, Q, CH), BF)],
        compiler_params=params(),
        name="norm_part",
    )(idx, s_in, e, d, c, cs, ydiag, gain)


def out_kernel(n, w, other, own):
    v = jnp.dot(n[...], w[...], preferred_element_type=F32).astype(BF)
    other[...] = v[0:64]
    own[...] = v[64:128]


def out_part(n, w, name):
    s = jax.ShapeDtypeStruct
    return pl.pallas_call(
        out_kernel,
        out_shape=(s((64, 4096), BF),) * 2,
        in_specs=[VMEM] * 2,
        out_specs=(VMEM,) * 2,
        compiler_params=params(),
        name=name,
    )(n, w)


UP = [(y * 2 + c, ((y + 1) % 4) * 2 + c) for y in range(4) for c in range(2)]
DOWN = [(y * 2 + c, ((y - 1) % 4) * 2 + c) for y in range(4) for c in range(2)]
SWAP = [(y * 2 + c, y * 2 + 1 - c) for y in range(4) for c in range(2)]


def up(v):
    return lax.ppermute(v, "tp", UP)


def down(v):
    return lax.ppermute(v, "tp", DOWN)


def swap(v):
    return lax.ppermute(v, "tp", SWAP)


def per_device(tokens, in_x, in_bc, in_dt, conv_x, conv_bc, dt_bias, a_log, skip_d, norm_gain, out_w):
    tp = lax.axis_index("tp")
    ctx = lax.axis_index("ctx")
    idx = jnp.stack([tp // 2, tp % 2, jnp.where(ctx > 0, 1, 0)]).astype(jnp.int32)
    lanes = lambda v: jnp.broadcast_to(v[:, None], (HH, Q))
    weights = (in_x, in_bc, in_dt)

    lo, hi = tokens[:32], tokens[32:]
    partner = swap(tokens)
    ua, db = up(lo), down(hi)
    ub, da = up(hi), down(lo)
    uua, ddb = up(ua), down(db)
    piece0 = project(idx, [tokens], [partner], *weights, "project_0")
    piece1 = project(idx, [ua, ub], [swap(ua), swap(ub)], *weights, "project_1")
    piece2 = project(idx, [da, db], [swap(da), swap(db)], *weights, "project_2")
    piece3 = project(idx, [uua, ddb], [swap(uua), swap(ddb)], *weights, "project_3")
    xs, bcs, dts = zip(piece0, piece1, piece2, piece3)

    y = tp // 2
    last = lambda vs: jnp.where(
        y == 3, vs[0][Q - 8 :], jnp.where(y == 2, vs[2][Q - 8 :], jnp.where(y == 0, vs[1][Q - 8 :], vs[3][Q - 8 :]))
    )
    halo = jnp.concatenate([last(xs), last(bcs)], 1)
    halo = lax.ppermute(halo, "ctx", [(i, i + 1) for i in range(lax.axis_size("ctx") - 1)])
    hx, hbc = halo[:, :CH], halo[:, CH:]

    xc, b, c, cs, dt, e, d, send = local_part(
        idx, xs, bcs, dts, hx, hbc, conv_x, conv_bc, lanes(dt_bias), lanes(a_log)
    )
    got = lax.all_to_all(send, "ctx", 0, 0, tiled=True)
    skip = jnp.repeat(skip_d, HD)[None, :]
    ydiag = diag_part(xc, b, c, cs, dt, skip)
    back = lax.all_to_all(prefix(got), "ctx", 0, 0, tiled=True)
    s_in = back.reshape(CH, NS)
    n2, n1, nm, n0 = norm_part(idx, s_in, e, d, c, cs, ydiag, norm_gain[None, :])

    def summed(n, name):
        other, own = out_part(n, out_w, name)
        return own.astype(F32) + swap(other).astype(F32)

    q2 = summed(n2, "out_2").astype(BF)
    u2, d2 = up(q2[:32]), down(q2[32:])
    q1 = summed(n1, "out_1")
    u1b = up(q1[32:].astype(BF))
    qm = summed(nm, "out_m")
    dma = down(qm[:32].astype(BF))
    u1a = up((q1[:32] + u2.astype(F32)).astype(BF))
    dmb = down((qm[32:] + d2.astype(F32)).astype(BF))
    q0 = summed(n0, "out_0")
    top = q0[:32] + u1a.astype(F32) + dma.astype(F32)
    bottom = q0[32:] + u1b.astype(F32) + dmb.astype(F32)
    return jnp.concatenate([top.astype(BF), bottom.astype(BF)], 0)


def solution(mesh):
    return jax.shard_map(
        per_device,
        mesh=mesh,
        in_specs=(
            P(("ctx", "tp"), None),
            P(None, "tp"),
            P(),
            P(None, "tp"),
            P(None, "tp"),
            P(),
            P("tp"),
            P("tp"),
            P("tp"),
            P("tp"),
            P("tp", None),
        ),
        out_specs=P(("ctx", "tp"), None),
        check_vma=False,
    )
```

```python
import functools

import jax
import jax.numpy as jnp
from jax import lax
from jax.experimental import pallas as pl
from jax.experimental.pallas import tpu as pltpu
from jax.sharding import PartitionSpec as P

BF = jnp.bfloat16
F32 = jnp.float32
VMEM = pl.BlockSpec(memory_space=pltpu.VMEM)
SMEM = pl.BlockSpec(memory_space=pltpu.SMEM)
LIMIT = 12 * 1024 * 1024

Q = 128
NQ = 4
HH = 8
HD = 64
NS = 128
CH = 512
BCW = 256


def params():
    return pltpu.CompilerParams(vmem_limit_bytes=LIMIT)


def dot_tn(a, b):
    return lax.dot_general(a, b, (((0,), (0,)), ((), ())), preferred_element_type=F32)


def dot_nt(a, b):
    return lax.dot_general(a, b, (((1,), (1,)), ((), ())), preferred_element_type=F32)


def two_parts(v):
    hi = v.astype(BF)
    return hi, (v - hi.astype(F32)).astype(BF)


def head_spread():
    row = lax.broadcasted_iota(jnp.int32, (2 * HH, CH), 0)
    lane = lax.broadcasted_iota(jnp.int32, (2 * HH, CH), 1)
    return jnp.where(lane // HD == row % HH, 1.0, 0.0).astype(BF)


def spread(v, ones):
    hi, lo = two_parts(v)
    both = jnp.concatenate([hi.astype(F32), lo.astype(F32)], 0).astype(BF)
    return dot_tn(both, ones)


def chip():
    return lax.axis_index("tp") // 2


def core():
    return lax.rem(lax.axis_index("tp"), 2)


def in_vmem(v):
    return pltpu.with_memory_space_constraint(v, pltpu.VMEM)


def fill(tok, own, other):
    c = core()
    for group, half in ((own, c), (other, 1 - c)):
        step = 64 // len(group)
        for j, r in enumerate(group):
            at = pl.multiple_of(half * 64 + j * step, step)
            tok[pl.ds(at, step), :] = r[0:step, :]


def project_kernel(n, *refs):
    own, other = refs[:n], refs[n : 2 * n]
    wx, wbc, wdt, xo, bco, dto, tok = refs[2 * n :]
    fill(tok, own, other)
    rows = tok[...]
    xo[...] = jnp.dot(rows, wx[...], preferred_element_type=F32).astype(BF)
    bco[...] = jnp.dot(rows, wbc[...], preferred_element_type=F32).astype(BF)
    dto[...] = dot_nt(rows, wdt[...]).T


def project(own, other, weights, name):
    n = len(own)
    return pl.pallas_call(
        functools.partial(project_kernel, n),
        out_shape=(
            pltpu.VMEM((Q, CH), BF),
            pltpu.VMEM((Q, BCW), BF),
            pltpu.VMEM((HH, Q), F32),
        ),
        in_specs=[VMEM] * (2 * n + 3),
        out_specs=(VMEM, VMEM, VMEM),
        scratch_shapes=[pltpu.VMEM((Q, 4096), BF)],
        compiler_params=params(),
        name=name,
    )(*[in_vmem(v) for v in (*own, *other, *weights)])


def silu(v):
    return v / (1.0 + jnp.exp(-v))


def softplus(v):
    return jnp.maximum(v, 0.0) + jnp.log1p(jnp.exp(-jnp.abs(v)))


def column(ref):
    row = lax.broadcasted_iota(jnp.int32, (HH, Q), 0)
    v = jnp.full((HH, Q), ref[0], F32)
    for h in range(1, HH):
        v = jnp.where(row == h, ref[h], v)
    return v


OFFS = (0, 3, 1, 2)


def local_kernel(bias, alog, *refs):
    xs, bcs, dts = refs[0:3], refs[3:6], refs[6:9]
    far, halo, haloswap = refs[9:13], refs[13], refs[14]
    wx, wbc, wdt, kx, kbc = refs[15:20]
    (xo, bo, co, cso, dto, eo, do, send) = refs[20:28]
    ext, extb, dtr, tok = refs[28:32]
    y = chip()
    fill(tok, far[0:2], far[2:4])
    mine = core() == 1
    edge = jnp.where(mine, halo[...].astype(F32), haloswap[...].astype(F32))
    tok[Q : Q + 16, :] = jnp.concatenate([edge, edge], 0).astype(BF)
    rows = tok[...]
    x3 = jnp.dot(rows, wx[...], preferred_element_type=F32).astype(BF).astype(F32)
    bc3 = jnp.dot(rows, wbc[...], preferred_element_type=F32).astype(BF).astype(F32)
    dt3 = dot_nt(rows[0:Q], wdt[...]).T
    ext[0:8, :] = x3[Q : Q + 8]
    extb[0:8, :] = bc3[Q : Q + 8]
    for k in range(4):
        a = lax.rem(y + OFFS[k], NQ)
        at = pl.multiple_of(a * Q + 8, 8)
        ext[pl.ds(at, Q), :] = x3[0:Q] if k == 3 else xs[k][...].astype(F32)
        extb[pl.ds(at, Q), :] = bc3[0:Q] if k == 3 else bcs[k][...].astype(F32)
        dtr[a] = dt3 if k == 3 else dts[k][...]
    ones = head_spread()
    lane = lax.broadcasted_iota(jnp.int32, (HH, Q), 1)
    decay = -jnp.exp(column(alog))
    bias_col = column(bias)
    total = jnp.zeros((HH, Q), F32)
    state = jnp.zeros((NS, CH), F32)
    for a in range(NQ):
        dt = softplus(dtr[a] + bias_col)
        cs = decay * dt
        for s in (1, 2, 4, 8, 16, 32, 64):
            cs = cs + jnp.where(lane >= s, pltpu.roll(cs, s, 1), 0.0)
        end = jnp.broadcast_to(cs[:, Q - 1 : Q], (HH, Q))
        dto[a] = dt
        cso[a] = cs
        total = total + end
        v = kbc[0:1, :] * extb[a * Q + 5 : a * Q + 5 + Q, :]
        for j in range(1, 4):
            v = v + kbc[j : j + 1, :] * extb[a * Q + 5 + j : a * Q + 5 + j + Q, :]
        bc = silu(v).astype(BF)
        b = bc[:, :NS]
        bo[a] = b
        co[a] = bc[:, NS:]
        v = kx[0:1, :] * ext[a * Q + 5 : a * Q + 5 + Q, :]
        for j in range(1, 4):
            v = v + kx[j : j + 1, :] * ext[a * Q + 5 + j : a * Q + 5 + j + Q, :]
        x = silu(v)
        xo[a] = x.astype(BF)
        w = spread(dt * jnp.exp(end - cs), ones)
        e = dot_tn(b, (x * w).astype(BF))
        eo[a] = e
        d = spread(jnp.exp(end), ones)[0:8, :]
        do[a] = d
        state = state * d[0:1, :] + e
    st = state.T
    dec = jnp.exp(total)
    hi = dec.astype(BF).astype(F32)
    mid = (dec - hi).astype(BF).astype(F32)
    low = dec - hi - mid
    row = lax.broadcasted_iota(jnp.int32, (HH, Q), 0)
    for h in range(HH):
        p = lambda t: jnp.broadcast_to(t[h : h + 1, :], (8, Q))
        tail = jnp.where(row == 0, p(hi), jnp.where(row == 1, p(mid), jnp.where(row == 2, p(low), 0.0)))
        for q in range(4):
            d = h * 4 + q
            send[d] = jnp.concatenate([st[16 * d : 16 * d + 16, :], tail], 0).astype(BF)


def local_part(bias, alog, xs, bcs, dts, far, halo, haloswap, weights, kx, kbc):
    s = pltpu.VMEM
    return pl.pallas_call(
        local_kernel,
        out_shape=(
            s((NQ, Q, CH), BF),
            s((NQ, Q, NS), BF),
            s((NQ, Q, NS), BF),
            s((NQ, HH, Q), F32),
            s((NQ, HH, Q), F32),
            s((NQ, NS, CH), F32),
            s((NQ, 8, CH), F32),
            s((32, 24, 128), BF),
        ),
        in_specs=[SMEM] * 2 + [VMEM] * 20,
        out_specs=(VMEM,) * 8,
        scratch_shapes=[
            pltpu.VMEM((8 + NQ * Q, CH), F32),
            pltpu.VMEM((8 + NQ * Q, BCW), F32),
            pltpu.VMEM((NQ, HH, Q), F32),
            pltpu.VMEM((Q + 16, 4096), BF),
        ],
        compiler_params=params(),
        name="local_part",
    )(bias, alog, *[in_vmem(v) for v in (*xs, *bcs, *dts, *far, halo, haloswap, *weights, kx, kbc)])


def prefix_kernel(r, o):
    s = jnp.zeros((16, 128), F32)
    for j in range(32):
        o[j] = s.astype(BF)
        v = r[j].astype(F32)
        s = s * (v[16:17] + v[17:18] + v[18:19]) + v[0:16]


def prefix(r):
    return pl.pallas_call(
        prefix_kernel,
        out_shape=pltpu.VMEM((32, 16, 128), BF),
        in_specs=[VMEM],
        out_specs=VMEM,
        compiler_params=params(),
        name="prefix",
    )(in_vmem(r))


def diag_kernel(skip, x, b, c, cs, dt, y):
    t = lax.broadcasted_iota(jnp.int32, (Q, Q), 0)
    u = lax.broadcasted_iota(jnp.int32, (Q, Q), 1)
    tri = t >= u
    left = u < HD
    for a in range(NQ):
        scores = dot_nt(c[a], b[a])
        csr = cs[a]
        csc = csr.T
        dtr = dt[a]
        for p in range(HH // 2):
            xp = x[a, :, 128 * p : 128 * p + 128]
            ms = []
            for h in (2 * p, 2 * p + 1):
                diff = csc[:, h : h + 1] - csr[h : h + 1, :]
                m = scores * jnp.exp(jnp.where(tri, diff, -jnp.inf)) * dtr[h : h + 1, :]
                ms.append(m.astype(BF))
            xf = xp.astype(F32)
            xx = jnp.concatenate([jnp.where(left, xf, 0.0), jnp.where(left, 0.0, xf)], 0).astype(BF)
            yy = jnp.dot(jnp.concatenate(ms, 1), xx, preferred_element_type=F32)
            y[a, :, 128 * p : 128 * p + 128] = yy + jnp.where(left, skip[2 * p], skip[2 * p + 1]) * xf


def diag_part(skip, *args):
    return pl.pallas_call(
        diag_kernel,
        out_shape=pltpu.VMEM((NQ, Q, CH), F32),
        in_specs=[SMEM] + [VMEM] * 5,
        out_specs=VMEM,
        compiler_params=params(),
        name="diag_part",
    )(skip, *[in_vmem(v) for v in args])


def norm_kernel(s_in, e, d, c, cs, ydiag, gain, w, other, own, rest, nb):
    y = chip()
    mine = core()
    ones = head_spread()
    r = lax.broadcasted_iota(jnp.int32, (Q, Q), 0) // HD
    l = lax.broadcasted_iota(jnp.int32, (Q, Q), 1) // HD
    mean = jnp.where(r == l, 1.0 / HD, 0.0).astype(BF)
    state = s_in[...].astype(F32).T
    for a in range(NQ):
        yst = jnp.dot(c[a], state.astype(BF), preferred_element_type=F32)
        g = spread(jnp.exp(cs[a]), ones)
        v = ydiag[a] + g * yst
        if a < NQ - 1:
            state = state * d[a][0:1, :] + e[a]
        hi, lo = two_parts(v * v)
        for p in range(HH // 2):
            at = slice(128 * p, 128 * p + 128)
            ms = jnp.dot(hi[:, at], mean, preferred_element_type=F32)
            ms = ms + jnp.dot(lo[:, at], mean, preferred_element_type=F32)
            nb[a, :, at] = (v[:, at] * lax.rsqrt(ms + 1e-05) * gain[0:1, at]).astype(BF)

    def half(a, h):
        return nb[a, pl.ds(pl.multiple_of(h * 64, 64), 64), :]

    a = lax.rem(y + 2, NQ)
    v = jnp.concatenate([half(a, 1 - mine), half(a, mine)], 0)
    v = jnp.dot(v, w[...], preferred_element_type=F32).astype(BF)
    other[...] = v[0:64]
    own[...] = v[64:128]
    for j, k in enumerate((1, 3, 0)):
        a = lax.rem(y + k, NQ)
        rest[64 * j : 64 * j + 64, :] = half(a, 1 - mine)
        rest[192 + 64 * j : 256 + 64 * j, :] = half(a, mine)


def norm_part(*args):
    s = pltpu.VMEM
    return pl.pallas_call(
        norm_kernel,
        out_shape=(s((64, 4096), BF), s((64, 4096), BF), s((384, CH), BF)),
        in_specs=[VMEM] * 8,
        out_specs=(VMEM,) * 3,
        scratch_shapes=[pltpu.VMEM((NQ, Q, CH), BF)],
        compiler_params=params(),
        name="norm_part",
    )(*[in_vmem(v) for v in args])


def out_kernel(n, w, other, own):
    other[...] = jnp.dot(n[0:192], w[...], preferred_element_type=F32).astype(BF)
    own[...] = jnp.dot(n[192:384], w[...], preferred_element_type=F32).astype(BF)


def out_part(n, w):
    s = pltpu.VMEM
    return pl.pallas_call(
        out_kernel,
        out_shape=(s((192, 4096), BF),) * 2,
        in_specs=[VMEM] * 2,
        out_specs=(VMEM,) * 2,
        compiler_params=params(),
        name="out_part",
    )(in_vmem(n), in_vmem(w))


UP = [(y * 2 + c, ((y + 1) % 4) * 2 + c) for y in range(4) for c in range(2)]
DOWN = [(y * 2 + c, ((y - 1) % 4) * 2 + c) for y in range(4) for c in range(2)]
SWAP = [(y * 2 + c, y * 2 + 1 - c) for y in range(4) for c in range(2)]


def up(v):
    return lax.ppermute(v, "tp", UP)


def down(v):
    return lax.ppermute(v, "tp", DOWN)


def swap(v):
    return lax.ppermute(v, "tp", SWAP)


def per_device(tokens, in_x, in_bc, in_dt, conv_x, conv_bc, dt_bias, a_log, skip_d, norm_gain, out_w):
    y = lax.axis_index("tp") // 2
    after = lax.optimization_barrier
    weights = (in_x, in_bc, in_dt.T)

    lo, hi = tokens[:32], tokens[32:]
    h = lax.ppermute(tokens[56:], "ctx", [(i, i + 1) for i in range(lax.axis_size("ctx") - 1)])
    partner = swap(tokens)
    ua, db = up(lo), down(hi)
    piece0 = project([tokens], [partner], weights, "project_0")
    up_b, down_a = jnp.concatenate([hi, h], 0), jnp.concatenate([lo, h], 0)
    ua, db, piece0, up_b, down_a = after((ua, db, piece0, up_b, down_a))
    ub, da = up(up_b), down(down_a)
    uua, ddb = up(ua), down(db)
    huu = up(ub[32:])
    edge = jnp.where(y == 3, h, jnp.where(y == 0, ub[32:], jnp.where(y == 2, da[32:], huu)))
    piece1 = project([ua, ub], [swap(ua), swap(ub)], weights, "project_1")
    piece2 = project([da, db], [swap(da), swap(db)], weights, "project_2")
    uua, ddb, piece1, piece2 = after((uua, ddb, piece1, piece2))
    xs, bcs, dts = zip(piece0, piece1, piece2)
    far = [uua, ddb, swap(uua), swap(ddb)]

    xc, b, c, cs, dt, e, d, send = local_part(
        dt_bias, a_log, xs, bcs, dts, far, edge, swap(edge), weights, conv_x, conv_bc
    )
    got = lax.all_to_all(send, "ctx", 0, 0, tiled=True)
    ydiag = diag_part(skip_d, xc, b, c, cs, dt)
    back = lax.all_to_all(prefix(got), "ctx", 0, 0, tiled=True)
    other, own, rest = norm_part(back.reshape(CH, NS), e, d, c, cs, ydiag, norm_gain[None, :], out_w)

    q2 = (own.astype(F32) + swap(other).astype(F32)).astype(BF)
    q2, rest = after((q2, rest))
    u2, d2 = up(q2[:32]), down(q2[32:])
    other, own = out_part(rest, out_w)
    q = own.astype(F32) + swap(other).astype(F32)
    u1b, dma = up(q[32:64].astype(BF)), down(q[64:96].astype(BF))
    u1a = up((q[:32] + u2.astype(F32)).astype(BF))
    dmb = down((q[96:128] + d2.astype(F32)).astype(BF))
    top = q[128:160] + u1a.astype(F32) + dma.astype(F32)
    bottom = q[160:192] + u1b.astype(F32) + dmb.astype(F32)
    return jnp.concatenate([top.astype(BF), bottom.astype(BF)], 0)


def solution(mesh):
    return jax.shard_map(
        per_device,
        mesh=mesh,
        in_specs=(
            P(("ctx", "tp"), None),
            P(None, "tp"),
            P(),
            P(None, "tp"),
            P(None, "tp"),
            P(),
            P("tp"),
            P("tp"),
            P("tp"),
            P("tp"),
            P("tp", None),
        ),
        out_specs=P(("ctx", "tp"), None),
        check_vma=False,
    )
```

```python
import functools

import jax
import jax.numpy as jnp
from jax import lax
from jax.experimental import pallas as pl
from jax.experimental.pallas import tpu as pltpu
from jax.sharding import PartitionSpec as P

BF = jnp.bfloat16
F32 = jnp.float32
VMEM = pl.BlockSpec(memory_space=pltpu.VMEM)
SMEM = pl.BlockSpec(memory_space=pltpu.SMEM)
LIMIT = 14 * 1024 * 1024

Q = 128
NQ = 4
HH = 8
HD = 64
NS = 128
CH = 512
BCW = 256


def params():
    return pltpu.CompilerParams(vmem_limit_bytes=LIMIT)


def dot_tn(a, b):
    return lax.dot_general(a, b, (((0,), (0,)), ((), ())), preferred_element_type=F32)


def dot_nt(a, b):
    return lax.dot_general(a, b, (((1,), (1,)), ((), ())), preferred_element_type=F32)


def two_parts(v):
    hi = v.astype(BF)
    return hi, (v - hi.astype(F32)).astype(BF)


def head_spread():
    row = lax.broadcasted_iota(jnp.int32, (2 * HH, CH), 0)
    lane = lax.broadcasted_iota(jnp.int32, (2 * HH, CH), 1)
    return jnp.where(lane // HD == row % HH, 1.0, 0.0).astype(BF)


def spread(v, ones):
    hi, lo = two_parts(v)
    both = jnp.concatenate([hi.astype(F32), lo.astype(F32)], 0).astype(BF)
    return dot_tn(both, ones)


def chip():
    return lax.axis_index("tp") // 2


def core():
    return lax.rem(lax.axis_index("tp"), 2)


def in_vmem(v):
    return pltpu.with_memory_space_constraint(v, pltpu.VMEM)


def fill(tok, own, other, base=0):
    c = core()
    for group, half in ((own, c), (other, 1 - c)):
        step = 64 // len(group)
        for j, r in enumerate(group):
            at = pl.multiple_of(base + half * 64 + j * step, step)
            tok[pl.ds(at, step), :] = r[...]


def project_kernel(n, *refs):
    own, other = refs[:n], refs[n : 2 * n]
    wx, wbc, wdt, xo, bco, dto, tok = refs[2 * n :]
    for j in range(n):
        fill(tok, [own[j]], [other[j]], j * Q)
    rows = tok[...]
    xo[...] = jnp.dot(rows, wx[...], preferred_element_type=F32).astype(BF)
    bco[...] = jnp.dot(rows, wbc[...], preferred_element_type=F32).astype(BF)
    dt = dot_nt(rows, wdt[...])
    for j in range(n):
        dto[j] = dt[j * Q : (j + 1) * Q].T


def project(own, other, weights, name):
    n = len(own)
    return pl.pallas_call(
        functools.partial(project_kernel, n),
        out_shape=(
            pltpu.VMEM((n * Q, CH), BF),
            pltpu.VMEM((n * Q, BCW), BF),
            pltpu.VMEM((n, HH, Q), F32),
        ),
        in_specs=[VMEM] * (2 * n + 3),
        out_specs=(VMEM, VMEM, VMEM),
        scratch_shapes=[pltpu.VMEM((n * Q, 4096), BF)],
        compiler_params=params(),
        name=name,
    )(*[in_vmem(v) for v in (*own, *other, *weights)])


def silu(v):
    return v / (1.0 + jnp.exp(-v))


def softplus(v):
    return jnp.maximum(v, 0.0) + jnp.log1p(jnp.exp(-jnp.abs(v)))


def column(ref):
    row = lax.broadcasted_iota(jnp.int32, (HH, Q), 0)
    v = jnp.full((HH, Q), ref[0], F32)
    for h in range(1, HH):
        v = jnp.where(row == h, ref[h], v)
    return v


OFFS = (0, 3, 1, 2)


def local_kernel(bias, alog, *refs):
    x0, bc0, dt0, x12, bc12, dt12 = refs[0:6]
    far, halo, haloswap = refs[6:10], refs[10], refs[11]
    wx, wbc, wdt, kx, kbc = refs[12:17]
    (xo, bo, co, cso, dto, eo, do, send) = refs[17:25]
    ext, extb, dtr, tok = refs[25:29]
    y = chip()
    fill(tok, far[0:2], far[2:4])
    edge = halo[...].astype(F32) + haloswap[...].astype(F32)
    tok[Q : Q + 16, :] = jnp.concatenate([edge, edge], 0).astype(BF)
    rows = tok[...]
    x3 = jnp.dot(rows, wx[...], preferred_element_type=F32).astype(BF).astype(F32)
    bc3 = jnp.dot(rows, wbc[...], preferred_element_type=F32).astype(BF).astype(F32)
    dt3 = dot_nt(rows[0:Q], wdt[...]).T
    ext[0:8, :] = x3[Q : Q + 8]
    extb[0:8, :] = bc3[Q : Q + 8]
    pieces = (
        (x0[...], bc0[...], dt0[0]),
        (x12[0:Q], bc12[0:Q], dt12[0]),
        (x12[Q : 2 * Q], bc12[Q : 2 * Q], dt12[1]),
        (x3[0:Q], bc3[0:Q], dt3),
    )
    for k, (px, pbc, pdt) in enumerate(pieces):
        a = lax.rem(y + OFFS[k], NQ)
        at = pl.multiple_of(a * Q + 8, 8)
        ext[pl.ds(at, Q), :] = px.astype(F32)
        extb[pl.ds(at, Q), :] = pbc.astype(F32)
        dtr[a] = pdt
    ones = head_spread()
    lane = lax.broadcasted_iota(jnp.int32, (HH, Q), 1)
    decay = -jnp.exp(column(alog))
    bias_col = column(bias)
    total = jnp.zeros((HH, Q), F32)
    state = jnp.zeros((NS, CH), F32)
    for a in range(NQ):
        dt = softplus(dtr[a] + bias_col)
        cs = decay * dt
        for s in (1, 2, 4, 8, 16, 32, 64):
            cs = cs + jnp.where(lane >= s, pltpu.roll(cs, s, 1), 0.0)
        end = jnp.broadcast_to(cs[:, Q - 1 : Q], (HH, Q))
        dto[a] = dt
        cso[a] = cs
        total = total + end
        v = kbc[0:1, :] * extb[a * Q + 5 : a * Q + 5 + Q, :]
        for j in range(1, 4):
            v = v + kbc[j : j + 1, :] * extb[a * Q + 5 + j : a * Q + 5 + j + Q, :]
        bc = silu(v).astype(BF)
        b = bc[:, :NS]
        bo[a] = b
        co[a] = bc[:, NS:]
        v = kx[0:1, :] * ext[a * Q + 5 : a * Q + 5 + Q, :]
        for j in range(1, 4):
            v = v + kx[j : j + 1, :] * ext[a * Q + 5 + j : a * Q + 5 + j + Q, :]
        x = silu(v)
        xo[a] = x.astype(BF)
        w = spread(dt * jnp.exp(end - cs), ones)
        e = dot_tn(b, (x * w).astype(BF))
        eo[a] = e
        d = spread(jnp.exp(end), ones)[0:8, :]
        do[a] = d
        state = state * d[0:1, :] + e
    st = state.T
    dec = jnp.exp(total)
    hi = dec.astype(BF).astype(F32)
    mid = (dec - hi).astype(BF).astype(F32)
    low = dec - hi - mid
    row = lax.broadcasted_iota(jnp.int32, (HH, Q), 0)
    for h in range(HH):
        p = lambda t: jnp.broadcast_to(t[h : h + 1, :], (8, Q))
        tail = jnp.where(row == 0, p(hi), jnp.where(row == 1, p(mid), jnp.where(row == 2, p(low), 0.0)))
        for q in range(4):
            d = h * 4 + q
            send[d] = jnp.concatenate([st[16 * d : 16 * d + 16, :], tail], 0).astype(BF)


def local_part(bias, alog, *args):
    s = pltpu.VMEM
    return pl.pallas_call(
        local_kernel,
        out_shape=(
            s((NQ, Q, CH), BF),
            s((NQ, Q, NS), BF),
            s((NQ, Q, NS), BF),
            s((NQ, HH, Q), F32),
            s((NQ, HH, Q), F32),
            s((NQ, NS, CH), F32),
            s((NQ, 8, CH), F32),
            s((32, 24, 128), BF),
        ),
        in_specs=[SMEM] * 2 + [VMEM] * 17,
        out_specs=(VMEM,) * 8,
        scratch_shapes=[
            pltpu.VMEM((8 + NQ * Q, CH), F32),
            pltpu.VMEM((8 + NQ * Q, BCW), F32),
            pltpu.VMEM((NQ, HH, Q), F32),
            pltpu.VMEM((Q + 16, 4096), BF),
        ],
        compiler_params=params(),
        name="local_part",
    )(bias, alog, *[in_vmem(v) for v in args])


def prefix_kernel(r, o):
    s = jnp.zeros((16, 128), F32)
    for j in range(32):
        o[j] = s.astype(BF)
        v = r[j].astype(F32)
        s = s * (v[16:17] + v[17:18] + v[18:19]) + v[0:16]


def prefix(r):
    return pl.pallas_call(
        prefix_kernel,
        out_shape=pltpu.VMEM((32, 16, 128), BF),
        in_specs=[VMEM],
        out_specs=VMEM,
        compiler_params=params(),
        name="prefix",
    )(in_vmem(r))


def diag_kernel(skip, x, b, c, cs, dt, y):
    t = lax.broadcasted_iota(jnp.int32, (Q, Q), 0)
    u = lax.broadcasted_iota(jnp.int32, (Q, Q), 1)
    tri = t >= u
    left = u < HD
    for a in range(NQ):
        scores = dot_nt(c[a], b[a])
        csr = cs[a]
        csc = csr.T
        dtr = dt[a]
        for p in range(HH // 2):
            xp = x[a, :, 128 * p : 128 * p + 128]
            ms = []
            for h in (2 * p, 2 * p + 1):
                diff = csc[:, h : h + 1] - csr[h : h + 1, :]
                m = scores * jnp.exp(jnp.where(tri, diff, -jnp.inf)) * dtr[h : h + 1, :]
                ms.append(m.astype(BF))
            xf = xp.astype(F32)
            xx = jnp.concatenate([jnp.where(left, xf, 0.0), jnp.where(left, 0.0, xf)], 0).astype(BF)
            yy = jnp.dot(jnp.concatenate(ms, 1), xx, preferred_element_type=F32)
            y[a, :, 128 * p : 128 * p + 128] = yy + jnp.where(left, skip[2 * p], skip[2 * p + 1]) * xf


def diag_part(skip, *args):
    return pl.pallas_call(
        diag_kernel,
        out_shape=pltpu.VMEM((NQ, Q, CH), F32),
        in_specs=[SMEM] + [VMEM] * 5,
        out_specs=VMEM,
        compiler_params=params(),
        name="diag_part",
    )(skip, *[in_vmem(v) for v in args])


def norm_kernel(s_in, e, d, c, cs, ydiag, gain, w, other, own, rest, nb):
    y = chip()
    mine = core()
    ones = head_spread()
    r = lax.broadcasted_iota(jnp.int32, (Q, Q), 0) // HD
    l = lax.broadcasted_iota(jnp.int32, (Q, Q), 1) // HD
    mean = jnp.where(r == l, 1.0 / HD, 0.0).astype(BF)
    state = s_in[...].astype(F32).T
    for a in range(NQ):
        yst = jnp.dot(c[a], state.astype(BF), preferred_element_type=F32)
        g = spread(jnp.exp(cs[a]), ones)
        v = ydiag[a] + g * yst
        if a < NQ - 1:
            state = state * d[a][0:1, :] + e[a]
        hi, lo = two_parts(v * v)
        for p in range(HH // 2):
            at = slice(128 * p, 128 * p + 128)
            ms = jnp.dot(hi[:, at], mean, preferred_element_type=F32)
            ms = ms + jnp.dot(lo[:, at], mean, preferred_element_type=F32)
            nb[a, :, at] = (v[:, at] * lax.rsqrt(ms + 1e-05) * gain[0:1, at]).astype(BF)

    def half(a, h):
        return nb[a, pl.ds(pl.multiple_of(h * 64, 64), 64), :]

    a = lax.rem(y + 2, NQ)
    v = jnp.concatenate([half(a, 1 - mine), half(a, mine)], 0)
    v = jnp.dot(v, w[...], preferred_element_type=F32).astype(BF)
    other[...] = v[0:64]
    own[...] = v[64:128]
    for j, k in enumerate((1, 3, 0)):
        a = lax.rem(y + k, NQ)
        rest[64 * j : 64 * j + 64, :] = half(a, 1 - mine)
        rest[192 + 64 * j : 256 + 64 * j, :] = half(a, mine)


def norm_part(*args):
    s = pltpu.VMEM
    return pl.pallas_call(
        norm_kernel,
        out_shape=(s((64, 4096), BF), s((64, 4096), BF), s((384, CH), BF)),
        in_specs=[VMEM] * 8,
        out_specs=(VMEM,) * 3,
        scratch_shapes=[pltpu.VMEM((NQ, Q, CH), BF)],
        compiler_params=params(),
        name="norm_part",
    )(*[in_vmem(v) for v in args])


def out_kernel(n, w, other, own):
    other[...] = jnp.dot(n[0:192], w[...], preferred_element_type=F32).astype(BF)
    own[...] = jnp.dot(n[192:384], w[...], preferred_element_type=F32).astype(BF)


def out_part(n, w):
    s = pltpu.VMEM
    return pl.pallas_call(
        out_kernel,
        out_shape=(s((192, 4096), BF),) * 2,
        in_specs=[VMEM] * 2,
        out_specs=(VMEM,) * 2,
        compiler_params=params(),
        name="out_part",
    )(in_vmem(n), in_vmem(w))


UP = [(y * 2 + c, ((y + 1) % 4) * 2 + c) for y in range(4) for c in range(2)]
DOWN = [(y * 2 + c, ((y - 1) % 4) * 2 + c) for y in range(4) for c in range(2)]
SWAP = [(y * 2 + c, y * 2 + 1 - c) for y in range(4) for c in range(2)]


def up(v):
    return lax.ppermute(v, "tp", UP)


def down(v):
    return lax.ppermute(v, "tp", DOWN)


def swap(v):
    return lax.ppermute(v, "tp", SWAP)


def per_device(tokens, in_x, in_bc, in_dt, conv_x, conv_bc, dt_bias, a_log, skip_d, norm_gain, out_w):
    after = lax.optimization_barrier
    weights = (in_x, in_bc, in_dt.T)

    u, d = up(tokens), down(tokens)
    partner = swap(tokens)
    piece0 = project([tokens], [partner], weights, "project_near")
    u, d, piece0, partner = after((u, d, piece0, partner))
    tp = lax.axis_index("tp")
    tail = jnp.where(
        tp == 7, tokens[56:], jnp.where(tp == 6, partner[56:], jnp.where(tp == 1, u[56:], d[56:]))
    )
    uu, dd = up(u[:32]), down(d[32:])
    spans = lax.axis_size("ctx")
    route = ((1, 1), (5, 5), (7, 7), (6, 3))
    edge = lax.ppermute(
        tail, ("ctx", "tp"), [(i * 8 + f, i * 8 + 8 + t) for i in range(spans - 1) for f, t in route]
    )
    su, sd, edge = after((swap(u), swap(d), edge))
    edges = swap(edge)
    piece12 = project([u, d], [su, sd], weights, "project_next")
    uu, dd, piece12 = after((uu, dd, piece12))
    far = [uu, dd, swap(uu), swap(dd)]

    xc, b, c, cs, dt, e, d, send = local_part(
        dt_bias, a_log, *piece0, *piece12, *far, edge, edges, *weights, conv_x, conv_bc
    )
    got = lax.all_to_all(send, "ctx", 0, 0, tiled=True)
    ydiag = diag_part(skip_d, xc, b, c, cs, dt)
    back = lax.all_to_all(prefix(got), "ctx", 0, 0, tiled=True)
    other, own, rest = norm_part(back.reshape(CH, NS), e, d, c, cs, ydiag, norm_gain[None, :], out_w)

    q2 = (own.astype(F32) + swap(other).astype(F32)).astype(BF)
    u2, d2 = up(q2[:32]), down(q2[32:])
    other, own = out_part(rest, out_w)
    q = own.astype(F32) + swap(other).astype(F32)
    u1b, dma = up(q[32:64].astype(BF)), down(q[64:96].astype(BF))
    u1a = up((q[:32] + u2.astype(F32)).astype(BF))
    dmb = down((q[96:128] + d2.astype(F32)).astype(BF))
    top = q[128:160] + u1a.astype(F32) + dma.astype(F32)
    bottom = q[160:192] + u1b.astype(F32) + dmb.astype(F32)
    return jnp.concatenate([top.astype(BF), bottom.astype(BF)], 0)


def solution(mesh):
    return jax.shard_map(
        per_device,
        mesh=mesh,
        in_specs=(
            P(("ctx", "tp"), None),
            P(None, "tp"),
            P(),
            P(None, "tp"),
            P(None, "tp"),
            P(),
            P("tp"),
            P("tp"),
            P("tp"),
            P("tp"),
            P("tp", None),
        ),
        out_specs=P(("ctx", "tp"), None),
        check_vma=False,
    )
```

```python
import functools

import jax
import jax.numpy as jnp
from jax import lax
from jax.experimental import pallas as pl
from jax.experimental.pallas import tpu as pltpu
from jax.sharding import PartitionSpec as P

BF = jnp.bfloat16
F32 = jnp.float32
VMEM = pl.BlockSpec(memory_space=pltpu.VMEM)
SMEM = pl.BlockSpec(memory_space=pltpu.SMEM)
LIMIT = 14 * 1024 * 1024

Q = 128
NQ = 4
HH = 8
HD = 64
NS = 128
CH = 512
BCW = 256


def params():
    return pltpu.CompilerParams(vmem_limit_bytes=LIMIT)


def dot_tn(a, b):
    return lax.dot_general(a, b, (((0,), (0,)), ((), ())), preferred_element_type=F32)


def dot_nt(a, b):
    return lax.dot_general(a, b, (((1,), (1,)), ((), ())), preferred_element_type=F32)


def two_parts(v):
    hi = v.astype(BF)
    return hi, (v - hi.astype(F32)).astype(BF)


def head_spread():
    row = lax.broadcasted_iota(jnp.int32, (2 * HH, CH), 0)
    lane = lax.broadcasted_iota(jnp.int32, (2 * HH, CH), 1)
    return jnp.where(lane // HD == row % HH, 1.0, 0.0).astype(BF)


def spread(v, ones):
    hi, lo = two_parts(v)
    both = jnp.concatenate([hi.astype(F32), lo.astype(F32)], 0).astype(BF)
    return dot_tn(both, ones)


def chip():
    return lax.axis_index("tp") // 2


def core():
    return lax.rem(lax.axis_index("tp"), 2)


def in_vmem(v):
    return pltpu.with_memory_space_constraint(v, pltpu.VMEM)


def fill(tok, own, other, base=0):
    c = core()
    for group, half in ((own, c), (other, 1 - c)):
        step = 64 // len(group)
        for j, r in enumerate(group):
            at = pl.multiple_of(base + half * 64 + j * step, step)
            tok[pl.ds(at, step), :] = r[...]


def project_kernel(n, parts, *refs):
    count = n * parts
    own, other = refs[:count], refs[count : 2 * count]
    wx, wbc, wdt, xo, bco, dto, tok = refs[2 * count :]
    for j in range(n):
        of = slice(j * parts, (j + 1) * parts)
        fill(tok, own[of], other[of], j * Q)
    rows = tok[...]
    xo[...] = jnp.dot(rows, wx[...], preferred_element_type=F32).astype(BF)
    bco[...] = jnp.dot(rows, wbc[...], preferred_element_type=F32).astype(BF)
    dt = dot_nt(rows, wdt[...])
    for j in range(n):
        dto[j] = dt[j * Q : (j + 1) * Q].T


def project(own, other, weights, parts, name):
    n = len(own) // parts
    return pl.pallas_call(
        functools.partial(project_kernel, n, parts),
        out_shape=(
            pltpu.VMEM((n * Q, CH), BF),
            pltpu.VMEM((n * Q, BCW), BF),
            pltpu.VMEM((n, HH, Q), F32),
        ),
        in_specs=[VMEM] * (2 * n * parts + 3),
        out_specs=(VMEM, VMEM, VMEM),
        scratch_shapes=[pltpu.VMEM((n * Q, 4096), BF)],
        compiler_params=params(),
        name=name,
    )(*[in_vmem(v) for v in (*own, *other, *weights)])


def last_kernel(mine, theirs, below, above, o):
    tp = lax.axis_index("tp")
    near = jnp.where(tp == 7, mine[48:64].astype(F32), theirs[48:64].astype(F32))
    far = jnp.where(tp == 1, below[16:32].astype(F32), above[16:32].astype(F32))
    o[...] = jnp.where(tp >= 6, near, far)[8:16].astype(BF)


def last_rows(*args):
    return pl.pallas_call(
        last_kernel,
        out_shape=pltpu.VMEM((8, 4096), BF),
        in_specs=[VMEM] * 4,
        out_specs=VMEM,
        compiler_params=params(),
        name="last_rows",
    )(*[in_vmem(v) for v in args])


def silu(v):
    return v / (1.0 + jnp.exp(-v))


def softplus(v):
    return jnp.maximum(v, 0.0) + jnp.log1p(jnp.exp(-jnp.abs(v)))


def column(ref):
    row = lax.broadcasted_iota(jnp.int32, (HH, Q), 0)
    v = jnp.full((HH, Q), ref[0], F32)
    for h in range(1, HH):
        v = jnp.where(row == h, ref[h], v)
    return v


OFFS = (0, 3, 1, 2)


def local_kernel(bias, alog, *refs):
    x0, bc0, dt0, x12, bc12, dt12 = refs[0:6]
    far, halo, haloswap = refs[6:10], refs[10], refs[11]
    wx, wbc, wdt, kx, kbc = refs[12:17]
    (xo, bo, co, cso, dto, eo, do, send) = refs[17:25]
    ext, extb, dtr, tok = refs[25:29]
    y = chip()
    fill(tok, far[0:2], far[2:4])
    edge = halo[...].astype(F32) + haloswap[...].astype(F32)
    tok[Q : Q + 16, :] = jnp.concatenate([edge, edge], 0).astype(BF)
    rows = tok[...]
    x3 = jnp.dot(rows, wx[...], preferred_element_type=F32).astype(BF).astype(F32)
    bc3 = jnp.dot(rows, wbc[...], preferred_element_type=F32).astype(BF).astype(F32)
    dt3 = dot_nt(rows[0:Q], wdt[...]).T
    ext[0:8, :] = x3[Q : Q + 8]
    extb[0:8, :] = bc3[Q : Q + 8]
    pieces = (
        (x0[...], bc0[...], dt0[0]),
        (x12[0:Q], bc12[0:Q], dt12[0]),
        (x12[Q : 2 * Q], bc12[Q : 2 * Q], dt12[1]),
        (x3[0:Q], bc3[0:Q], dt3),
    )
    for k, (px, pbc, pdt) in enumerate(pieces):
        a = lax.rem(y + OFFS[k], NQ)
        at = pl.multiple_of(a * Q + 8, 8)
        ext[pl.ds(at, Q), :] = px.astype(F32)
        extb[pl.ds(at, Q), :] = pbc.astype(F32)
        dtr[a] = pdt
    ones = head_spread()
    lane = lax.broadcasted_iota(jnp.int32, (HH, Q), 1)
    decay = -jnp.exp(column(alog))
    bias_col = column(bias)
    total = jnp.zeros((HH, Q), F32)
    state = jnp.zeros((NS, CH), F32)
    for a in range(NQ):
        dt = softplus(dtr[a] + bias_col)
        cs = decay * dt
        for s in (1, 2, 4, 8, 16, 32, 64):
            cs = cs + jnp.where(lane >= s, pltpu.roll(cs, s, 1), 0.0)
        end = jnp.broadcast_to(cs[:, Q - 1 : Q], (HH, Q))
        dto[a] = dt
        cso[a] = cs
        total = total + end
        v = kbc[0:1, :] * extb[a * Q + 5 : a * Q + 5 + Q, :]
        for j in range(1, 4):
            v = v + kbc[j : j + 1, :] * extb[a * Q + 5 + j : a * Q + 5 + j + Q, :]
        bc = silu(v).astype(BF)
        b = bc[:, :NS]
        bo[a] = b
        co[a] = bc[:, NS:]
        v = kx[0:1, :] * ext[a * Q + 5 : a * Q + 5 + Q, :]
        for j in range(1, 4):
            v = v + kx[j : j + 1, :] * ext[a * Q + 5 + j : a * Q + 5 + j + Q, :]
        x = silu(v)
        xo[a] = x.astype(BF)
        w = spread(dt * jnp.exp(end - cs), ones)
        e = dot_tn(b, (x * w).astype(BF))
        eo[a] = e
        d = spread(jnp.exp(end), ones)[0:8, :]
        do[a] = d
        state = state * d[0:1, :] + e
    st = state.T
    dec = jnp.exp(total)
    hi = dec.astype(BF).astype(F32)
    mid = (dec - hi).astype(BF).astype(F32)
    low = dec - hi - mid
    row = lax.broadcasted_iota(jnp.int32, (HH, Q), 0)
    for h in range(HH):
        p = lambda t: jnp.broadcast_to(t[h : h + 1, :], (8, Q))
        tail = jnp.where(row == 0, p(hi), jnp.where(row == 1, p(mid), jnp.where(row == 2, p(low), 0.0)))
        for q in range(4):
            d = h * 4 + q
            send[d] = jnp.concatenate([st[16 * d : 16 * d + 16, :], tail], 0).astype(BF)


def local_part(bias, alog, *args):
    s = pltpu.VMEM
    return pl.pallas_call(
        local_kernel,
        out_shape=(
            s((NQ, Q, CH), BF),
            s((NQ, Q, NS), BF),
            s((NQ, Q, NS), BF),
            s((NQ, HH, Q), F32),
            s((NQ, HH, Q), F32),
            s((NQ, NS, CH), F32),
            s((NQ, 8, CH), F32),
            s((32, 24, 128), BF),
        ),
        in_specs=[SMEM] * 2 + [VMEM] * 17,
        out_specs=(VMEM,) * 8,
        scratch_shapes=[
            pltpu.VMEM((8 + NQ * Q, CH), F32),
            pltpu.VMEM((8 + NQ * Q, BCW), F32),
            pltpu.VMEM((NQ, HH, Q), F32),
            pltpu.VMEM((Q + 16, 4096), BF),
        ],
        compiler_params=params(),
        name="local_part",
    )(bias, alog, *[in_vmem(v) for v in args])


def prefix_kernel(r, o):
    s = jnp.zeros((16, 128), F32)
    for j in range(32):
        o[j] = s.astype(BF)
        v = r[j].astype(F32)
        s = s * (v[16:17] + v[17:18] + v[18:19]) + v[0:16]


def prefix(r):
    return pl.pallas_call(
        prefix_kernel,
        out_shape=pltpu.VMEM((32, 16, 128), BF),
        in_specs=[VMEM],
        out_specs=VMEM,
        compiler_params=params(),
        name="prefix",
    )(in_vmem(r))


def diag_kernel(skip, x, b, c, cs, dt, y):
    t = lax.broadcasted_iota(jnp.int32, (Q, Q), 0)
    u = lax.broadcasted_iota(jnp.int32, (Q, Q), 1)
    tri = t >= u
    left = u < HD
    for a in range(NQ):
        scores = dot_nt(c[a], b[a])
        csr = cs[a]
        csc = csr.T
        dtr = dt[a]
        for p in range(HH // 2):
            xp = x[a, :, 128 * p : 128 * p + 128]
            ms = []
            for h in (2 * p, 2 * p + 1):
                diff = csc[:, h : h + 1] - csr[h : h + 1, :]
                m = scores * jnp.exp(jnp.where(tri, diff, -jnp.inf)) * dtr[h : h + 1, :]
                ms.append(m.astype(BF))
            xf = xp.astype(F32)
            xx = jnp.concatenate([jnp.where(left, xf, 0.0), jnp.where(left, 0.0, xf)], 0).astype(BF)
            yy = jnp.dot(jnp.concatenate(ms, 1), xx, preferred_element_type=F32)
            y[a, :, 128 * p : 128 * p + 128] = yy + jnp.where(left, skip[2 * p], skip[2 * p + 1]) * xf


def diag_part(skip, *args):
    return pl.pallas_call(
        diag_kernel,
        out_shape=pltpu.VMEM((NQ, Q, CH), F32),
        in_specs=[SMEM] + [VMEM] * 5,
        out_specs=VMEM,
        compiler_params=params(),
        name="diag_part",
    )(skip, *[in_vmem(v) for v in args])


def norm_kernel(s_in, e, d, c, cs, ydiag, gain, w_far, other, own, rest, w, nb, sem):
    copy = pltpu.make_async_copy(w_far, w, sem)
    copy.start()
    y = chip()
    mine = core()
    ones = head_spread()
    r = lax.broadcasted_iota(jnp.int32, (Q, Q), 0) // HD
    l = lax.broadcasted_iota(jnp.int32, (Q, Q), 1) // HD
    mean = jnp.where(r == l, 1.0 / HD, 0.0).astype(BF)
    state = s_in[...].astype(F32).T
    for a in range(NQ):
        yst = jnp.dot(c[a], state.astype(BF), preferred_element_type=F32)
        g = spread(jnp.exp(cs[a]), ones)
        v = ydiag[a] + g * yst
        if a < NQ - 1:
            state = state * d[a][0:1, :] + e[a]
        hi, lo = two_parts(v * v)
        for p in range(HH // 2):
            at = slice(128 * p, 128 * p + 128)
            ms = jnp.dot(hi[:, at], mean, preferred_element_type=F32)
            ms = ms + jnp.dot(lo[:, at], mean, preferred_element_type=F32)
            nb[a, :, at] = (v[:, at] * lax.rsqrt(ms + 1e-05) * gain[0:1, at]).astype(BF)

    def half(a, h):
        return nb[a, pl.ds(pl.multiple_of(h * 64, 64), 64), :]

    a = lax.rem(y + 2, NQ)
    v = jnp.concatenate([half(a, 1 - mine), half(a, mine)], 0)
    copy.wait()
    v = jnp.dot(v, w[...], preferred_element_type=F32).astype(BF)
    other[...] = v[0:64]
    own[...] = v[64:128]
    for j, k in enumerate((1, 3, 0)):
        a = lax.rem(y + k, NQ)
        rest[64 * j : 64 * j + 64, :] = half(a, 1 - mine)
        rest[192 + 64 * j : 256 + 64 * j, :] = half(a, mine)


def norm_part(*args):
    s = pltpu.VMEM
    return pl.pallas_call(
        norm_kernel,
        out_shape=(s((64, 4096), BF), s((64, 4096), BF), s((384, CH), BF), s((CH, 4096), BF)),
        in_specs=[VMEM] * 7 + [pl.BlockSpec(memory_space=pltpu.HBM)],
        out_specs=(VMEM,) * 4,
        scratch_shapes=[pltpu.VMEM((NQ, Q, CH), BF), pltpu.SemaphoreType.DMA],
        compiler_params=params(),
        name="norm_part",
    )(*[in_vmem(v) for v in args[:7]], pltpu.with_memory_space_constraint(args[7], pltpu.HBM))


def out_kernel(n, w, *outs):
    v = jnp.dot(n[...], w[...], preferred_element_type=F32).astype(BF)
    for j, o in enumerate(outs):
        o[...] = v[64 * j : 64 * j + 64]


def out_part(n, w):
    s = pltpu.VMEM
    return pl.pallas_call(
        out_kernel,
        out_shape=(s((64, 4096), BF),) * 6,
        in_specs=[VMEM] * 2,
        out_specs=(VMEM,) * 6,
        compiler_params=params(),
        name="out_part",
    )(in_vmem(n), in_vmem(w))


UP = [(y * 2 + c, ((y + 1) % 4) * 2 + c) for y in range(4) for c in range(2)]
DOWN = [(y * 2 + c, ((y - 1) % 4) * 2 + c) for y in range(4) for c in range(2)]
SWAP = [(y * 2 + c, y * 2 + 1 - c) for y in range(4) for c in range(2)]


def up(v):
    return lax.ppermute(v, "tp", UP)


def down(v):
    return lax.ppermute(v, "tp", DOWN)


def swap(v):
    return lax.ppermute(v, "tp", SWAP)


def per_device(tokens, in_x, in_bc, in_dt, conv_x, conv_bc, dt_bias, a_log, skip_d, norm_gain, out_w):
    after = lax.optimization_barrier
    weights = (in_x, in_bc, in_dt.T)

    lo, hi = tokens[:32], tokens[32:]
    ua, db = up(lo), down(hi)
    ub, da = up(hi), down(lo)
    partner = swap(tokens)
    piece0 = project([tokens], [partner], weights, 1, "project_near")
    uu, dd = up(ua), down(db)
    ub, da, piece0 = after((ub, da, piece0))
    tail = last_rows(tokens, partner, ub, db)
    spans = lax.axis_size("ctx")
    route = ((1, 1), (5, 5), (7, 7), (6, 3))
    edge = lax.ppermute(
        tail, ("ctx", "tp"), [(i * 8 + f, i * 8 + 8 + t) for i in range(spans - 1) for f, t in route]
    )
    own = [ua, ub, da, db]
    other = [swap(v) for v in own]
    *other, edge, uu, dd = after((*other, edge, uu, dd))
    edges = swap(edge)
    far = [uu, dd, swap(uu), swap(dd)]
    piece12 = project(own, other, weights, 2, "project_next")

    xc, b, c, cs, dt, e, d, send = local_part(
        dt_bias, a_log, *piece0, *piece12, *far, edge, edges, *weights, conv_x, conv_bc
    )
    got = lax.all_to_all(send, "ctx", 0, 0, tiled=True)
    ydiag = diag_part(skip_d, xc, b, c, cs, dt)
    back = lax.all_to_all(prefix(got), "ctx", 0, 0, tiled=True)
    other, own, rest, w = norm_part(back.reshape(CH, NS), e, d, c, cs, ydiag, norm_gain[None, :], out_w)

    def both(mine, theirs):
        return mine.astype(F32) + swap(theirs).astype(F32)

    q2 = both(own, other).astype(BF)
    u2, d2 = up(q2[:32]), down(q2[32:])
    t1, tm, t0, m1, mm, m0 = out_part(rest, w)
    q1 = both(m1, t1)
    u1b = up(q1[32:].astype(BF))
    qm = both(mm, tm)
    dma = down(qm[:32].astype(BF))
    u1a = up((q1[:32] + u2.astype(F32)).astype(BF))
    dmb = down((qm[32:] + d2.astype(F32)).astype(BF))
    q0 = both(m0, t0)
    top = q0[:32] + u1a.astype(F32) + dma.astype(F32)
    bottom = q0[32:] + u1b.astype(F32) + dmb.astype(F32)
    return jnp.concatenate([top.astype(BF), bottom.astype(BF)], 0)


def solution(mesh):
    return jax.shard_map(
        per_device,
        mesh=mesh,
        in_specs=(
            P(("ctx", "tp"), None),
            P(None, "tp"),
            P(),
            P(None, "tp"),
            P(None, "tp"),
            P(),
            P("tp"),
            P("tp"),
            P("tp"),
            P("tp"),
            P("tp", None),
        ),
        out_specs=P(("ctx", "tp"), None),
        check_vma=False,
    )
```

```python
import functools

import jax
import jax.numpy as jnp
from jax import lax
from jax.experimental import pallas as pl
from jax.experimental.pallas import tpu as pltpu
from jax.sharding import PartitionSpec as P

BF = jnp.bfloat16
F32 = jnp.float32
VMEM = pl.BlockSpec(memory_space=pltpu.VMEM)
SMEM = pl.BlockSpec(memory_space=pltpu.SMEM)
LIMIT = 14 * 1024 * 1024

Q = 128
NQ = 4
HH = 8
HD = 64
NS = 128
CH = 512
BCW = 256


def params():
    return pltpu.CompilerParams(vmem_limit_bytes=LIMIT)


def dot_tn(a, b):
    return lax.dot_general(a, b, (((0,), (0,)), ((), ())), preferred_element_type=F32)


def dot_nt(a, b):
    return lax.dot_general(a, b, (((1,), (1,)), ((), ())), preferred_element_type=F32)


def two_parts(v):
    hi = v.astype(BF)
    return hi, (v - hi.astype(F32)).astype(BF)


def head_spread():
    row = lax.broadcasted_iota(jnp.int32, (2 * HH, CH), 0)
    lane = lax.broadcasted_iota(jnp.int32, (2 * HH, CH), 1)
    return jnp.where(lane // HD == row % HH, 1.0, 0.0).astype(BF)


def spread(v, ones):
    hi, lo = two_parts(v)
    both = jnp.concatenate([hi.astype(F32), lo.astype(F32)], 0).astype(BF)
    return dot_tn(both, ones)


def chip():
    return lax.axis_index("tp") // 2


def core():
    return lax.rem(lax.axis_index("tp"), 2)


def in_vmem(v):
    return pltpu.with_memory_space_constraint(v, pltpu.VMEM)


def fill(tok, own, other, base=0):
    c = core()
    for group, half in ((own, c), (other, 1 - c)):
        step = 64 // len(group)
        for j, r in enumerate(group):
            at = pl.multiple_of(base + half * 64 + j * step, step)
            tok[pl.ds(at, step), :] = r[...]


def project_kernel(n, parts, *refs):
    count = n * parts
    own, other = refs[:count], refs[count : 2 * count]
    wx, wbc, wdt, xo, bco, dto, tok = refs[2 * count :]
    for j in range(n):
        of = slice(j * parts, (j + 1) * parts)
        fill(tok, own[of], other[of], j * Q)
    rows = tok[...]
    xo[...] = jnp.dot(rows, wx[...], preferred_element_type=F32).astype(BF)
    bco[...] = jnp.dot(rows, wbc[...], preferred_element_type=F32).astype(BF)
    dt = dot_nt(rows, wdt[...])
    for j in range(n):
        dto[j] = dt[j * Q : (j + 1) * Q].T


def project(own, other, weights, parts, name):
    n = len(own) // parts
    return pl.pallas_call(
        functools.partial(project_kernel, n, parts),
        out_shape=(
            pltpu.VMEM((n * Q, CH), BF),
            pltpu.VMEM((n * Q, BCW), BF),
            pltpu.VMEM((n, HH, Q), F32),
        ),
        in_specs=[VMEM] * (2 * n * parts + 3),
        out_specs=(VMEM, VMEM, VMEM),
        scratch_shapes=[pltpu.VMEM((n * Q, 4096), BF)],
        compiler_params=params(),
        name=name,
    )(*[in_vmem(v) for v in (*own, *other, *weights)])


def near_kernel(mine, theirs, wx_far, wbc_far, wdt_far, xo, bco, dto, last, wx, wbc, wdt, tok, sems):
    c = core()
    pairs = (
        (mine, tok.at[pl.ds(pl.multiple_of(c * 64, 64), 64), :]),
        (wx_far, wx),
        (wdt_far, wdt),
        (wbc_far, wbc),
    )
    copies = [pltpu.make_async_copy(f, t, sems.at[j]) for j, (f, t) in enumerate(pairs)]
    for copy in copies:
        copy.start()
    tok[pl.ds(pl.multiple_of((1 - c) * 64, 64), 64), :] = theirs[...]
    copies[0].wait()
    last[...] = tok[Q - 16 : Q, :][8:16]
    copies[1].wait()
    rows = tok[...]
    xo[...] = jnp.dot(rows, wx[...], preferred_element_type=F32).astype(BF)
    copies[2].wait()
    dto[0] = dot_nt(rows, wdt[...]).T
    copies[3].wait()
    bco[...] = jnp.dot(rows, wbc[...], preferred_element_type=F32).astype(BF)


def project_near(mine, theirs, in_x, in_bc, in_dt):
    hbm = pl.BlockSpec(memory_space=pltpu.HBM)
    far = lambda v: pltpu.with_memory_space_constraint(v, pltpu.HBM)
    return pl.pallas_call(
        near_kernel,
        out_shape=(
            pltpu.VMEM((Q, CH), BF),
            pltpu.VMEM((Q, BCW), BF),
            pltpu.VMEM((1, HH, Q), F32),
            pltpu.VMEM((8, 4096), BF),
            pltpu.VMEM(in_x.shape, BF),
            pltpu.VMEM(in_bc.shape, BF),
            pltpu.VMEM(in_dt.shape, BF),
        ),
        in_specs=[hbm, VMEM, hbm, hbm, hbm],
        out_specs=(VMEM,) * 7,
        scratch_shapes=[pltpu.VMEM((Q, 4096), BF), pltpu.SemaphoreType.DMA((4,))],
        compiler_params=params(),
        name="project_near",
    )(far(mine), in_vmem(theirs), far(in_x), far(in_bc), far(in_dt))


def silu(v):
    return v / (1.0 + jnp.exp(-v))


def softplus(v):
    return jnp.maximum(v, 0.0) + jnp.log1p(jnp.exp(-jnp.abs(v)))


def column(ref):
    row = lax.broadcasted_iota(jnp.int32, (HH, Q), 0)
    v = jnp.full((HH, Q), ref[0], F32)
    for h in range(1, HH):
        v = jnp.where(row == h, ref[h], v)
    return v


OFFS = (0, 3, 1, 2)


def local_kernel(bias, alog, *refs):
    x0, bc0, dt0, x12, bc12, dt12 = refs[0:6]
    far, halo, haloswap = refs[6:10], refs[10], refs[11]
    wx, wbc, wdt, kx, kbc = refs[12:17]
    (xo, bo, co, cso, dto, eo, do, send) = refs[17:25]
    ext, extb, dtr, tok = refs[25:29]
    y = chip()
    fill(tok, far[0:2], far[2:4])
    edge = halo[...].astype(F32) + haloswap[...].astype(F32)
    tok[Q : Q + 16, :] = jnp.concatenate([edge, edge], 0).astype(BF)
    rows = tok[...]
    x3 = jnp.dot(rows, wx[...], preferred_element_type=F32).astype(BF).astype(F32)
    bc3 = jnp.dot(rows, wbc[...], preferred_element_type=F32).astype(BF).astype(F32)
    dt3 = dot_nt(rows[0:Q], wdt[...]).T
    ext[0:8, :] = x3[Q : Q + 8]
    extb[0:8, :] = bc3[Q : Q + 8]
    pieces = (
        (x0[...], bc0[...], dt0[0]),
        (x12[0:Q], bc12[0:Q], dt12[0]),
        (x12[Q : 2 * Q], bc12[Q : 2 * Q], dt12[1]),
        (x3[0:Q], bc3[0:Q], dt3),
    )
    for k, (px, pbc, pdt) in enumerate(pieces):
        a = lax.rem(y + OFFS[k], NQ)
        at = pl.multiple_of(a * Q + 8, 8)
        ext[pl.ds(at, Q), :] = px.astype(F32)
        extb[pl.ds(at, Q), :] = pbc.astype(F32)
        dtr[a] = pdt
    ones = head_spread()
    lane = lax.broadcasted_iota(jnp.int32, (HH, Q), 1)
    decay = -jnp.exp(column(alog))
    bias_col = column(bias)
    total = jnp.zeros((HH, Q), F32)
    state = jnp.zeros((NS, CH), F32)
    for a in range(NQ):
        dt = softplus(dtr[a] + bias_col)
        cs = decay * dt
        for s in (1, 2, 4, 8, 16, 32, 64):
            cs = cs + jnp.where(lane >= s, pltpu.roll(cs, s, 1), 0.0)
        end = jnp.broadcast_to(cs[:, Q - 1 : Q], (HH, Q))
        dto[a] = dt
        cso[a] = cs
        total = total + end
        v = kbc[0:1, :] * extb[a * Q + 5 : a * Q + 5 + Q, :]
        for j in range(1, 4):
            v = v + kbc[j : j + 1, :] * extb[a * Q + 5 + j : a * Q + 5 + j + Q, :]
        bc = silu(v).astype(BF)
        b = bc[:, :NS]
        bo[a] = b
        co[a] = bc[:, NS:]
        v = kx[0:1, :] * ext[a * Q + 5 : a * Q + 5 + Q, :]
        for j in range(1, 4):
            v = v + kx[j : j + 1, :] * ext[a * Q + 5 + j : a * Q + 5 + j + Q, :]
        x = silu(v)
        xo[a] = x.astype(BF)
        w = spread(dt * jnp.exp(end - cs), ones)
        e = dot_tn(b, (x * w).astype(BF))
        eo[a] = e
        d = spread(jnp.exp(end), ones)[0:8, :]
        do[a] = d
        state = state * d[0:1, :] + e
    st = state.T
    dec = jnp.exp(total)
    hi = dec.astype(BF).astype(F32)
    mid = (dec - hi).astype(BF).astype(F32)
    low = dec - hi - mid
    row = lax.broadcasted_iota(jnp.int32, (HH, Q), 0)
    for h in range(HH):
        p = lambda t: jnp.broadcast_to(t[h : h + 1, :], (8, Q))
        tail = jnp.where(row == 0, p(hi), jnp.where(row == 1, p(mid), jnp.where(row == 2, p(low), 0.0)))
        for q in range(4):
            d = h * 4 + q
            send[d] = jnp.concatenate([st[16 * d : 16 * d + 16, :], tail], 0).astype(BF)


def local_part(bias, alog, *args):
    s = pltpu.VMEM
    return pl.pallas_call(
        local_kernel,
        out_shape=(
            s((NQ, Q, CH), BF),
            s((NQ, Q, NS), BF),
            s((NQ, Q, NS), BF),
            s((NQ, HH, Q), F32),
            s((NQ, HH, Q), F32),
            s((NQ, NS, CH), F32),
            s((NQ, 8, CH), F32),
            s((32, 24, 128), BF),
        ),
        in_specs=[SMEM] * 2 + [VMEM] * 17,
        out_specs=(VMEM,) * 8,
        scratch_shapes=[
            pltpu.VMEM((8 + NQ * Q, CH), F32),
            pltpu.VMEM((8 + NQ * Q, BCW), F32),
            pltpu.VMEM((NQ, HH, Q), F32),
            pltpu.VMEM((Q + 16, 4096), BF),
        ],
        compiler_params=params(),
        name="local_part",
    )(bias, alog, *[in_vmem(v) for v in args])


def prefix_kernel(r, o):
    s = jnp.zeros((16, 128), F32)
    for j in range(32):
        o[j] = s.astype(BF)
        v = r[j].astype(F32)
        s = s * (v[16:17] + v[17:18] + v[18:19]) + v[0:16]


def prefix(r):
    return pl.pallas_call(
        prefix_kernel,
        out_shape=pltpu.VMEM((32, 16, 128), BF),
        in_specs=[VMEM],
        out_specs=VMEM,
        compiler_params=params(),
        name="prefix",
    )(in_vmem(r))


def diag_kernel(skip, x, b, c, cs, dt, y):
    t = lax.broadcasted_iota(jnp.int32, (Q, Q), 0)
    u = lax.broadcasted_iota(jnp.int32, (Q, Q), 1)
    tri = t >= u
    left = u < HD
    for a in range(NQ):
        scores = dot_nt(c[a], b[a])
        csr = cs[a]
        csc = csr.T
        dtr = dt[a]
        for p in range(HH // 2):
            xp = x[a, :, 128 * p : 128 * p + 128]
            ms = []
            for h in (2 * p, 2 * p + 1):
                diff = csc[:, h : h + 1] - csr[h : h + 1, :]
                m = scores * jnp.exp(jnp.where(tri, diff, -jnp.inf)) * dtr[h : h + 1, :]
                ms.append(m.astype(BF))
            xf = xp.astype(F32)
            xx = jnp.concatenate([jnp.where(left, xf, 0.0), jnp.where(left, 0.0, xf)], 0).astype(BF)
            yy = jnp.dot(jnp.concatenate(ms, 1), xx, preferred_element_type=F32)
            y[a, :, 128 * p : 128 * p + 128] = yy + jnp.where(left, skip[2 * p], skip[2 * p + 1]) * xf


def diag_part(skip, *args):
    return pl.pallas_call(
        diag_kernel,
        out_shape=pltpu.VMEM((NQ, Q, CH), F32),
        in_specs=[SMEM] + [VMEM] * 5,
        out_specs=VMEM,
        compiler_params=params(),
        name="diag_part",
    )(skip, *[in_vmem(v) for v in args])


def norm_kernel(s_in, e, d, c, cs, ydiag, gain, w_far, other, own, rest, w, nb, sem):
    copy = pltpu.make_async_copy(w_far, w, sem)
    copy.start()
    y = chip()
    mine = core()
    ones = head_spread()
    r = lax.broadcasted_iota(jnp.int32, (Q, Q), 0) // HD
    l = lax.broadcasted_iota(jnp.int32, (Q, Q), 1) // HD
    mean = jnp.where(r == l, 1.0 / HD, 0.0).astype(BF)
    state = s_in[...].astype(F32).T
    for a in range(NQ):
        yst = jnp.dot(c[a], state.astype(BF), preferred_element_type=F32)
        g = spread(jnp.exp(cs[a]), ones)
        v = ydiag[a] + g * yst
        if a < NQ - 1:
            state = state * d[a][0:1, :] + e[a]
        hi, lo = two_parts(v * v)
        for p in range(HH // 2):
            at = slice(128 * p, 128 * p + 128)
            ms = jnp.dot(hi[:, at], mean, preferred_element_type=F32)
            ms = ms + jnp.dot(lo[:, at], mean, preferred_element_type=F32)
            nb[a, :, at] = (v[:, at] * lax.rsqrt(ms + 1e-05) * gain[0:1, at]).astype(BF)

    def half(a, h):
        return nb[a, pl.ds(pl.multiple_of(h * 64, 64), 64), :]

    a = lax.rem(y + 2, NQ)
    v = jnp.concatenate([half(a, 1 - mine), half(a, mine)], 0)
    copy.wait()
    v = jnp.dot(v, w[...], preferred_element_type=F32).astype(BF)
    other[...] = v[0:64]
    own[...] = v[64:128]
    for j, k in enumerate((1, 3, 0)):
        a = lax.rem(y + k, NQ)
        rest[64 * j : 64 * j + 64, :] = half(a, 1 - mine)
        rest[192 + 64 * j : 256 + 64 * j, :] = half(a, mine)


def norm_part(*args):
    s = pltpu.VMEM
    return pl.pallas_call(
        norm_kernel,
        out_shape=(s((64, 4096), BF), s((64, 4096), BF), s((384, CH), BF), s((CH, 4096), BF)),
        in_specs=[VMEM] * 7 + [pl.BlockSpec(memory_space=pltpu.HBM)],
        out_specs=(VMEM,) * 4,
        scratch_shapes=[pltpu.VMEM((NQ, Q, CH), BF), pltpu.SemaphoreType.DMA],
        compiler_params=params(),
        name="norm_part",
    )(*[in_vmem(v) for v in args[:7]], pltpu.with_memory_space_constraint(args[7], pltpu.HBM))


def out_kernel(n, w, *outs):
    v = jnp.dot(n[...], w[...], preferred_element_type=F32).astype(BF)
    for j, o in enumerate(outs):
        o[...] = v[64 * j : 64 * j + 64]


def out_part(n, w):
    s = pltpu.VMEM
    return pl.pallas_call(
        out_kernel,
        out_shape=(s((64, 4096), BF),) * 6,
        in_specs=[VMEM] * 2,
        out_specs=(VMEM,) * 6,
        compiler_params=params(),
        name="out_part",
    )(in_vmem(n), in_vmem(w))


UP = [(y * 2 + c, ((y + 1) % 4) * 2 + c) for y in range(4) for c in range(2)]
DOWN = [(y * 2 + c, ((y - 1) % 4) * 2 + c) for y in range(4) for c in range(2)]
SWAP = [(y * 2 + c, y * 2 + 1 - c) for y in range(4) for c in range(2)]


def up(v):
    return lax.ppermute(v, "tp", UP)


def down(v):
    return lax.ppermute(v, "tp", DOWN)


def swap(v):
    return lax.ppermute(v, "tp", SWAP)


def per_device(tokens, in_x, in_bc, in_dt, conv_x, conv_bc, dt_bias, a_log, skip_d, norm_gain, out_w):
    after = lax.optimization_barrier
    lo, hi = tokens[:32], tokens[32:]
    ua, db = up(lo), down(hi)
    ub, da = up(hi), down(lo)
    *piece0, last, wx, wbc, wdt = project_near(tokens, swap(tokens), in_x, in_bc, in_dt.T)
    weights = (wx, wbc, wdt)
    spans = lax.axis_size("ctx")

    def onward(*route):
        return lax.ppermute(
            last, ("ctx", "tp"), [(i * 8 + f, i * 8 + 8 + t) for i in range(spans - 1) for f, t in route]
        )

    edge = onward((7, 7), (6, 1)) + onward((7, 5), (6, 3))
    ua, db, wx = after((ua, db, wx))
    ub, da, edge = after((ub, da, edge))
    edges = swap(edge)
    uu, dd = up(ua), down(db)
    own = [ua, ub, da, db]
    other = [swap(v) for v in own]
    *other, uu, dd = after((*other, uu, dd))
    far = [uu, dd, swap(uu), swap(dd)]
    piece12 = project(own, other, weights, 2, "project_next")

    xc, b, c, cs, dt, e, d, send = local_part(
        dt_bias, a_log, *piece0, *piece12, *far, edge, edges, *weights, conv_x, conv_bc
    )
    got = lax.all_to_all(send, "ctx", 0, 0, tiled=True)
    ydiag = diag_part(skip_d, xc, b, c, cs, dt)
    back = lax.all_to_all(prefix(got), "ctx", 0, 0, tiled=True)
    other, own, rest, w = norm_part(back.reshape(CH, NS), e, d, c, cs, ydiag, norm_gain[None, :], out_w)

    def both(mine, theirs):
        return mine.astype(F32) + swap(theirs).astype(F32)

    q2 = both(own, other).astype(BF)
    u2, d2 = up(q2[:32]), down(q2[32:])
    t1, tm, t0, m1, mm, m0 = out_part(rest, w)
    q1 = both(m1, t1)
    u1b = up(q1[32:].astype(BF))
    qm = both(mm, tm)
    dma = down(qm[:32].astype(BF))
    u1a = up((q1[:32] + u2.astype(F32)).astype(BF))
    dmb = down((qm[32:] + d2.astype(F32)).astype(BF))
    q0 = both(m0, t0)
    top = q0[:32] + u1a.astype(F32) + dma.astype(F32)
    bottom = q0[32:] + u1b.astype(F32) + dmb.astype(F32)
    return jnp.concatenate([top.astype(BF), bottom.astype(BF)], 0)


def solution(mesh):
    return jax.shard_map(
        per_device,
        mesh=mesh,
        in_specs=(
            P(("ctx", "tp"), None),
            P(None, "tp"),
            P(),
            P(None, "tp"),
            P(None, "tp"),
            P(),
            P("tp"),
            P("tp"),
            P("tp"),
            P("tp"),
            P("tp", None),
        ),
        out_specs=P(("ctx", "tp"), None),
        check_vma=False,
    )
```

```python
import functools

import jax
import jax.numpy as jnp
from jax import lax
from jax.experimental import pallas as pl
from jax.experimental.pallas import tpu as pltpu
from jax.sharding import PartitionSpec as P

BF = jnp.bfloat16
F32 = jnp.float32
VMEM = pl.BlockSpec(memory_space=pltpu.VMEM)
SMEM = pl.BlockSpec(memory_space=pltpu.SMEM)
LIMIT = 14 * 1024 * 1024

Q = 128
NQ = 4
HH = 8
HD = 64
NS = 128
CH = 512
BCW = 256


def params():
    return pltpu.CompilerParams(vmem_limit_bytes=LIMIT)


def dot_tn(a, b):
    return lax.dot_general(a, b, (((0,), (0,)), ((), ())), preferred_element_type=F32)


def dot_nt(a, b):
    return lax.dot_general(a, b, (((1,), (1,)), ((), ())), preferred_element_type=F32)


def two_parts(v):
    hi = v.astype(BF)
    return hi, (v - hi.astype(F32)).astype(BF)


def head_spread():
    row = lax.broadcasted_iota(jnp.int32, (2 * HH, CH), 0)
    lane = lax.broadcasted_iota(jnp.int32, (2 * HH, CH), 1)
    return jnp.where(lane // HD == row % HH, 1.0, 0.0).astype(BF)


def spread(v, ones):
    hi, lo = two_parts(v)
    both = jnp.concatenate([hi.astype(F32), lo.astype(F32)], 0).astype(BF)
    return dot_tn(both, ones)


def chip():
    return lax.axis_index("tp") // 2


def core():
    return lax.rem(lax.axis_index("tp"), 2)


def in_vmem(v):
    return pltpu.with_memory_space_constraint(v, pltpu.VMEM)


def fill(tok, own, other, base=0):
    c = core()
    for group, half in ((own, c), (other, 1 - c)):
        step = 64 // len(group)
        for j, r in enumerate(group):
            at = pl.multiple_of(base + half * 64 + j * step, step)
            tok[pl.ds(at, step), :] = r[...]


def project_kernel(n, parts, *refs):
    count = n * parts
    own, other = refs[:count], refs[count : 2 * count]
    wx, wbc, wdt, xo, bco, dto, tok = refs[2 * count :]
    for j in range(n):
        of = slice(j * parts, (j + 1) * parts)
        fill(tok, own[of], other[of], j * Q)
    rows = tok[...]
    xo[...] = jnp.dot(rows, wx[...], preferred_element_type=F32).astype(BF)
    bco[...] = jnp.dot(rows, wbc[...], preferred_element_type=F32).astype(BF)
    dt = dot_nt(rows, wdt[...])
    for j in range(n):
        dto[j] = dt[j * Q : (j + 1) * Q].T


def project(own, other, weights, parts, name):
    n = len(own) // parts
    return pl.pallas_call(
        functools.partial(project_kernel, n, parts),
        out_shape=(
            pltpu.VMEM((n * Q, CH), BF),
            pltpu.VMEM((n * Q, BCW), BF),
            pltpu.VMEM((n, HH, Q), F32),
        ),
        in_specs=[VMEM] * (2 * n * parts + 3),
        out_specs=(VMEM, VMEM, VMEM),
        scratch_shapes=[pltpu.VMEM((n * Q, 4096), BF)],
        compiler_params=params(),
        name=name,
    )(*[in_vmem(v) for v in (*own, *other, *weights)])


def near_kernel(mine, theirs, wx_far, wbc_far, wdt_far, xo, bco, dto, last, wx, wbc, wdt, tok, sems):
    c = core()
    pairs = (
        (mine, tok.at[pl.ds(pl.multiple_of(c * 64, 64), 64), :]),
        (wx_far, wx),
        (wdt_far, wdt),
        (wbc_far, wbc),
    )
    copies = [pltpu.make_async_copy(f, t, sems.at[j]) for j, (f, t) in enumerate(pairs)]
    for copy in copies:
        copy.start()
    tok[pl.ds(pl.multiple_of((1 - c) * 64, 64), 64), :] = theirs[...]
    copies[0].wait()
    last[...] = tok[Q - 16 : Q, :][8:16]
    copies[1].wait()
    rows = tok[...]
    xo[...] = jnp.dot(rows, wx[...], preferred_element_type=F32).astype(BF)
    copies[2].wait()
    dto[0] = dot_nt(rows, wdt[...]).T
    copies[3].wait()
    bco[...] = jnp.dot(rows, wbc[...], preferred_element_type=F32).astype(BF)


def project_near(mine, theirs, in_x, in_bc, in_dt):
    hbm = pl.BlockSpec(memory_space=pltpu.HBM)
    far = lambda v: pltpu.with_memory_space_constraint(v, pltpu.HBM)
    return pl.pallas_call(
        near_kernel,
        out_shape=(
            pltpu.VMEM((Q, CH), BF),
            pltpu.VMEM((Q, BCW), BF),
            pltpu.VMEM((1, HH, Q), F32),
            pltpu.VMEM((8, 4096), BF),
            pltpu.VMEM(in_x.shape, BF),
            pltpu.VMEM(in_bc.shape, BF),
            pltpu.VMEM(in_dt.shape, BF),
        ),
        in_specs=[hbm, VMEM, hbm, hbm, hbm],
        out_specs=(VMEM,) * 7,
        scratch_shapes=[pltpu.VMEM((Q, 4096), BF), pltpu.SemaphoreType.DMA((4,))],
        compiler_params=params(),
        name="project_near",
    )(far(mine), in_vmem(theirs), far(in_x), far(in_bc), far(in_dt))


def silu(v):
    return v / (1.0 + jnp.exp(-v))


def softplus(v):
    return jnp.maximum(v, 0.0) + jnp.log1p(jnp.exp(-jnp.abs(v)))


def column(ref):
    row = lax.broadcasted_iota(jnp.int32, (HH, Q), 0)
    v = jnp.full((HH, Q), ref[0], F32)
    for h in range(1, HH):
        v = jnp.where(row == h, ref[h], v)
    return v


OFFS = (0, 3, 1, 2)


def local_kernel(bias, alog, *refs):
    x0, bc0, dt0, x12, bc12, dt12 = refs[0:6]
    far, halo, haloswap = refs[6:10], refs[10], refs[11]
    wx, wbc, wdt, kx, kbc = refs[12:17]
    (xo, bo, co, cso, dto, eo, do, send) = refs[17:25]
    ext, extb, dtr, tok = refs[25:29]
    y = chip()
    fill(tok, far[0:2], far[2:4])
    edge = halo[...].astype(F32) + haloswap[...].astype(F32)
    tok[Q : Q + 16, :] = jnp.concatenate([edge, edge], 0).astype(BF)
    rows = tok[...]
    x3 = jnp.dot(rows, wx[...], preferred_element_type=F32).astype(BF).astype(F32)
    bc3 = jnp.dot(rows, wbc[...], preferred_element_type=F32).astype(BF).astype(F32)
    dt3 = dot_nt(rows[0:Q], wdt[...]).T
    ext[0:8, :] = x3[Q : Q + 8]
    extb[0:8, :] = bc3[Q : Q + 8]
    pieces = (
        (x0[...], bc0[...], dt0[0]),
        (x12[0:Q], bc12[0:Q], dt12[0]),
        (x12[Q : 2 * Q], bc12[Q : 2 * Q], dt12[1]),
        (x3[0:Q], bc3[0:Q], dt3),
    )
    for k, (px, pbc, pdt) in enumerate(pieces):
        a = lax.rem(y + OFFS[k], NQ)
        at = pl.multiple_of(a * Q + 8, 8)
        ext[pl.ds(at, Q), :] = px.astype(F32)
        extb[pl.ds(at, Q), :] = pbc.astype(F32)
        dtr[a] = pdt
    ones = head_spread()
    lane = lax.broadcasted_iota(jnp.int32, (HH, Q), 1)
    decay = -jnp.exp(column(alog))
    bias_col = column(bias)
    total = jnp.zeros((HH, Q), F32)
    state = jnp.zeros((NS, CH), F32)
    for a in range(NQ):
        dt = softplus(dtr[a] + bias_col)
        cs = decay * dt
        for s in (1, 2, 4, 8, 16, 32, 64):
            cs = cs + jnp.where(lane >= s, pltpu.roll(cs, s, 1), 0.0)
        end = jnp.broadcast_to(cs[:, Q - 1 : Q], (HH, Q))
        dto[a] = dt
        cso[a] = cs
        total = total + end
        v = kbc[0:1, :] * extb[a * Q + 5 : a * Q + 5 + Q, :]
        for j in range(1, 4):
            v = v + kbc[j : j + 1, :] * extb[a * Q + 5 + j : a * Q + 5 + j + Q, :]
        bc = silu(v).astype(BF)
        b = bc[:, :NS]
        bo[a] = b
        co[a] = bc[:, NS:]
        v = kx[0:1, :] * ext[a * Q + 5 : a * Q + 5 + Q, :]
        for j in range(1, 4):
            v = v + kx[j : j + 1, :] * ext[a * Q + 5 + j : a * Q + 5 + j + Q, :]
        x = silu(v)
        xo[a] = x.astype(BF)
        w = spread(dt * jnp.exp(end - cs), ones)
        e = dot_tn(b, (x * w).astype(BF))
        eo[a] = e
        d = spread(jnp.exp(end), ones)[0:8, :]
        do[a] = d
        state = state * d[0:1, :] + e
    st = state.T
    dec = jnp.exp(total)
    hi = dec.astype(BF).astype(F32)
    mid = (dec - hi).astype(BF).astype(F32)
    low = dec - hi - mid
    row = lax.broadcasted_iota(jnp.int32, (HH, Q), 0)
    for h in range(HH):
        p = lambda t: jnp.broadcast_to(t[h : h + 1, :], (8, Q))
        tail = jnp.where(row == 0, p(hi), jnp.where(row == 1, p(mid), jnp.where(row == 2, p(low), 0.0)))
        for q in range(4):
            d = h * 4 + q
            send[d] = jnp.concatenate([st[16 * d : 16 * d + 16, :], tail], 0).astype(BF)


def local_part(bias, alog, *args):
    s = pltpu.VMEM
    return pl.pallas_call(
        local_kernel,
        out_shape=(
            s((NQ, Q, CH), BF),
            s((NQ, Q, NS), BF),
            s((NQ, Q, NS), BF),
            s((NQ, HH, Q), F32),
            s((NQ, HH, Q), F32),
            s((NQ, NS, CH), F32),
            s((NQ, 8, CH), F32),
            s((32, 24, 128), BF),
        ),
        in_specs=[SMEM] * 2 + [VMEM] * 17,
        out_specs=(VMEM,) * 8,
        scratch_shapes=[
            pltpu.VMEM((8 + NQ * Q, CH), F32),
            pltpu.VMEM((8 + NQ * Q, BCW), F32),
            pltpu.VMEM((NQ, HH, Q), F32),
            pltpu.VMEM((Q + 16, 4096), BF),
        ],
        compiler_params=params(),
        name="local_part",
    )(bias, alog, *[in_vmem(v) for v in args])


def prefix_kernel(r, o):
    s = jnp.zeros((16, 128), F32)
    for j in range(32):
        o[j] = s.astype(BF)
        v = r[j].astype(F32)
        s = s * (v[16:17] + v[17:18] + v[18:19]) + v[0:16]


def prefix(r):
    return pl.pallas_call(
        prefix_kernel,
        out_shape=pltpu.VMEM((32, 16, 128), BF),
        in_specs=[VMEM],
        out_specs=VMEM,
        compiler_params=params(),
        name="prefix",
    )(in_vmem(r))


def diag_kernel(skip, x, b, c, cs, dt, y):
    t = lax.broadcasted_iota(jnp.int32, (Q, Q), 0)
    u = lax.broadcasted_iota(jnp.int32, (Q, Q), 1)
    tri = t >= u
    left = u < HD
    for a in range(NQ):
        scores = dot_nt(c[a], b[a])
        csr = cs[a]
        csc = csr.T
        dtr = dt[a]
        for p in range(HH // 2):
            xp = x[a, :, 128 * p : 128 * p + 128]
            ms = []
            for h in (2 * p, 2 * p + 1):
                diff = csc[:, h : h + 1] - csr[h : h + 1, :]
                m = scores * jnp.exp(jnp.where(tri, diff, -jnp.inf)) * dtr[h : h + 1, :]
                ms.append(m.astype(BF))
            xf = xp.astype(F32)
            xx = jnp.concatenate([jnp.where(left, xf, 0.0), jnp.where(left, 0.0, xf)], 0).astype(BF)
            yy = jnp.dot(jnp.concatenate(ms, 1), xx, preferred_element_type=F32)
            y[a, :, 128 * p : 128 * p + 128] = yy + jnp.where(left, skip[2 * p], skip[2 * p + 1]) * xf


def diag_part(skip, *args):
    return pl.pallas_call(
        diag_kernel,
        out_shape=pltpu.VMEM((NQ, Q, CH), F32),
        in_specs=[SMEM] + [VMEM] * 5,
        out_specs=VMEM,
        compiler_params=params(),
        name="diag_part",
    )(skip, *[in_vmem(v) for v in args])


def norm_kernel(s_in, e, d, c, cs, ydiag, gain, w_far, *refs):
    outs, (nb, w, sem) = refs[:8], refs[8:]
    copy = pltpu.make_async_copy(w_far, w, sem)
    copy.start()
    y = chip()
    mine = core()
    ones = head_spread()
    r = lax.broadcasted_iota(jnp.int32, (Q, Q), 0) // HD
    l = lax.broadcasted_iota(jnp.int32, (Q, Q), 1) // HD
    mean = jnp.where(r == l, 1.0 / HD, 0.0).astype(BF)
    state = s_in[...].astype(F32).T
    for a in range(NQ):
        yst = jnp.dot(c[a], state.astype(BF), preferred_element_type=F32)
        g = spread(jnp.exp(cs[a]), ones)
        v = ydiag[a] + g * yst
        if a < NQ - 1:
            state = state * d[a][0:1, :] + e[a]
        hi, lo = two_parts(v * v)
        for p in range(HH // 2):
            at = slice(128 * p, 128 * p + 128)
            ms = jnp.dot(hi[:, at], mean, preferred_element_type=F32)
            ms = ms + jnp.dot(lo[:, at], mean, preferred_element_type=F32)
            nb[a, :, at] = (v[:, at] * lax.rsqrt(ms + 1e-05) * gain[0:1, at]).astype(BF)

    def half(a, h):
        return nb[a, pl.ds(pl.multiple_of(h * 64, 64), 64), :]

    copy.wait()
    for j, k in enumerate((2, 1, 3, 0)):
        a = lax.rem(y + k, NQ)
        v = jnp.concatenate([half(a, 1 - mine), half(a, mine)], 0)
        v = jnp.dot(v, w[...], preferred_element_type=F32).astype(BF)
        outs[2 * j][...] = v[0:64]
        outs[2 * j + 1][...] = v[64:128]


def norm_part(*args):
    s = pltpu.VMEM
    return pl.pallas_call(
        norm_kernel,
        out_shape=(s((64, 4096), BF),) * 8,
        in_specs=[VMEM] * 7 + [pl.BlockSpec(memory_space=pltpu.HBM)],
        out_specs=(VMEM,) * 8,
        scratch_shapes=[pltpu.VMEM((NQ, Q, CH), BF), pltpu.VMEM((CH, 4096), BF), pltpu.SemaphoreType.DMA],
        compiler_params=params(),
        name="norm_part",
    )(*[in_vmem(v) for v in args[:7]], pltpu.with_memory_space_constraint(args[7], pltpu.HBM))


UP = [(y * 2 + c, ((y + 1) % 4) * 2 + c) for y in range(4) for c in range(2)]
DOWN = [(y * 2 + c, ((y - 1) % 4) * 2 + c) for y in range(4) for c in range(2)]
SWAP = [(y * 2 + c, y * 2 + 1 - c) for y in range(4) for c in range(2)]


def up(v):
    return lax.ppermute(v, "tp", UP)


def down(v):
    return lax.ppermute(v, "tp", DOWN)


def swap(v):
    return lax.ppermute(v, "tp", SWAP)


def per_device(tokens, in_x, in_bc, in_dt, conv_x, conv_bc, dt_bias, a_log, skip_d, norm_gain, out_w):
    after = lax.optimization_barrier
    lo, hi = tokens[:32], tokens[32:]
    ua, db = up(lo), down(hi)
    ub, da = up(hi), down(lo)
    *piece0, last, wx, wbc, wdt = project_near(tokens, swap(tokens), in_x, in_bc, in_dt.T)
    weights = (wx, wbc, wdt)
    spans = lax.axis_size("ctx")

    def onward(*route):
        return lax.ppermute(
            last, ("ctx", "tp"), [(i * 8 + f, i * 8 + 8 + t) for i in range(spans - 1) for f, t in route]
        )

    ua, db, wx = after((ua, db, wx))
    uu, dd = up(ua), down(db)
    ub, da, last = after((ub, da, last))
    edge_a, edge_b = onward((7, 7), (6, 1)), onward((7, 5), (6, 3))
    own = [ua, ub, da, db]
    other = [swap(v) for v in own]
    *other, uu, dd = after((*other, uu, dd))
    far = [uu, dd, swap(uu), swap(dd)]
    piece12 = project(own, other, weights, 2, "project_next")
    edge_a, edge_b, *piece12 = after((edge_a, edge_b, *piece12))
    edge = edge_a + edge_b
    edges = swap(edge)

    xc, b, c, cs, dt, e, d, send = local_part(
        dt_bias, a_log, *piece0, *piece12, *far, edge, edges, *weights, conv_x, conv_bc
    )
    got = lax.all_to_all(send, "ctx", 0, 0, tiled=True)
    ydiag = diag_part(skip_d, xc, b, c, cs, dt)
    back = lax.all_to_all(prefix(got), "ctx", 0, 0, tiled=True)
    t2, m2, t1, m1, tm, mm, t0, m0 = norm_part(back.reshape(CH, NS), e, d, c, cs, ydiag, norm_gain[None, :], out_w)

    def both(mine, theirs):
        return mine.astype(F32) + swap(theirs).astype(F32)

    q2 = both(m2, t2).astype(BF)
    q2, t1, tm, t0 = after((q2, t1, tm, t0))
    u2, d2 = up(q2[:32]), down(q2[32:])
    q1 = both(m1, t1)
    u1b = up(q1[32:].astype(BF))
    qm = both(mm, tm)
    dma = down(qm[:32].astype(BF))
    u1a = up((q1[:32] + u2.astype(F32)).astype(BF))
    dmb = down((qm[32:] + d2.astype(F32)).astype(BF))
    q0 = both(m0, t0)
    top = q0[:32] + u1a.astype(F32) + dma.astype(F32)
    bottom = q0[32:] + u1b.astype(F32) + dmb.astype(F32)
    return jnp.concatenate([top.astype(BF), bottom.astype(BF)], 0)


def solution(mesh):
    return jax.shard_map(
        per_device,
        mesh=mesh,
        in_specs=(
            P(("ctx", "tp"), None),
            P(None, "tp"),
            P(),
            P(None, "tp"),
            P(None, "tp"),
            P(),
            P("tp"),
            P("tp"),
            P("tp"),
            P("tp"),
            P("tp", None),
        ),
        out_specs=P(("ctx", "tp"), None),
        check_vma=False,
    )
```

```python
import functools

import jax
import jax.numpy as jnp
from jax import lax
from jax.experimental import pallas as pl
from jax.experimental.pallas import tpu as pltpu
from jax.sharding import PartitionSpec as P

BF = jnp.bfloat16
F32 = jnp.float32
VMEM = pl.BlockSpec(memory_space=pltpu.VMEM)
SMEM = pl.BlockSpec(memory_space=pltpu.SMEM)
LIMIT = 14 * 1024 * 1024

Q = 128
NQ = 4
HH = 8
HD = 64
NS = 128
CH = 512
BCW = 256


def params():
    return pltpu.CompilerParams(vmem_limit_bytes=LIMIT)


def dot_tn(a, b):
    return lax.dot_general(a, b, (((0,), (0,)), ((), ())), preferred_element_type=F32)


def dot_nt(a, b):
    return lax.dot_general(a, b, (((1,), (1,)), ((), ())), preferred_element_type=F32)


def two_parts(v):
    hi = v.astype(BF)
    return hi, (v - hi.astype(F32)).astype(BF)


def head_spread():
    row = lax.broadcasted_iota(jnp.int32, (2 * HH, CH), 0)
    lane = lax.broadcasted_iota(jnp.int32, (2 * HH, CH), 1)
    return jnp.where(lane // HD == row % HH, 1.0, 0.0).astype(BF)


def spread(v, ones):
    hi, lo = two_parts(v)
    both = jnp.concatenate([hi.astype(F32), lo.astype(F32)], 0).astype(BF)
    return dot_tn(both, ones)


def chip():
    return lax.axis_index("tp") // 2


def core():
    return lax.rem(lax.axis_index("tp"), 2)


def in_vmem(v):
    return pltpu.with_memory_space_constraint(v, pltpu.VMEM)


def place(tok, ref, base, half):
    at = base + half * 32
    tok[pl.ds(pl.multiple_of(at, 32), 32), :] = ref[0:32, :]
    tok[pl.ds(pl.multiple_of(at + 64, 32), 32), :] = ref[32:64, :]


def pack_kernel(mine, theirs, first, second, last):
    c = core()
    for part, ref in ((c, mine), (1 - c, theirs)):
        at = pl.ds(pl.multiple_of(part * 32, 32), 32)
        first[at, :] = ref[pl.ds(pl.multiple_of(c * 32, 32), 32), :]
        second[at, :] = ref[pl.ds(pl.multiple_of((1 - c) * 32, 32), 32), :]
    end = jnp.where(c == 1, mine[48:64].astype(F32), theirs[48:64].astype(F32))
    last[...] = end[8:16].astype(BF)


def pack(mine, theirs):
    return pl.pallas_call(
        pack_kernel,
        out_shape=(pltpu.VMEM((64, 4096), BF), pltpu.VMEM((64, 4096), BF), pltpu.VMEM((8, 4096), BF)),
        in_specs=[VMEM] * 2,
        out_specs=(VMEM,) * 3,
        compiler_params=params(),
        name="pack",
    )(in_vmem(mine), in_vmem(theirs))


def next_kernel(r1, r2, s1, s2, wx, wbc, wdt, xo, bco, dto, tok):
    c = core()
    place(tok, r1, c * Q, c)
    place(tok, r2, c * Q, 1 - c)
    place(tok, s1, (1 - c) * Q, 1 - c)
    place(tok, s2, (1 - c) * Q, c)
    rows = tok[...]
    xo[...] = jnp.dot(rows, wx[...], preferred_element_type=F32).astype(BF)
    bco[...] = jnp.dot(rows, wbc[...], preferred_element_type=F32).astype(BF)
    dt = dot_nt(rows, wdt[...])
    for j in range(2):
        dto[j] = dt[j * Q : (j + 1) * Q].T


def project_next(*args):
    return pl.pallas_call(
        next_kernel,
        out_shape=(
            pltpu.VMEM((2 * Q, CH), BF),
            pltpu.VMEM((2 * Q, BCW), BF),
            pltpu.VMEM((2, HH, Q), F32),
        ),
        in_specs=[VMEM] * 7,
        out_specs=(VMEM, VMEM, VMEM),
        scratch_shapes=[pltpu.VMEM((2 * Q, 4096), BF)],
        compiler_params=params(),
        name="project_next",
    )(*[in_vmem(v) for v in args])


def near_kernel(mine, theirs, wx_far, wbc_far, wdt_far, xo, bco, dto, wx, wbc, wdt, tok, sems):
    c = core()
    pairs = (
        (mine, tok.at[pl.ds(pl.multiple_of(c * 64, 64), 64), :]),
        (wx_far, wx),
        (wdt_far, wdt),
        (wbc_far, wbc),
    )
    copies = [pltpu.make_async_copy(f, t, sems.at[j]) for j, (f, t) in enumerate(pairs)]
    for copy in copies:
        copy.start()
    tok[pl.ds(pl.multiple_of((1 - c) * 64, 64), 64), :] = theirs[...]
    copies[0].wait()
    copies[1].wait()
    rows = tok[...]
    xo[...] = jnp.dot(rows, wx[...], preferred_element_type=F32).astype(BF)
    copies[2].wait()
    dto[0] = dot_nt(rows, wdt[...]).T
    copies[3].wait()
    bco[...] = jnp.dot(rows, wbc[...], preferred_element_type=F32).astype(BF)


def project_near(mine, theirs, in_x, in_bc, in_dt):
    hbm = pl.BlockSpec(memory_space=pltpu.HBM)
    far = lambda v: pltpu.with_memory_space_constraint(v, pltpu.HBM)
    return pl.pallas_call(
        near_kernel,
        out_shape=(
            pltpu.VMEM((Q, CH), BF),
            pltpu.VMEM((Q, BCW), BF),
            pltpu.VMEM((1, HH, Q), F32),
            pltpu.VMEM(in_x.shape, BF),
            pltpu.VMEM(in_bc.shape, BF),
            pltpu.VMEM(in_dt.shape, BF),
        ),
        in_specs=[hbm, VMEM, hbm, hbm, hbm],
        out_specs=(VMEM,) * 6,
        scratch_shapes=[pltpu.VMEM((Q, 4096), BF), pltpu.SemaphoreType.DMA((4,))],
        compiler_params=params(),
        name="project_near",
    )(far(mine), in_vmem(theirs), far(in_x), far(in_bc), far(in_dt))


def silu(v):
    return v / (1.0 + jnp.exp(-v))


def softplus(v):
    return jnp.maximum(v, 0.0) + jnp.log1p(jnp.exp(-jnp.abs(v)))


def column(ref):
    row = lax.broadcasted_iota(jnp.int32, (HH, Q), 0)
    v = jnp.full((HH, Q), ref[0], F32)
    for h in range(1, HH):
        v = jnp.where(row == h, ref[h], v)
    return v


OFFS = (0, 3, 1, 2)


def local_kernel(bias, alog, *refs):
    x0, bc0, dt0, x12, bc12, dt12 = refs[0:6]
    far, far_swap, halo, haloswap = refs[6:10]
    wx, wbc, wdt, kx, kbc = refs[10:15]
    (xo, bo, co, cso, dto, eo, do, send) = refs[15:23]
    ext, extb, dtr, tok = refs[23:27]
    y = chip()
    place(tok, far, 0, core())
    place(tok, far_swap, 0, 1 - core())
    edge = halo[...].astype(F32) + haloswap[...].astype(F32)
    tok[Q : Q + 16, :] = jnp.concatenate([edge, edge], 0).astype(BF)
    rows = tok[...]
    x3 = jnp.dot(rows, wx[...], preferred_element_type=F32).astype(BF).astype(F32)
    bc3 = jnp.dot(rows, wbc[...], preferred_element_type=F32).astype(BF).astype(F32)
    dt3 = dot_nt(rows[0:Q], wdt[...]).T
    ext[0:8, :] = x3[Q : Q + 8]
    extb[0:8, :] = bc3[Q : Q + 8]
    pieces = (
        (x0[...], bc0[...], dt0[0]),
        (x12[0:Q], bc12[0:Q], dt12[0]),
        (x12[Q : 2 * Q], bc12[Q : 2 * Q], dt12[1]),
        (x3[0:Q], bc3[0:Q], dt3),
    )
    for k, (px, pbc, pdt) in enumerate(pieces):
        a = lax.rem(y + OFFS[k], NQ)
        at = pl.multiple_of(a * Q + 8, 8)
        ext[pl.ds(at, Q), :] = px.astype(F32)
        extb[pl.ds(at, Q), :] = pbc.astype(F32)
        dtr[a] = pdt
    ones = head_spread()
    lane = lax.broadcasted_iota(jnp.int32, (HH, Q), 1)
    decay = -jnp.exp(column(alog))
    bias_col = column(bias)
    total = jnp.zeros((HH, Q), F32)
    state = jnp.zeros((NS, CH), F32)
    for a in range(NQ):
        dt = softplus(dtr[a] + bias_col)
        cs = decay * dt
        for s in (1, 2, 4, 8, 16, 32, 64):
            cs = cs + jnp.where(lane >= s, pltpu.roll(cs, s, 1), 0.0)
        end = jnp.broadcast_to(cs[:, Q - 1 : Q], (HH, Q))
        dto[a] = dt
        cso[a] = cs
        total = total + end
        v = kbc[0:1, :] * extb[a * Q + 5 : a * Q + 5 + Q, :]
        for j in range(1, 4):
            v = v + kbc[j : j + 1, :] * extb[a * Q + 5 + j : a * Q + 5 + j + Q, :]
        bc = silu(v).astype(BF)
        b = bc[:, :NS]
        bo[a] = b
        co[a] = bc[:, NS:]
        v = kx[0:1, :] * ext[a * Q + 5 : a * Q + 5 + Q, :]
        for j in range(1, 4):
            v = v + kx[j : j + 1, :] * ext[a * Q + 5 + j : a * Q + 5 + j + Q, :]
        x = silu(v)
        xo[a] = x.astype(BF)
        w = spread(dt * jnp.exp(end - cs), ones)
        e = dot_tn(b, (x * w).astype(BF))
        eo[a] = e
        d = spread(jnp.exp(end), ones)[0:8, :]
        do[a] = d
        state = state * d[0:1, :] + e
    st = state.T
    dec = jnp.exp(total)
    hi = dec.astype(BF).astype(F32)
    mid = (dec - hi).astype(BF).astype(F32)
    low = dec - hi - mid
    row = lax.broadcasted_iota(jnp.int32, (HH, Q), 0)
    for h in range(HH):
        p = lambda t: jnp.broadcast_to(t[h : h + 1, :], (8, Q))
        tail = jnp.where(row == 0, p(hi), jnp.where(row == 1, p(mid), jnp.where(row == 2, p(low), 0.0)))
        for q in range(4):
            d = h * 4 + q
            send[d] = jnp.concatenate([st[16 * d : 16 * d + 16, :], tail], 0).astype(BF)


def local_part(bias, alog, *args):
    s = pltpu.VMEM
    return pl.pallas_call(
        local_kernel,
        out_shape=(
            s((NQ, Q, CH), BF),
            s((NQ, Q, NS), BF),
            s((NQ, Q, NS), BF),
            s((NQ, HH, Q), F32),
            s((NQ, HH, Q), F32),
            s((NQ, NS, CH), F32),
            s((NQ, 8, CH), F32),
            s((32, 24, 128), BF),
        ),
        in_specs=[SMEM] * 2 + [VMEM] * 15,
        out_specs=(VMEM,) * 8,
        scratch_shapes=[
            pltpu.VMEM((8 + NQ * Q, CH), F32),
            pltpu.VMEM((8 + NQ * Q, BCW), F32),
            pltpu.VMEM((NQ, HH, Q), F32),
            pltpu.VMEM((Q + 16, 4096), BF),
        ],
        compiler_params=params(),
        name="local_part",
    )(bias, alog, *[in_vmem(v) for v in args])


def prefix_kernel(r, o):
    s = jnp.zeros((16, 128), F32)
    for j in range(32):
        o[j] = s.astype(BF)
        v = r[j].astype(F32)
        s = s * (v[16:17] + v[17:18] + v[18:19]) + v[0:16]


def prefix(r):
    return pl.pallas_call(
        prefix_kernel,
        out_shape=pltpu.VMEM((32, 16, 128), BF),
        in_specs=[VMEM],
        out_specs=VMEM,
        compiler_params=params(),
        name="prefix",
    )(in_vmem(r))


def diag_kernel(skip, x, b, c, cs, dt, y):
    t = lax.broadcasted_iota(jnp.int32, (Q, Q), 0)
    u = lax.broadcasted_iota(jnp.int32, (Q, Q), 1)
    tri = t >= u
    left = u < HD
    for a in range(NQ):
        scores = dot_nt(c[a], b[a])
        csr = cs[a]
        csc = csr.T
        dtr = dt[a]
        for p in range(HH // 2):
            xp = x[a, :, 128 * p : 128 * p + 128]
            ms = []
            for h in (2 * p, 2 * p + 1):
                diff = csc[:, h : h + 1] - csr[h : h + 1, :]
                m = scores * jnp.exp(jnp.where(tri, diff, -jnp.inf)) * dtr[h : h + 1, :]
                ms.append(m.astype(BF))
            xf = xp.astype(F32)
            xx = jnp.concatenate([jnp.where(left, xf, 0.0), jnp.where(left, 0.0, xf)], 0).astype(BF)
            yy = jnp.dot(jnp.concatenate(ms, 1), xx, preferred_element_type=F32)
            y[a, :, 128 * p : 128 * p + 128] = yy + jnp.where(left, skip[2 * p], skip[2 * p + 1]) * xf


def diag_part(skip, *args):
    return pl.pallas_call(
        diag_kernel,
        out_shape=pltpu.VMEM((NQ, Q, CH), F32),
        in_specs=[SMEM] + [VMEM] * 5,
        out_specs=VMEM,
        compiler_params=params(),
        name="diag_part",
    )(skip, *[in_vmem(v) for v in args])


def norm_kernel(s_in, e, d, c, cs, ydiag, gain, w_far, other, own, rest, w, nb, sem):
    copy = pltpu.make_async_copy(w_far, w, sem)
    copy.start()
    y = chip()
    mine = core()
    ones = head_spread()
    r = lax.broadcasted_iota(jnp.int32, (Q, Q), 0) // HD
    l = lax.broadcasted_iota(jnp.int32, (Q, Q), 1) // HD
    mean = jnp.where(r == l, 1.0 / HD, 0.0).astype(BF)
    state = s_in[...].astype(F32).T
    for a in range(NQ):
        yst = jnp.dot(c[a], state.astype(BF), preferred_element_type=F32)
        g = spread(jnp.exp(cs[a]), ones)
        v = ydiag[a] + g * yst
        if a < NQ - 1:
            state = state * d[a][0:1, :] + e[a]
        hi, lo = two_parts(v * v)
        for p in range(HH // 2):
            at = slice(128 * p, 128 * p + 128)
            ms = jnp.dot(hi[:, at], mean, preferred_element_type=F32)
            ms = ms + jnp.dot(lo[:, at], mean, preferred_element_type=F32)
            nb[a, :, at] = (v[:, at] * lax.rsqrt(ms + 1e-05) * gain[0:1, at]).astype(BF)

    def half(a, h):
        return nb[a, pl.ds(pl.multiple_of(h * 64, 64), 64), :]

    a = lax.rem(y + 2, NQ)
    v = jnp.concatenate([half(a, 1 - mine), half(a, mine)], 0)
    copy.wait()
    v = jnp.dot(v, w[...], preferred_element_type=F32).astype(BF)
    other[...] = v[0:64]
    own[...] = v[64:128]
    side, across = lax.rem(y + 1 + 2 * mine, NQ), lax.rem(y + 3 - 2 * mine, NQ)
    parts = ((across, mine), (across, 1 - mine), (side, 1 - mine), (side, mine), (y, 1 - mine), (y, mine))
    for j, (a, h) in enumerate(parts):
        rest[64 * j : 64 * j + 64, :] = half(a, h)


def norm_part(*args):
    s = pltpu.VMEM
    return pl.pallas_call(
        norm_kernel,
        out_shape=(s((64, 4096), BF), s((64, 4096), BF), s((384, CH), BF), s((CH, 4096), BF)),
        in_specs=[VMEM] * 7 + [pl.BlockSpec(memory_space=pltpu.HBM)],
        out_specs=(VMEM,) * 4,
        scratch_shapes=[pltpu.VMEM((NQ, Q, CH), BF), pltpu.SemaphoreType.DMA],
        compiler_params=params(),
        name="norm_part",
    )(*[in_vmem(v) for v in args[:7]], pltpu.with_memory_space_constraint(args[7], pltpu.HBM))


def out_kernel(n, w, *outs):
    v = jnp.dot(n[...], w[...], preferred_element_type=F32).astype(BF)
    for j, o in enumerate(outs):
        o[...] = v[64 * j : 64 * j + 64]


def out_part(n, w):
    s = pltpu.VMEM
    return pl.pallas_call(
        out_kernel,
        out_shape=(s((64, 4096), BF),) * 6,
        in_specs=[VMEM] * 2,
        out_specs=(VMEM,) * 6,
        compiler_params=params(),
        name="out_part",
    )(in_vmem(n), in_vmem(w))


SWAP = [(y * 2 + c, y * 2 + 1 - c) for y in range(4) for c in range(2)]


AROUND = [(y * 2 + c, ((y + 1 - 2 * c) % 4) * 2 + c) for y in range(4) for c in range(2)]


def around(v):
    return lax.ppermute(v, "tp", AROUND)


def swap(v):
    return lax.ppermute(v, "tp", SWAP)


def per_device(tokens, in_x, in_bc, in_dt, conv_x, conv_bc, dt_bias, a_log, skip_d, norm_gain, out_w):
    after = lax.optimization_barrier
    partner = swap(tokens)
    first, second, last = pack(tokens, partner)
    r1, r2 = around(first), around(second)
    spans = lax.axis_size("ctx")

    def onward(*route):
        return lax.ppermute(
            last, ("ctx", "tp"), [(i * 8 + f, i * 8 + 8 + t) for i in range(spans - 1) for f, t in route]
        )

    edge = onward((7, 7), (6, 1)) + onward((7, 5), (6, 3))
    *piece0, wx, wbc, wdt = project_near(tokens, partner, in_x, in_bc, in_dt.T)
    weights = (wx, wbc, wdt)
    r1, wx = after((r1, wx))
    far = around(r1)
    r2, edge = after((r2, edge))
    edges = swap(edge)
    piece12 = project_next(r1, r2, swap(r1), swap(r2), *weights)
    far, *piece12 = after((far, *piece12))

    xc, b, c, cs, dt, e, d, send = local_part(
        dt_bias, a_log, *piece0, *piece12, far, swap(far), edge, edges, *weights, conv_x, conv_bc
    )
    got = lax.all_to_all(send, "ctx", 0, 0, tiled=True)
    ydiag = diag_part(skip_d, xc, b, c, cs, dt)
    back = lax.all_to_all(prefix(got), "ctx", 0, 0, tiled=True)
    other, own, rest, w = norm_part(back.reshape(CH, NS), e, d, c, cs, ydiag, norm_gain[None, :], out_w)

    def both(mine, theirs):
        return mine.astype(F32) + swap(theirs).astype(F32)

    q2 = both(own, other).astype(BF)
    give_raw, give_sum, keep_raw, keep_sum, give, keep = out_part(rest, w)
    q2, give_raw, give_sum, give = after((q2, give_raw, give_sum, give))
    first = around(q2)
    raw = around(both(keep_raw, give_raw).astype(BF))
    summed = around((both(keep_sum, give_sum) + first.astype(F32)).astype(BF))
    return (both(keep, give) + swap(raw).astype(F32) + summed.astype(F32)).astype(BF)


def solution(mesh):
    return jax.shard_map(
        per_device,
        mesh=mesh,
        in_specs=(
            P(("ctx", "tp"), None),
            P(None, "tp"),
            P(),
            P(None, "tp"),
            P(None, "tp"),
            P(),
            P("tp"),
            P("tp"),
            P("tp"),
            P("tp"),
            P("tp", None),
        ),
        out_specs=P(("ctx", "tp"), None),
        check_vma=False,
    )
```

```python
import functools

import jax
import jax.numpy as jnp
from jax import lax
from jax.experimental import pallas as pl
from jax.experimental.pallas import tpu as pltpu
from jax.sharding import PartitionSpec as P

BF = jnp.bfloat16
F32 = jnp.float32
VMEM = pl.BlockSpec(memory_space=pltpu.VMEM)
SMEM = pl.BlockSpec(memory_space=pltpu.SMEM)
LIMIT = 14 * 1024 * 1024

Q = 128
NQ = 4
HH = 8
HD = 64
NS = 128
CH = 512
BCW = 256


def params():
    return pltpu.CompilerParams(vmem_limit_bytes=LIMIT)


def dot_tn(a, b):
    return lax.dot_general(a, b, (((0,), (0,)), ((), ())), preferred_element_type=F32)


def dot_nt(a, b):
    return lax.dot_general(a, b, (((1,), (1,)), ((), ())), preferred_element_type=F32)


def two_parts(v):
    hi = v.astype(BF)
    return hi, (v - hi.astype(F32)).astype(BF)


def head_spread():
    row = lax.broadcasted_iota(jnp.int32, (2 * HH, CH), 0)
    lane = lax.broadcasted_iota(jnp.int32, (2 * HH, CH), 1)
    return jnp.where(lane // HD == row % HH, 1.0, 0.0).astype(BF)


def spread(v, ones):
    hi, lo = two_parts(v)
    both = jnp.concatenate([hi.astype(F32), lo.astype(F32)], 0).astype(BF)
    return dot_tn(both, ones)


def chip():
    return lax.axis_index("tp") // 2


def core():
    return lax.rem(lax.axis_index("tp"), 2)


def in_vmem(v):
    return pltpu.with_memory_space_constraint(v, pltpu.VMEM)


def place(tok, ref, base, half):
    at = base + half * 32
    tok[pl.ds(pl.multiple_of(at, 32), 32), :] = ref[0:32, :]
    tok[pl.ds(pl.multiple_of(at + 64, 32), 32), :] = ref[32:64, :]


def pack_kernel(far, theirs, first, second, last, mine, sem):
    c = core()
    copy = pltpu.make_async_copy(far, mine, sem)
    copy.start()
    for part, ref in ((1 - c, theirs), (c, mine)):
        if ref is mine:
            copy.wait()
        at = pl.ds(pl.multiple_of(part * 32, 32), 32)
        first[at, :] = ref[pl.ds(pl.multiple_of(c * 32, 32), 32), :]
        second[at, :] = ref[pl.ds(pl.multiple_of((1 - c) * 32, 32), 32), :]
    end = jnp.where(c == 1, mine[48:64].astype(F32), theirs[48:64].astype(F32))
    last[...] = end[8:16].astype(BF)


def pack(mine, theirs):
    return pl.pallas_call(
        pack_kernel,
        out_shape=(pltpu.VMEM((64, 4096), BF), pltpu.VMEM((64, 4096), BF), pltpu.VMEM((8, 4096), BF)),
        in_specs=[pl.BlockSpec(memory_space=pltpu.HBM), VMEM],
        out_specs=(VMEM,) * 3,
        scratch_shapes=[pltpu.VMEM((64, 4096), BF), pltpu.SemaphoreType.DMA],
        compiler_params=params(),
        name="pack",
    )(pltpu.with_memory_space_constraint(mine, pltpu.HBM), in_vmem(theirs))


def next_kernel(r1, r2, s1, s2, wx, wbc, wdt, xo, bco, dto, tok):
    c = core()
    place(tok, r1, c * Q, c)
    place(tok, r2, c * Q, 1 - c)
    place(tok, s1, (1 - c) * Q, 1 - c)
    place(tok, s2, (1 - c) * Q, c)
    rows = tok[...]
    xo[...] = jnp.dot(rows, wx[...], preferred_element_type=F32).astype(BF)
    bco[...] = jnp.dot(rows, wbc[...], preferred_element_type=F32).astype(BF)
    dt = dot_nt(rows, wdt[...])
    for j in range(2):
        dto[j] = dt[j * Q : (j + 1) * Q].T


def project_next(*args):
    return pl.pallas_call(
        next_kernel,
        out_shape=(
            pltpu.VMEM((2 * Q, CH), BF),
            pltpu.VMEM((2 * Q, BCW), BF),
            pltpu.VMEM((2, HH, Q), F32),
        ),
        in_specs=[VMEM] * 7,
        out_specs=(VMEM, VMEM, VMEM),
        scratch_shapes=[pltpu.VMEM((2 * Q, 4096), BF)],
        compiler_params=params(),
        name="project_next",
    )(*[in_vmem(v) for v in args])


def near_kernel(mine, theirs, wx_far, wbc_far, wdt_far, xo, bco, dto, wx, wbc, wdt, tok, sems):
    c = core()
    pairs = (
        (mine, tok.at[pl.ds(pl.multiple_of(c * 64, 64), 64), :]),
        (wx_far, wx),
        (wdt_far, wdt),
        (wbc_far, wbc),
    )
    copies = [pltpu.make_async_copy(f, t, sems.at[j]) for j, (f, t) in enumerate(pairs)]
    for copy in copies:
        copy.start()
    tok[pl.ds(pl.multiple_of((1 - c) * 64, 64), 64), :] = theirs[...]
    copies[0].wait()
    copies[1].wait()
    rows = tok[...]
    xo[...] = jnp.dot(rows, wx[...], preferred_element_type=F32).astype(BF)
    copies[2].wait()
    dto[0] = dot_nt(rows, wdt[...]).T
    copies[3].wait()
    bco[...] = jnp.dot(rows, wbc[...], preferred_element_type=F32).astype(BF)


def project_near(mine, theirs, in_x, in_bc, in_dt):
    hbm = pl.BlockSpec(memory_space=pltpu.HBM)
    far = lambda v: pltpu.with_memory_space_constraint(v, pltpu.HBM)
    return pl.pallas_call(
        near_kernel,
        out_shape=(
            pltpu.VMEM((Q, CH), BF),
            pltpu.VMEM((Q, BCW), BF),
            pltpu.VMEM((1, HH, Q), F32),
            pltpu.VMEM(in_x.shape, BF),
            pltpu.VMEM(in_bc.shape, BF),
            pltpu.VMEM(in_dt.shape, BF),
        ),
        in_specs=[hbm, VMEM, hbm, hbm, hbm],
        out_specs=(VMEM,) * 6,
        scratch_shapes=[pltpu.VMEM((Q, 4096), BF), pltpu.SemaphoreType.DMA((4,))],
        compiler_params=params(),
        name="project_near",
    )(far(mine), in_vmem(theirs), far(in_x), far(in_bc), far(in_dt))


def silu(v):
    half = 0.5 * v
    return half + half * jnp.tanh(half)


def softplus(v):
    return jnp.maximum(v, 0.0) + jnp.log1p(jnp.exp(-jnp.abs(v)))


def column(ref):
    row = lax.broadcasted_iota(jnp.int32, (HH, Q), 0)
    v = jnp.full((HH, Q), ref[0], F32)
    for h in range(1, HH):
        v = jnp.where(row == h, ref[h], v)
    return v


OFFS = (0, 3, 1, 2)


def local_kernel(bias, alog, *refs):
    x0, bc0, dt0, x12, bc12, dt12 = refs[0:6]
    far, far_swap, halo, haloswap = refs[6:10]
    wx, wbc, wdt, kx, kbc = refs[10:15]
    (xo, bo, co, cso, dto, eo, do, send) = refs[15:23]
    ext, extb, dtr, tok = refs[23:27]
    y = chip()
    place(tok, far, 0, core())
    place(tok, far_swap, 0, 1 - core())
    edge = halo[...].astype(F32) + haloswap[...].astype(F32)
    tok[Q : Q + 16, :] = jnp.concatenate([edge, edge], 0).astype(BF)
    rows = tok[...]
    x3 = jnp.dot(rows, wx[...], preferred_element_type=F32).astype(BF).astype(F32)
    bc3 = jnp.dot(rows, wbc[...], preferred_element_type=F32).astype(BF).astype(F32)
    dt3 = dot_nt(rows[0:Q], wdt[...]).T
    ext[0:8, :] = x3[Q : Q + 8]
    extb[0:8, :] = bc3[Q : Q + 8]
    pieces = (
        (x0[...], bc0[...], dt0[0]),
        (x12[0:Q], bc12[0:Q], dt12[0]),
        (x12[Q : 2 * Q], bc12[Q : 2 * Q], dt12[1]),
        (x3[0:Q], bc3[0:Q], dt3),
    )
    for k, (px, pbc, pdt) in enumerate(pieces):
        a = lax.rem(y + OFFS[k], NQ)
        at = pl.multiple_of(a * Q + 8, 8)
        ext[pl.ds(at, Q), :] = px.astype(F32)
        extb[pl.ds(at, Q), :] = pbc.astype(F32)
        dtr[a] = pdt
    ones = head_spread()
    lane = lax.broadcasted_iota(jnp.int32, (HH, Q), 1)
    decay = -jnp.exp(column(alog))
    bias_col = column(bias)
    total = jnp.zeros((HH, Q), F32)
    state = jnp.zeros((NS, CH), F32)
    for a in range(NQ):
        dt = softplus(dtr[a] + bias_col)
        cs = decay * dt
        for s in (1, 2, 4, 8, 16, 32, 64):
            cs = cs + jnp.where(lane >= s, pltpu.roll(cs, s, 1), 0.0)
        end = jnp.broadcast_to(cs[:, Q - 1 : Q], (HH, Q))
        dto[a] = dt
        cso[a] = cs
        total = total + end
        v = kbc[0:1, :] * extb[a * Q + 5 : a * Q + 5 + Q, :]
        for j in range(1, 4):
            v = v + kbc[j : j + 1, :] * extb[a * Q + 5 + j : a * Q + 5 + j + Q, :]
        bc = silu(v).astype(BF)
        b = bc[:, :NS]
        bo[a] = b
        co[a] = bc[:, NS:]
        v = kx[0:1, :] * ext[a * Q + 5 : a * Q + 5 + Q, :]
        for j in range(1, 4):
            v = v + kx[j : j + 1, :] * ext[a * Q + 5 + j : a * Q + 5 + j + Q, :]
        x = silu(v)
        xo[a] = x.astype(BF)
        w = spread(dt * jnp.exp(end - cs), ones)
        e = dot_tn(b, (x * w).astype(BF))
        eo[a] = e
        d = spread(jnp.exp(end), ones)[0:8, :]
        do[a] = d
        state = state * d[0:1, :] + e
    st = state.T
    dec = jnp.exp(total)
    hi = dec.astype(BF).astype(F32)
    mid = (dec - hi).astype(BF).astype(F32)
    low = dec - hi - mid
    row = lax.broadcasted_iota(jnp.int32, (HH, Q), 0)
    for h in range(HH):
        p = lambda t: jnp.broadcast_to(t[h : h + 1, :], (8, Q))
        tail = jnp.where(row == 0, p(hi), jnp.where(row == 1, p(mid), jnp.where(row == 2, p(low), 0.0)))
        for q in range(4):
            d = h * 4 + q
            send[d] = jnp.concatenate([st[16 * d : 16 * d + 16, :], tail], 0).astype(BF)


def local_part(bias, alog, *args):
    s = pltpu.VMEM
    return pl.pallas_call(
        local_kernel,
        out_shape=(
            s((NQ, Q, CH), BF),
            s((NQ, Q, NS), BF),
            s((NQ, Q, NS), BF),
            s((NQ, HH, Q), F32),
            s((NQ, HH, Q), F32),
            s((NQ, NS, CH), F32),
            s((NQ, 8, CH), F32),
            s((32, 24, 128), BF),
        ),
        in_specs=[SMEM] * 2 + [VMEM] * 15,
        out_specs=(VMEM,) * 8,
        scratch_shapes=[
            pltpu.VMEM((8 + NQ * Q, CH), F32),
            pltpu.VMEM((8 + NQ * Q, BCW), F32),
            pltpu.VMEM((NQ, HH, Q), F32),
            pltpu.VMEM((Q + 16, 4096), BF),
        ],
        compiler_params=params(),
        name="local_part",
    )(bias, alog, *[in_vmem(v) for v in args])


def prefix_kernel(r, o):
    s = jnp.zeros((16, 128), F32)
    for j in range(32):
        o[j] = s.astype(BF)
        v = r[j].astype(F32)
        s = s * (v[16:17] + v[17:18] + v[18:19]) + v[0:16]


def prefix(r):
    return pl.pallas_call(
        prefix_kernel,
        out_shape=pltpu.VMEM((32, 16, 128), BF),
        in_specs=[VMEM],
        out_specs=VMEM,
        compiler_params=params(),
        name="prefix",
    )(in_vmem(r))


def diag_kernel(skip, w_far, x, b, c, cs, dt, y, w, sem):
    copy = pltpu.make_async_copy(w_far, w, sem)
    copy.start()
    t = lax.broadcasted_iota(jnp.int32, (Q, Q), 0)
    u = lax.broadcasted_iota(jnp.int32, (Q, Q), 1)
    tri = t >= u
    left = u < HD
    for a in range(NQ):
        scores = dot_nt(c[a], b[a])
        csr = cs[a]
        csc = csr.T
        dtr = dt[a]
        for p in range(HH // 2):
            xp = x[a, :, 128 * p : 128 * p + 128]
            ms = []
            for h in (2 * p, 2 * p + 1):
                diff = csc[:, h : h + 1] - csr[h : h + 1, :]
                m = scores * jnp.exp(jnp.where(tri, diff, -jnp.inf)) * dtr[h : h + 1, :]
                ms.append(m.astype(BF))
            xf = xp.astype(F32)
            xx = jnp.concatenate([jnp.where(left, xf, 0.0), jnp.where(left, 0.0, xf)], 0).astype(BF)
            yy = jnp.dot(jnp.concatenate(ms, 1), xx, preferred_element_type=F32)
            y[a, :, 128 * p : 128 * p + 128] = yy + jnp.where(left, skip[2 * p], skip[2 * p + 1]) * xf
    copy.wait()


def diag_part(skip, w, *args):
    return pl.pallas_call(
        diag_kernel,
        out_shape=(pltpu.VMEM((NQ, Q, CH), F32), pltpu.VMEM(w.shape, BF)),
        in_specs=[SMEM, pl.BlockSpec(memory_space=pltpu.HBM)] + [VMEM] * 5,
        out_specs=(VMEM, VMEM),
        scratch_shapes=[pltpu.SemaphoreType.DMA],
        compiler_params=params(),
        name="diag_part",
    )(skip, pltpu.with_memory_space_constraint(w, pltpu.HBM), *[in_vmem(v) for v in args])


def norm_kernel(s_in, e, d, c, cs, ydiag, gain, w, other, own, rest, nb):
    y = chip()
    mine = core()
    ones = head_spread()
    r = lax.broadcasted_iota(jnp.int32, (Q, Q), 0) // HD
    l = lax.broadcasted_iota(jnp.int32, (Q, Q), 1) // HD
    mean = jnp.where(r == l, 1.0 / HD, 0.0).astype(BF)
    state = s_in[...].astype(F32).T
    for a in range(NQ):
        yst = jnp.dot(c[a], state.astype(BF), preferred_element_type=F32)
        g = spread(jnp.exp(cs[a]), ones)
        v = ydiag[a] + g * yst
        if a < NQ - 1:
            state = state * d[a][0:1, :] + e[a]
        hi, lo = two_parts(v * v)
        for p in range(HH // 2):
            at = slice(128 * p, 128 * p + 128)
            ms = jnp.dot(hi[:, at], mean, preferred_element_type=F32)
            ms = ms + jnp.dot(lo[:, at], mean, preferred_element_type=F32)
            nb[a, :, at] = (v[:, at] * lax.rsqrt(ms + 1e-05) * gain[0:1, at]).astype(BF)

    def half(a, h):
        return nb[a, pl.ds(pl.multiple_of(h * 64, 64), 64), :]

    a = lax.rem(y + 2, NQ)
    v = jnp.concatenate([half(a, 1 - mine), half(a, mine)], 0)
    v = jnp.dot(v, w[...], preferred_element_type=F32).astype(BF)
    other[...] = v[0:64]
    own[...] = v[64:128]
    side, across = lax.rem(y + 1 + 2 * mine, NQ), lax.rem(y + 3 - 2 * mine, NQ)
    parts = ((across, mine), (across, 1 - mine), (side, 1 - mine), (side, mine), (y, 1 - mine), (y, mine))
    for j, (a, h) in enumerate(parts):
        rest[64 * j : 64 * j + 64, :] = half(a, h)


def norm_part(*args):
    s = pltpu.VMEM
    return pl.pallas_call(
        norm_kernel,
        out_shape=(s((64, 4096), BF), s((64, 4096), BF), s((384, CH), BF)),
        in_specs=[VMEM] * 8,
        out_specs=(VMEM,) * 3,
        scratch_shapes=[pltpu.VMEM((NQ, Q, CH), BF)],
        compiler_params=params(),
        name="norm_part",
    )(*[in_vmem(v) for v in args])


def out_kernel(n, w, *outs):
    v = jnp.dot(n[...], w[...], preferred_element_type=F32).astype(BF)
    for j, o in enumerate(outs):
        o[...] = v[64 * j : 64 * j + 64]


def out_part(n, w):
    s = pltpu.VMEM
    return pl.pallas_call(
        out_kernel,
        out_shape=(s((64, 4096), BF),) * 6,
        in_specs=[VMEM] * 2,
        out_specs=(VMEM,) * 6,
        compiler_params=params(),
        name="out_part",
    )(in_vmem(n), in_vmem(w))


SWAP = [(y * 2 + c, y * 2 + 1 - c) for y in range(4) for c in range(2)]


AROUND = [(y * 2 + c, ((y + 1 - 2 * c) % 4) * 2 + c) for y in range(4) for c in range(2)]


def around(v):
    return lax.ppermute(v, "tp", AROUND)


def swap(v):
    return lax.ppermute(v, "tp", SWAP)


def per_device(tokens, in_x, in_bc, in_dt, conv_x, conv_bc, dt_bias, a_log, skip_d, norm_gain, out_w):
    after = lax.optimization_barrier
    partner = swap(tokens)
    first, second, last = pack(tokens, partner)
    r1, r2 = around(first), around(second)
    spans = lax.axis_size("ctx")

    def onward(*route):
        return lax.ppermute(
            last, ("ctx", "tp"), [(i * 8 + f, i * 8 + 8 + t) for i in range(spans - 1) for f, t in route]
        )

    edge = onward((7, 7), (6, 1)) + onward((7, 5), (6, 3))
    *piece0, wx, wbc, wdt = project_near(tokens, partner, in_x, in_bc, in_dt.T)
    weights = (wx, wbc, wdt)
    r1, wx, edge = after((r1, wx, edge))
    far = around(r1)
    edges = swap(edge)
    far, r2 = after((far, r2))
    piece12 = project_next(r1, r2, swap(r1), swap(r2), *weights)

    xc, b, c, cs, dt, e, d, send = local_part(
        dt_bias, a_log, *piece0, *piece12, far, swap(far), edge, edges, *weights, conv_x, conv_bc
    )
    got = lax.all_to_all(send, "ctx", 0, 0, tiled=True)
    ydiag, w = diag_part(skip_d, out_w, xc, b, c, cs, dt)
    back = lax.all_to_all(prefix(got), "ctx", 0, 0, tiled=True)
    other, own, rest = norm_part(back.reshape(CH, NS), e, d, c, cs, ydiag, norm_gain[None, :], w)

    def both(mine, theirs):
        return mine.astype(F32) + swap(theirs).astype(F32)

    q2 = both(own, other).astype(BF)
    give_raw, give_sum, keep_raw, keep_sum, give, keep = out_part(rest, w)
    q2, give_raw, give_sum, give = after((q2, give_raw, give_sum, give))
    first = around(q2)
    raw = around(both(keep_raw, give_raw).astype(BF))
    summed = around((both(keep_sum, give_sum) + first.astype(F32)).astype(BF))
    return (both(keep, give) + swap(raw).astype(F32) + summed.astype(F32)).astype(BF)


def solution(mesh):
    return jax.shard_map(
        per_device,
        mesh=mesh,
        in_specs=(
            P(("ctx", "tp"), None),
            P(None, "tp"),
            P(),
            P(None, "tp"),
            P(None, "tp"),
            P(),
            P("tp"),
            P("tp"),
            P("tp"),
            P("tp"),
            P("tp", None),
        ),
        out_specs=P(("ctx", "tp"), None),
        check_vma=False,
    )
```

```python
import functools

import jax
import jax.numpy as jnp
from jax import lax
from jax.experimental import pallas as pl
from jax.experimental.pallas import tpu as pltpu
from jax.sharding import PartitionSpec as P

BF = jnp.bfloat16
F32 = jnp.float32
VMEM = pl.BlockSpec(memory_space=pltpu.VMEM)
SMEM = pl.BlockSpec(memory_space=pltpu.SMEM)
LIMIT = 14 * 1024 * 1024

Q = 128
NQ = 4
HH = 8
HD = 64
NS = 128
CH = 512
BCW = 256


def params():
    return pltpu.CompilerParams(vmem_limit_bytes=LIMIT)


def dot_tn(a, b):
    return lax.dot_general(a, b, (((0,), (0,)), ((), ())), preferred_element_type=F32)


def dot_nt(a, b):
    return lax.dot_general(a, b, (((1,), (1,)), ((), ())), preferred_element_type=F32)


def two_parts(v):
    hi = v.astype(BF)
    return hi, (v - hi.astype(F32)).astype(BF)


def head_spread():
    row = lax.broadcasted_iota(jnp.int32, (2 * HH, CH), 0)
    lane = lax.broadcasted_iota(jnp.int32, (2 * HH, CH), 1)
    return jnp.where(lane // HD == row % HH, 1.0, 0.0).astype(BF)


def spread(v, ones):
    hi, lo = two_parts(v)
    both = jnp.concatenate([hi.astype(F32), lo.astype(F32)], 0).astype(BF)
    return dot_tn(both, ones)


def chip():
    return lax.axis_index("tp") // 2


def core():
    return lax.rem(lax.axis_index("tp"), 2)


def in_vmem(v):
    return pltpu.with_memory_space_constraint(v, pltpu.VMEM)


def place(tok, ref, base, half):
    at = base + half * 32
    tok[pl.ds(pl.multiple_of(at, 32), 32), :] = ref[0:32, :]
    tok[pl.ds(pl.multiple_of(at + 64, 32), 32), :] = ref[32:64, :]


def pack_kernel(far, theirs, first, second, last, mine, sem):
    c = core()
    copy = pltpu.make_async_copy(far, mine, sem)
    copy.start()
    for part, ref in ((1 - c, theirs), (c, mine)):
        if ref is mine:
            copy.wait()
        at = pl.ds(pl.multiple_of(part * 32, 32), 32)
        first[at, :] = ref[pl.ds(pl.multiple_of(c * 32, 32), 32), :]
        second[at, :] = ref[pl.ds(pl.multiple_of((1 - c) * 32, 32), 32), :]
    end = jnp.where(c == 1, mine[48:64].astype(F32), theirs[48:64].astype(F32))
    last[...] = end[8:16].astype(BF)


def pack(mine, theirs):
    return pl.pallas_call(
        pack_kernel,
        out_shape=(pltpu.VMEM((64, 4096), BF), pltpu.VMEM((64, 4096), BF), pltpu.VMEM((8, 4096), BF)),
        in_specs=[pl.BlockSpec(memory_space=pltpu.HBM), VMEM],
        out_specs=(VMEM,) * 3,
        scratch_shapes=[pltpu.VMEM((64, 4096), BF), pltpu.SemaphoreType.DMA],
        compiler_params=params(),
        name="pack",
    )(pltpu.with_memory_space_constraint(mine, pltpu.HBM), in_vmem(theirs))


def next_kernel(r1, r2, s1, s2, wx, wbc, wdt, xo, bco, dto, tok):
    c = core()
    place(tok, r1, c * Q, c)
    place(tok, r2, c * Q, 1 - c)
    place(tok, s1, (1 - c) * Q, 1 - c)
    place(tok, s2, (1 - c) * Q, c)
    rows = tok[...]
    xo[...] = jnp.dot(rows, wx[...], preferred_element_type=F32).astype(BF)
    bco[...] = jnp.dot(rows, wbc[...], preferred_element_type=F32).astype(BF)
    dt = dot_nt(rows, wdt[...])
    for j in range(2):
        dto[j] = dt[j * Q : (j + 1) * Q].T


def project_next(*args):
    return pl.pallas_call(
        next_kernel,
        out_shape=(
            pltpu.VMEM((2 * Q, CH), BF),
            pltpu.VMEM((2 * Q, BCW), BF),
            pltpu.VMEM((2, HH, Q), F32),
        ),
        in_specs=[VMEM] * 7,
        out_specs=(VMEM, VMEM, VMEM),
        scratch_shapes=[pltpu.VMEM((2 * Q, 4096), BF)],
        compiler_params=params(),
        name="project_next",
    )(*[in_vmem(v) for v in args])


def near_kernel(mine, theirs, wx_far, wbc_far, wdt_far, xo, bco, dto, wx, wbc, wdt, tok, sems):
    c = core()
    pairs = (
        (mine, tok.at[pl.ds(pl.multiple_of(c * 64, 64), 64), :]),
        (wx_far, wx),
        (wdt_far, wdt),
        (wbc_far, wbc),
    )
    copies = [pltpu.make_async_copy(f, t, sems.at[j]) for j, (f, t) in enumerate(pairs)]
    for copy in copies:
        copy.start()
    tok[pl.ds(pl.multiple_of((1 - c) * 64, 64), 64), :] = theirs[...]
    copies[0].wait()
    copies[1].wait()
    rows = tok[...]
    xo[...] = jnp.dot(rows, wx[...], preferred_element_type=F32).astype(BF)
    copies[2].wait()
    dto[0] = dot_nt(rows, wdt[...]).T
    copies[3].wait()
    bco[...] = jnp.dot(rows, wbc[...], preferred_element_type=F32).astype(BF)


def project_near(mine, theirs, in_x, in_bc, in_dt):
    hbm = pl.BlockSpec(memory_space=pltpu.HBM)
    far = lambda v: pltpu.with_memory_space_constraint(v, pltpu.HBM)
    return pl.pallas_call(
        near_kernel,
        out_shape=(
            pltpu.VMEM((Q, CH), BF),
            pltpu.VMEM((Q, BCW), BF),
            pltpu.VMEM((1, HH, Q), F32),
            pltpu.VMEM(in_x.shape, BF),
            pltpu.VMEM(in_bc.shape, BF),
            pltpu.VMEM(in_dt.shape, BF),
        ),
        in_specs=[hbm, VMEM, hbm, hbm, hbm],
        out_specs=(VMEM,) * 6,
        scratch_shapes=[pltpu.VMEM((Q, 4096), BF), pltpu.SemaphoreType.DMA((4,))],
        compiler_params=params(),
        name="project_near",
    )(far(mine), in_vmem(theirs), far(in_x), far(in_bc), far(in_dt))


def silu(v):
    return v / (1.0 + jnp.exp(-v))


def softplus(v):
    return jnp.maximum(v, 0.0) + jnp.log1p(jnp.exp(-jnp.abs(v)))


def column(ref):
    row = lax.broadcasted_iota(jnp.int32, (HH, Q), 0)
    v = jnp.full((HH, Q), ref[0], F32)
    for h in range(1, HH):
        v = jnp.where(row == h, ref[h], v)
    return v


OFFS = (0, 3, 1, 2)


def local_kernel(bias, alog, *refs):
    x0, bc0, dt0, x12, bc12, dt12 = refs[0:6]
    far, far_swap, halo, haloswap = refs[6:10]
    wx, wbc, wdt, kx, kbc = refs[10:15]
    (xo, bo, co, cso, dto, eo, do, send) = refs[15:23]
    ext, extb, dtr, tok = refs[23:27]
    y = chip()
    place(tok, far, 0, core())
    place(tok, far_swap, 0, 1 - core())
    edge = halo[...].astype(F32) + haloswap[...].astype(F32)
    tok[Q : Q + 16, :] = jnp.concatenate([edge, edge], 0).astype(BF)
    rows = tok[...]
    x3 = jnp.dot(rows, wx[...], preferred_element_type=F32).astype(BF).astype(F32)
    bc3 = jnp.dot(rows, wbc[...], preferred_element_type=F32).astype(BF).astype(F32)
    dt3 = dot_nt(rows[0:Q], wdt[...]).T
    ext[0:8, :] = x3[Q : Q + 8]
    extb[0:8, :] = bc3[Q : Q + 8]
    pieces = (
        (x0[...], bc0[...], dt0[0]),
        (x12[0:Q], bc12[0:Q], dt12[0]),
        (x12[Q : 2 * Q], bc12[Q : 2 * Q], dt12[1]),
        (x3[0:Q], bc3[0:Q], dt3),
    )
    for k, (px, pbc, pdt) in enumerate(pieces):
        a = lax.rem(y + OFFS[k], NQ)
        at = pl.multiple_of(a * Q + 8, 8)
        ext[pl.ds(at, Q), :] = px.astype(F32)
        extb[pl.ds(at, Q), :] = pbc.astype(F32)
        dtr[a] = pdt
    ones = head_spread()
    lane = lax.broadcasted_iota(jnp.int32, (HH, Q), 1)
    decay = -jnp.exp(column(alog))
    bias_col = column(bias)
    total = jnp.zeros((HH, Q), F32)
    state = jnp.zeros((NS, CH), F32)
    for a in range(NQ):
        dt = softplus(dtr[a] + bias_col)
        cs = decay * dt
        for s in (1, 2, 4, 8, 16, 32, 64):
            cs = cs + jnp.where(lane >= s, pltpu.roll(cs, s, 1), 0.0)
        end = jnp.broadcast_to(cs[:, Q - 1 : Q], (HH, Q))
        dto[a] = dt
        cso[a] = cs
        total = total + end
        v = kbc[0:1, :] * extb[a * Q + 5 : a * Q + 5 + Q, :]
        for j in range(1, 4):
            v = v + kbc[j : j + 1, :] * extb[a * Q + 5 + j : a * Q + 5 + j + Q, :]
        bc = silu(v).astype(BF)
        b = bc[:, :NS]
        bo[a] = b
        co[a] = bc[:, NS:]
        v = kx[0:1, :] * ext[a * Q + 5 : a * Q + 5 + Q, :]
        for j in range(1, 4):
            v = v + kx[j : j + 1, :] * ext[a * Q + 5 + j : a * Q + 5 + j + Q, :]
        x = silu(v)
        xo[a] = x.astype(BF)
        w = spread(dt * jnp.exp(end - cs), ones)
        e = dot_tn(b, (x * w).astype(BF))
        eo[a] = e
        d = spread(jnp.exp(end), ones)[0:8, :]
        do[a] = d
        state = state * d[0:1, :] + e
    st = state.T
    dec = jnp.exp(total)
    hi = dec.astype(BF).astype(F32)
    mid = (dec - hi).astype(BF).astype(F32)
    low = dec - hi - mid
    row = lax.broadcasted_iota(jnp.int32, (HH, Q), 0)
    for h in range(HH):
        p = lambda t: jnp.broadcast_to(t[h : h + 1, :], (8, Q))
        tail = jnp.where(row == 0, p(hi), jnp.where(row == 1, p(mid), jnp.where(row == 2, p(low), 0.0)))
        for q in range(4):
            d = h * 4 + q
            send[d] = jnp.concatenate([st[16 * d : 16 * d + 16, :], tail], 0).astype(BF)


def local_part(bias, alog, *args):
    s = pltpu.VMEM
    return pl.pallas_call(
        local_kernel,
        out_shape=(
            s((NQ, Q, CH), BF),
            s((NQ, Q, NS), BF),
            s((NQ, Q, NS), BF),
            s((NQ, HH, Q), F32),
            s((NQ, HH, Q), F32),
            s((NQ, NS, CH), F32),
            s((NQ, 8, CH), F32),
            s((32, 24, 128), BF),
        ),
        in_specs=[SMEM] * 2 + [VMEM] * 15,
        out_specs=(VMEM,) * 8,
        scratch_shapes=[
            pltpu.VMEM((8 + NQ * Q, CH), F32),
            pltpu.VMEM((8 + NQ * Q, BCW), F32),
            pltpu.VMEM((NQ, HH, Q), F32),
            pltpu.VMEM((Q + 16, 4096), BF),
        ],
        compiler_params=params(),
        name="local_part",
    )(bias, alog, *[in_vmem(v) for v in args])


def prefix_kernel(r, o):
    s = jnp.zeros((16, 128), F32)
    for j in range(32):
        o[j] = s.astype(BF)
        v = r[j].astype(F32)
        s = s * (v[16:17] + v[17:18] + v[18:19]) + v[0:16]


def prefix(r):
    return pl.pallas_call(
        prefix_kernel,
        out_shape=pltpu.VMEM((32, 16, 128), BF),
        in_specs=[VMEM],
        out_specs=VMEM,
        compiler_params=params(),
        name="prefix",
    )(in_vmem(r))


def diag_kernel(skip, x, b, c, cs, dt, y):
    t = lax.broadcasted_iota(jnp.int32, (Q, Q), 0)
    u = lax.broadcasted_iota(jnp.int32, (Q, Q), 1)
    tri = t >= u
    left = u < HD
    for a in range(NQ):
        scores = dot_nt(c[a], b[a])
        csr = cs[a]
        csc = csr.T
        dtr = dt[a]
        for p in range(HH // 2):
            xp = x[a, :, 128 * p : 128 * p + 128]
            ms = []
            for h in (2 * p, 2 * p + 1):
                diff = csc[:, h : h + 1] - csr[h : h + 1, :]
                m = scores * jnp.exp(jnp.where(tri, diff, -jnp.inf)) * dtr[h : h + 1, :]
                ms.append(m.astype(BF))
            xf = xp.astype(F32)
            xx = jnp.concatenate([jnp.where(left, xf, 0.0), jnp.where(left, 0.0, xf)], 0).astype(BF)
            yy = jnp.dot(jnp.concatenate(ms, 1), xx, preferred_element_type=F32)
            y[a, :, 128 * p : 128 * p + 128] = yy + jnp.where(left, skip[2 * p], skip[2 * p + 1]) * xf


def diag_part(skip, *args):
    return pl.pallas_call(
        diag_kernel,
        out_shape=pltpu.VMEM((NQ, Q, CH), F32),
        in_specs=[SMEM] + [VMEM] * 5,
        out_specs=VMEM,
        compiler_params=params(),
        name="diag_part",
    )(skip, *[in_vmem(v) for v in args])


def norm_kernel(s_in, e, d, c, cs, ydiag, gain, w_far, other, own, rest, w, nb, sem):
    copy = pltpu.make_async_copy(w_far, w, sem)
    copy.start()
    y = chip()
    mine = core()
    ones = head_spread()
    r = lax.broadcasted_iota(jnp.int32, (Q, Q), 0) // HD
    l = lax.broadcasted_iota(jnp.int32, (Q, Q), 1) // HD
    mean = jnp.where(r == l, 1.0 / HD, 0.0).astype(BF)
    state = s_in[...].astype(F32).T
    for a in range(NQ):
        yst = jnp.dot(c[a], state.astype(BF), preferred_element_type=F32)
        g = spread(jnp.exp(cs[a]), ones)
        v = ydiag[a] + g * yst
        if a < NQ - 1:
            state = state * d[a][0:1, :] + e[a]
        hi, lo = two_parts(v * v)
        for p in range(HH // 2):
            at = slice(128 * p, 128 * p + 128)
            ms = jnp.dot(hi[:, at], mean, preferred_element_type=F32)
            ms = ms + jnp.dot(lo[:, at], mean, preferred_element_type=F32)
            nb[a, :, at] = (v[:, at] * lax.rsqrt(ms + 1e-05) * gain[0:1, at]).astype(BF)

    def half(a, h):
        return nb[a, pl.ds(pl.multiple_of(h * 64, 64), 64), :]

    a = lax.rem(y + 2, NQ)
    v = jnp.concatenate([half(a, 1 - mine), half(a, mine)], 0)
    copy.wait()
    v = jnp.dot(v, w[...], preferred_element_type=F32).astype(BF)
    other[...] = v[0:64]
    own[...] = v[64:128]
    side, across = lax.rem(y + 1 + 2 * mine, NQ), lax.rem(y + 3 - 2 * mine, NQ)
    parts = ((across, mine), (across, 1 - mine), (side, 1 - mine), (side, mine), (y, 1 - mine), (y, mine))
    for j, (a, h) in enumerate(parts):
        rest[64 * j : 64 * j + 64, :] = half(a, h)


def norm_part(*args):
    s = pltpu.VMEM
    return pl.pallas_call(
        norm_kernel,
        out_shape=(s((64, 4096), BF), s((64, 4096), BF), s((384, CH), BF), s((CH, 4096), BF)),
        in_specs=[VMEM] * 7 + [pl.BlockSpec(memory_space=pltpu.HBM)],
        out_specs=(VMEM,) * 4,
        scratch_shapes=[pltpu.VMEM((NQ, Q, CH), BF), pltpu.SemaphoreType.DMA],
        compiler_params=params(),
        name="norm_part",
    )(*[in_vmem(v) for v in args[:7]], pltpu.with_memory_space_constraint(args[7], pltpu.HBM))


def out_kernel(n, w, *outs):
    v = jnp.dot(n[...], w[...], preferred_element_type=F32).astype(BF)
    for j, o in enumerate(outs):
        o[...] = v[64 * j : 64 * j + 64]


def out_part(n, w):
    s = pltpu.VMEM
    return pl.pallas_call(
        out_kernel,
        out_shape=(s((64, 4096), BF),) * 6,
        in_specs=[VMEM] * 2,
        out_specs=(VMEM,) * 6,
        compiler_params=params(),
        name="out_part",
    )(in_vmem(n), in_vmem(w))


SWAP = [(y * 2 + c, y * 2 + 1 - c) for y in range(4) for c in range(2)]


AROUND = [(y * 2 + c, ((y + 1 - 2 * c) % 4) * 2 + c) for y in range(4) for c in range(2)]


def around(v):
    return lax.ppermute(v, "tp", AROUND)


def swap(v):
    return lax.ppermute(v, "tp", SWAP)


def per_device(tokens, in_x, in_bc, in_dt, conv_x, conv_bc, dt_bias, a_log, skip_d, norm_gain, out_w):
    after = lax.optimization_barrier
    partner = swap(tokens)
    first, second, last = pack(tokens, partner)
    r1, r2 = around(first), around(second)
    *piece0, wx, wbc, wdt = project_near(tokens, partner, in_x, in_bc, in_dt.T)
    weights = (wx, wbc, wdt)
    r1, wx, last = after((r1, wx, last))
    far = around(r1)
    spans = lax.axis_size("ctx")

    def onward(*route):
        return lax.ppermute(
            last, ("ctx", "tp"), [(i * 8 + f, i * 8 + 8 + t) for i in range(spans - 1) for f, t in route]
        )

    edge_a, edge_b = onward((7, 7), (6, 1)), onward((7, 5), (6, 3))
    far, r2 = after((far, r2))
    piece12 = project_next(r1, r2, swap(r1), swap(r2), *weights)
    edge_a, edge_b, far = after((edge_a, edge_b, far))
    edge = edge_a + edge_b
    edges = swap(edge)

    xc, b, c, cs, dt, e, d, send = local_part(
        dt_bias, a_log, *piece0, *piece12, far, swap(far), edge, edges, *weights, conv_x, conv_bc
    )
    got = lax.all_to_all(send, "ctx", 0, 0, tiled=True)
    ydiag = diag_part(skip_d, xc, b, c, cs, dt)
    back = lax.all_to_all(prefix(got), "ctx", 0, 0, tiled=True)
    other, own, rest, w = norm_part(back.reshape(CH, NS), e, d, c, cs, ydiag, norm_gain[None, :], out_w)

    def both(mine, theirs):
        return mine.astype(F32) + swap(theirs).astype(F32)

    q2 = both(own, other).astype(BF)
    give_raw, give_sum, keep_raw, keep_sum, give, keep = out_part(rest, w)
    q2, give_raw, give_sum, give = after((q2, give_raw, give_sum, give))
    first = around(q2)
    raw = around(both(keep_raw, give_raw).astype(BF))
    summed = around((both(keep_sum, give_sum) + first.astype(F32)).astype(BF))
    return (both(keep, give) + swap(raw).astype(F32) + summed.astype(F32)).astype(BF)


def solution(mesh):
    return jax.shard_map(
        per_device,
        mesh=mesh,
        in_specs=(
            P(("ctx", "tp"), None),
            P(None, "tp"),
            P(),
            P(None, "tp"),
            P(None, "tp"),
            P(),
            P("tp"),
            P("tp"),
            P("tp"),
            P("tp"),
            P("tp", None),
        ),
        out_specs=P(("ctx", "tp"), None),
        check_vma=False,
    )
```

```python
import functools

import jax
import jax.numpy as jnp
from jax import lax
from jax.experimental import pallas as pl
from jax.experimental.pallas import tpu as pltpu
from jax.sharding import PartitionSpec as P

BF = jnp.bfloat16
F32 = jnp.float32
VMEM = pl.BlockSpec(memory_space=pltpu.VMEM)
SMEM = pl.BlockSpec(memory_space=pltpu.SMEM)
LIMIT = 14 * 1024 * 1024

Q = 128
NQ = 4
HH = 8
HD = 64
NS = 128
CH = 512
BCW = 256


def params():
    return pltpu.CompilerParams(vmem_limit_bytes=LIMIT)


def dot_tn(a, b):
    return lax.dot_general(a, b, (((0,), (0,)), ((), ())), preferred_element_type=F32)


def dot_nt(a, b):
    return lax.dot_general(a, b, (((1,), (1,)), ((), ())), preferred_element_type=F32)


def two_parts(v):
    hi = v.astype(BF)
    return hi, (v - hi.astype(F32)).astype(BF)


def head_spread():
    row = lax.broadcasted_iota(jnp.int32, (2 * HH, CH), 0)
    lane = lax.broadcasted_iota(jnp.int32, (2 * HH, CH), 1)
    return jnp.where(lane // HD == row % HH, 1.0, 0.0).astype(BF)


def spread(v, ones):
    hi, lo = two_parts(v)
    both = jnp.concatenate([hi.astype(F32), lo.astype(F32)], 0).astype(BF)
    return dot_tn(both, ones)


def chip():
    return lax.axis_index("tp") // 2


def core():
    return lax.rem(lax.axis_index("tp"), 2)


def in_vmem(v):
    return pltpu.with_memory_space_constraint(v, pltpu.VMEM)


def place(tok, ref, base, half):
    at = base + half * 32
    tok[pl.ds(pl.multiple_of(at, 32), 32), :] = ref[0:32, :]
    tok[pl.ds(pl.multiple_of(at + 64, 32), 32), :] = ref[32:64, :]


def pack_kernel(far, theirs, first, second, last, mine, sem):
    c = core()
    copy = pltpu.make_async_copy(far, mine, sem)
    copy.start()
    for part, ref in ((1 - c, theirs), (c, mine)):
        if ref is mine:
            copy.wait()
        at = pl.ds(pl.multiple_of(part * 32, 32), 32)
        first[at, :] = ref[pl.ds(pl.multiple_of(c * 32, 32), 32), :]
        second[at, :] = ref[pl.ds(pl.multiple_of((1 - c) * 32, 32), 32), :]
    end = jnp.where(c == 1, mine[48:64].astype(F32), theirs[48:64].astype(F32))
    last[...] = end[8:16].astype(BF)


def pack(mine, theirs):
    return pl.pallas_call(
        pack_kernel,
        out_shape=(pltpu.VMEM((64, 4096), BF), pltpu.VMEM((64, 4096), BF), pltpu.VMEM((8, 4096), BF)),
        in_specs=[pl.BlockSpec(memory_space=pltpu.HBM), VMEM],
        out_specs=(VMEM,) * 3,
        scratch_shapes=[pltpu.VMEM((64, 4096), BF), pltpu.SemaphoreType.DMA],
        compiler_params=params(),
        name="pack",
    )(pltpu.with_memory_space_constraint(mine, pltpu.HBM), in_vmem(theirs))


def half_kernel(mine, theirs, wx, wbc, wdt, xo, bco, dto):
    rows = jnp.concatenate([mine[...], theirs[...]], 0)
    xo[...] = jnp.dot(rows, wx[...], preferred_element_type=F32).astype(BF)
    bco[...] = jnp.dot(rows, wbc[...], preferred_element_type=F32).astype(BF)
    dto[...] = dot_nt(rows, wdt[...])


def project_half(mine, theirs, weights, name):
    return pl.pallas_call(
        half_kernel,
        out_shape=(pltpu.VMEM((Q, CH), BF), pltpu.VMEM((Q, BCW), BF), pltpu.VMEM((Q, HH), F32)),
        in_specs=[VMEM] * 5,
        out_specs=(VMEM, VMEM, VMEM),
        compiler_params=params(),
        name=name,
    )(*[in_vmem(v) for v in (mine, theirs, *weights)])


def near_kernel(mine, theirs, wx_far, wbc_far, wdt_far, xo, bco, dto, wx, wbc, wdt, tok, sems):
    c = core()
    pairs = (
        (mine, tok.at[pl.ds(pl.multiple_of(c * 64, 64), 64), :]),
        (wx_far, wx),
        (wdt_far, wdt),
        (wbc_far, wbc),
    )
    copies = [pltpu.make_async_copy(f, t, sems.at[j]) for j, (f, t) in enumerate(pairs)]
    for copy in copies:
        copy.start()
    tok[pl.ds(pl.multiple_of((1 - c) * 64, 64), 64), :] = theirs[...]
    copies[0].wait()
    copies[1].wait()
    rows = tok[...]
    xo[...] = jnp.dot(rows, wx[...], preferred_element_type=F32).astype(BF)
    copies[2].wait()
    dto[...] = dot_nt(rows, wdt[...])
    copies[3].wait()
    bco[...] = jnp.dot(rows, wbc[...], preferred_element_type=F32).astype(BF)


def project_near(mine, theirs, in_x, in_bc, in_dt):
    hbm = pl.BlockSpec(memory_space=pltpu.HBM)
    far = lambda v: pltpu.with_memory_space_constraint(v, pltpu.HBM)
    return pl.pallas_call(
        near_kernel,
        out_shape=(
            pltpu.VMEM((Q, CH), BF),
            pltpu.VMEM((Q, BCW), BF),
            pltpu.VMEM((Q, HH), F32),
            pltpu.VMEM(in_x.shape, BF),
            pltpu.VMEM(in_bc.shape, BF),
            pltpu.VMEM(in_dt.shape, BF),
        ),
        in_specs=[hbm, VMEM, hbm, hbm, hbm],
        out_specs=(VMEM,) * 6,
        scratch_shapes=[pltpu.VMEM((Q, 4096), BF), pltpu.SemaphoreType.DMA((4,))],
        compiler_params=params(),
        name="project_near",
    )(far(mine), in_vmem(theirs), far(in_x), far(in_bc), far(in_dt))


def silu(v):
    return v / (1.0 + jnp.exp(-v))


def softplus(v):
    return jnp.maximum(v, 0.0) + jnp.log1p(jnp.exp(-jnp.abs(v)))


def column(ref):
    row = lax.broadcasted_iota(jnp.int32, (HH, Q), 0)
    v = jnp.full((HH, Q), ref[0], F32)
    for h in range(1, HH):
        v = jnp.where(row == h, ref[h], v)
    return v


def local_kernel(bias, alog, *refs):
    near, one, two = refs[0:3], refs[3:6], refs[6:9]
    far, far_swap, halo, haloswap = refs[9:13]
    wx, wbc, wdt, kx, kbc = refs[13:18]
    (xo, bo, co, cso, dto, eo, do, send) = refs[18:26]
    ext, extb, dtr, tok = refs[26:30]
    y = chip()
    c = core()
    place(tok, far, 0, c)
    place(tok, far_swap, 0, 1 - c)
    edge = halo[...].astype(F32) + haloswap[...].astype(F32)
    tok[Q : Q + 16, :] = jnp.concatenate([edge, edge], 0).astype(BF)
    rows = tok[...]
    x3 = jnp.dot(rows, wx[...], preferred_element_type=F32).astype(BF).astype(F32)
    bc3 = jnp.dot(rows, wbc[...], preferred_element_type=F32).astype(BF).astype(F32)
    dt3 = dot_nt(rows[0:Q], wdt[...])
    ext[0:8, :] = x3[Q : Q + 8]
    extb[0:8, :] = bc3[Q : Q + 8]

    def put(at, n, px, pbc, pdt):
        ext[pl.ds(pl.multiple_of(at + 8, 8), n), :] = px.astype(F32)
        extb[pl.ds(pl.multiple_of(at + 8, 8), n), :] = pbc.astype(F32)
        dtr[pl.ds(pl.multiple_of(at, 8), n), :] = pdt

    put(y * Q, Q, near[0][...], near[1][...], near[2][...])
    put(lax.rem(y + 2, NQ) * Q, Q, x3[0:Q], bc3[0:Q], dt3)
    sides = (lax.rem(y + 3 - 2 * c, NQ), lax.rem(y + 1 + 2 * c, NQ))
    for piece, halves in ((one, (c, 1 - c)), (two, (1 - c, c))):
        for j in range(4):
            at = sides[j // 2] * Q + halves[j // 2] * 32 + (j % 2) * 64
            of = slice(32 * j, 32 * j + 32)
            put(at, 32, piece[0][of, :], piece[1][of, :], piece[2][of, :])
    ones = head_spread()
    lane = lax.broadcasted_iota(jnp.int32, (HH, Q), 1)
    decay = -jnp.exp(column(alog))
    bias_col = column(bias)
    total = jnp.zeros((HH, Q), F32)
    state = jnp.zeros((NS, CH), F32)
    for a in range(NQ):
        dt = softplus(dtr[a * Q : (a + 1) * Q, :].T + bias_col)
        cs = decay * dt
        for s in (1, 2, 4, 8, 16, 32, 64):
            cs = cs + jnp.where(lane >= s, pltpu.roll(cs, s, 1), 0.0)
        end = jnp.broadcast_to(cs[:, Q - 1 : Q], (HH, Q))
        dto[a] = dt
        cso[a] = cs
        total = total + end
        v = kbc[0:1, :] * extb[a * Q + 5 : a * Q + 5 + Q, :]
        for j in range(1, 4):
            v = v + kbc[j : j + 1, :] * extb[a * Q + 5 + j : a * Q + 5 + j + Q, :]
        bc = silu(v).astype(BF)
        b = bc[:, :NS]
        bo[a] = b
        co[a] = bc[:, NS:]
        v = kx[0:1, :] * ext[a * Q + 5 : a * Q + 5 + Q, :]
        for j in range(1, 4):
            v = v + kx[j : j + 1, :] * ext[a * Q + 5 + j : a * Q + 5 + j + Q, :]
        x = silu(v)
        xo[a] = x.astype(BF)
        w = spread(dt * jnp.exp(end - cs), ones)
        e = dot_tn(b, (x * w).astype(BF))
        eo[a] = e
        d = spread(jnp.exp(end), ones)[0:8, :]
        do[a] = d
        state = state * d[0:1, :] + e
    st = state.T
    dec = jnp.exp(total)
    hi = dec.astype(BF).astype(F32)
    mid = (dec - hi).astype(BF).astype(F32)
    low = dec - hi - mid
    row = lax.broadcasted_iota(jnp.int32, (HH, Q), 0)
    for h in range(HH):
        p = lambda t: jnp.broadcast_to(t[h : h + 1, :], (8, Q))
        tail = jnp.where(row == 0, p(hi), jnp.where(row == 1, p(mid), jnp.where(row == 2, p(low), 0.0)))
        for q in range(4):
            d = h * 4 + q
            send[d] = jnp.concatenate([st[16 * d : 16 * d + 16, :], tail], 0).astype(BF)


def local_part(bias, alog, *args):
    s = pltpu.VMEM
    return pl.pallas_call(
        local_kernel,
        out_shape=(
            s((NQ, Q, CH), BF),
            s((NQ, Q, NS), BF),
            s((NQ, Q, NS), BF),
            s((NQ, HH, Q), F32),
            s((NQ, HH, Q), F32),
            s((NQ, NS, CH), F32),
            s((NQ, 8, CH), F32),
            s((32, 24, 128), BF),
        ),
        in_specs=[SMEM] * 2 + [VMEM] * 18,
        out_specs=(VMEM,) * 8,
        scratch_shapes=[
            pltpu.VMEM((8 + NQ * Q, CH), F32),
            pltpu.VMEM((8 + NQ * Q, BCW), F32),
            pltpu.VMEM((NQ * Q, HH), F32),
            pltpu.VMEM((Q + 16, 4096), BF),
        ],
        compiler_params=params(),
        name="local_part",
    )(bias, alog, *[in_vmem(v) for v in args])


def prefix_kernel(r, o):
    s = jnp.zeros((16, 128), F32)
    for j in range(32):
        o[j] = s.astype(BF)
        v = r[j].astype(F32)
        s = s * (v[16:17] + v[17:18] + v[18:19]) + v[0:16]


def prefix(r):
    return pl.pallas_call(
        prefix_kernel,
        out_shape=pltpu.VMEM((32, 16, 128), BF),
        in_specs=[VMEM],
        out_specs=VMEM,
        compiler_params=params(),
        name="prefix",
    )(in_vmem(r))


def diag_kernel(skip, x, b, c, cs, dt, y):
    t = lax.broadcasted_iota(jnp.int32, (Q, Q), 0)
    u = lax.broadcasted_iota(jnp.int32, (Q, Q), 1)
    tri = t >= u
    left = u < HD
    for a in range(NQ):
        scores = dot_nt(c[a], b[a])
        csr = cs[a]
        csc = csr.T
        dtr = dt[a]
        for p in range(HH // 2):
            xp = x[a, :, 128 * p : 128 * p + 128]
            ms = []
            for h in (2 * p, 2 * p + 1):
                diff = csc[:, h : h + 1] - csr[h : h + 1, :]
                m = scores * jnp.exp(jnp.where(tri, diff, -jnp.inf)) * dtr[h : h + 1, :]
                ms.append(m.astype(BF))
            xf = xp.astype(F32)
            xx = jnp.concatenate([jnp.where(left, xf, 0.0), jnp.where(left, 0.0, xf)], 0).astype(BF)
            yy = jnp.dot(jnp.concatenate(ms, 1), xx, preferred_element_type=F32)
            y[a, :, 128 * p : 128 * p + 128] = yy + jnp.where(left, skip[2 * p], skip[2 * p + 1]) * xf


def diag_part(skip, *args):
    return pl.pallas_call(
        diag_kernel,
        out_shape=pltpu.VMEM((NQ, Q, CH), F32),
        in_specs=[SMEM] + [VMEM] * 5,
        out_specs=VMEM,
        compiler_params=params(),
        name="diag_part",
    )(skip, *[in_vmem(v) for v in args])


def norm_kernel(s_in, e, d, c, cs, ydiag, gain, w_far, other, own, rest, w, nb, sem):
    blocks = [pl.ds(1024 * j, 1024) for j in range(4)]
    copies = [pltpu.make_async_copy(w_far.at[:, k], w.at[:, k], sem.at[j]) for j, k in enumerate(blocks)]
    for copy in copies:
        copy.start()
    y = chip()
    mine = core()
    ones = head_spread()
    r = lax.broadcasted_iota(jnp.int32, (Q, Q), 0) // HD
    l = lax.broadcasted_iota(jnp.int32, (Q, Q), 1) // HD
    mean = jnp.where(r == l, 1.0 / HD, 0.0).astype(BF)
    state = s_in[...].astype(F32).T
    for a in range(NQ):
        yst = jnp.dot(c[a], state.astype(BF), preferred_element_type=F32)
        g = spread(jnp.exp(cs[a]), ones)
        v = ydiag[a] + g * yst
        if a < NQ - 1:
            state = state * d[a][0:1, :] + e[a]
        hi, lo = two_parts(v * v)
        for p in range(HH // 2):
            at = slice(128 * p, 128 * p + 128)
            ms = jnp.dot(hi[:, at], mean, preferred_element_type=F32)
            ms = ms + jnp.dot(lo[:, at], mean, preferred_element_type=F32)
            nb[a, :, at] = (v[:, at] * lax.rsqrt(ms + 1e-05) * gain[0:1, at]).astype(BF)

    def half(a, h):
        return nb[a, pl.ds(pl.multiple_of(h * 64, 64), 64), :]

    a = lax.rem(y + 2, NQ)
    v = jnp.concatenate([half(a, 1 - mine), half(a, mine)], 0)
    for k, copy in zip(blocks, copies):
        copy.wait()
        o = jnp.dot(v, w[:, k], preferred_element_type=F32).astype(BF)
        other[:, k] = o[0:64]
        own[:, k] = o[64:128]
    side, across = lax.rem(y + 1 + 2 * mine, NQ), lax.rem(y + 3 - 2 * mine, NQ)
    parts = ((across, mine), (across, 1 - mine), (side, 1 - mine), (side, mine), (y, 1 - mine), (y, mine))
    for j, (a, h) in enumerate(parts):
        rest[64 * j : 64 * j + 64, :] = half(a, h)


def norm_part(*args):
    s = pltpu.VMEM
    return pl.pallas_call(
        norm_kernel,
        out_shape=(s((64, 4096), BF), s((64, 4096), BF), s((384, CH), BF), s((CH, 4096), BF)),
        in_specs=[VMEM] * 7 + [pl.BlockSpec(memory_space=pltpu.HBM)],
        out_specs=(VMEM,) * 4,
        scratch_shapes=[pltpu.VMEM((NQ, Q, CH), BF), pltpu.SemaphoreType.DMA((4,))],
        compiler_params=params(),
        name="norm_part",
    )(*[in_vmem(v) for v in args[:7]], pltpu.with_memory_space_constraint(args[7], pltpu.HBM))


def out_kernel(n, w, *outs):
    v = jnp.dot(n[...], w[...], preferred_element_type=F32).astype(BF)
    for j, o in enumerate(outs):
        o[...] = v[64 * j : 64 * j + 64]


def out_part(n, w):
    s = pltpu.VMEM
    return pl.pallas_call(
        out_kernel,
        out_shape=(s((64, 4096), BF),) * 6,
        in_specs=[VMEM] * 2,
        out_specs=(VMEM,) * 6,
        compiler_params=params(),
        name="out_part",
    )(in_vmem(n), in_vmem(w))


SWAP = [(y * 2 + c, y * 2 + 1 - c) for y in range(4) for c in range(2)]


AROUND = [(y * 2 + c, ((y + 1 - 2 * c) % 4) * 2 + c) for y in range(4) for c in range(2)]


def around(v):
    return lax.ppermute(v, "tp", AROUND)


def swap(v):
    return lax.ppermute(v, "tp", SWAP)


def per_device(tokens, in_x, in_bc, in_dt, conv_x, conv_bc, dt_bias, a_log, skip_d, norm_gain, out_w):
    after = lax.optimization_barrier
    partner = swap(tokens)
    first, second, last = pack(tokens, partner)
    r1, r2 = around(first), around(second)
    *piece0, wx, wbc, wdt = project_near(tokens, partner, in_x, in_bc, in_dt.T)
    weights = (wx, wbc, wdt)
    r1, wx, last = after((r1, wx, last))
    far = around(r1)
    spans = lax.axis_size("ctx")

    def onward(*route):
        return lax.ppermute(
            last, ("ctx", "tp"), [(i * 8 + f, i * 8 + 8 + t) for i in range(spans - 1) for f, t in route]
        )

    edge_a, edge_b = onward((7, 7), (6, 1)), onward((7, 5), (6, 3))
    s1 = swap(r1)
    r2, edge_a, edge_b = after((r2, edge_a, edge_b))
    s2 = swap(r2)
    piece1 = project_half(r1, s1, weights, "project_one")
    far, s2, *piece1 = after((far, s2, *piece1))
    piece2 = project_half(r2, s2, weights, "project_two")
    edge = edge_a + edge_b
    edges = swap(edge)

    xc, b, c, cs, dt, e, d, send = local_part(
        dt_bias, a_log, *piece0, *piece1, *piece2, far, swap(far), edge, edges, *weights, conv_x, conv_bc
    )
    got = lax.all_to_all(send, "ctx", 0, 0, tiled=True)
    ydiag = diag_part(skip_d, xc, b, c, cs, dt)
    back = lax.all_to_all(prefix(got), "ctx", 0, 0, tiled=True)
    other, own, rest, w = norm_part(back.reshape(CH, NS), e, d, c, cs, ydiag, norm_gain[None, :], out_w)

    def both(mine, theirs):
        return mine.astype(F32) + swap(theirs).astype(F32)

    q2 = both(own, other).astype(BF)
    give_raw, give_sum, keep_raw, keep_sum, give, keep = out_part(rest, w)
    q2, give_raw, give_sum, give = after((q2, give_raw, give_sum, give))
    first = around(q2)
    raw = around(both(keep_raw, give_raw).astype(BF))
    summed = around((both(keep_sum, give_sum) + first.astype(F32)).astype(BF))
    return (both(keep, give) + swap(raw).astype(F32) + summed.astype(F32)).astype(BF)


def solution(mesh):
    return jax.shard_map(
        per_device,
        mesh=mesh,
        in_specs=(
            P(("ctx", "tp"), None),
            P(None, "tp"),
            P(),
            P(None, "tp"),
            P(None, "tp"),
            P(),
            P("tp"),
            P("tp"),
            P("tp"),
            P("tp"),
            P("tp", None),
        ),
        out_specs=P(("ctx", "tp"), None),
        check_vma=False,
    )
```

```python
import functools

import jax
import jax.numpy as jnp
from jax import lax
from jax.experimental import pallas as pl
from jax.experimental.pallas import tpu as pltpu
from jax.sharding import PartitionSpec as P

BF = jnp.bfloat16
F32 = jnp.float32
VMEM = pl.BlockSpec(memory_space=pltpu.VMEM)
SMEM = pl.BlockSpec(memory_space=pltpu.SMEM)
LIMIT = 14 * 1024 * 1024

Q = 128
NQ = 4
HH = 8
HD = 64
NS = 128
CH = 512
BCW = 256


def params():
    return pltpu.CompilerParams(vmem_limit_bytes=LIMIT)


def dot_tn(a, b):
    return lax.dot_general(a, b, (((0,), (0,)), ((), ())), preferred_element_type=F32)


def dot_nt(a, b):
    return lax.dot_general(a, b, (((1,), (1,)), ((), ())), preferred_element_type=F32)


def two_parts(v):
    hi = v.astype(BF)
    return hi, (v - hi.astype(F32)).astype(BF)


def head_spread():
    row = lax.broadcasted_iota(jnp.int32, (2 * HH, CH), 0)
    lane = lax.broadcasted_iota(jnp.int32, (2 * HH, CH), 1)
    return jnp.where(lane // HD == row % HH, 1.0, 0.0).astype(BF)


def spread(v, ones):
    hi, lo = two_parts(v)
    both = jnp.concatenate([hi.astype(F32), lo.astype(F32)], 0).astype(BF)
    return dot_tn(both, ones)


def chip():
    return lax.axis_index("tp") // 2


def core():
    return lax.rem(lax.axis_index("tp"), 2)


def in_vmem(v):
    return pltpu.with_memory_space_constraint(v, pltpu.VMEM)


def place(tok, ref, base, half):
    at = base + half * 32
    tok[pl.ds(pl.multiple_of(at, 32), 32), :] = ref[0:32, :]
    tok[pl.ds(pl.multiple_of(at + 64, 32), 32), :] = ref[32:64, :]


def pack_kernel(far, theirs, first, second, last, mine, sem):
    c = core()
    copy = pltpu.make_async_copy(far, mine, sem)
    copy.start()
    for part, ref in ((1 - c, theirs), (c, mine)):
        if ref is mine:
            copy.wait()
        at = pl.ds(pl.multiple_of(part * 32, 32), 32)
        first[at, :] = ref[pl.ds(pl.multiple_of(c * 32, 32), 32), :]
        second[at, :] = ref[pl.ds(pl.multiple_of((1 - c) * 32, 32), 32), :]
    end = jnp.where(c == 1, mine[48:64].astype(F32), theirs[48:64].astype(F32))
    last[...] = end[8:16].astype(BF)


def pack(mine, theirs):
    return pl.pallas_call(
        pack_kernel,
        out_shape=(pltpu.VMEM((64, 4096), BF), pltpu.VMEM((64, 4096), BF), pltpu.VMEM((8, 4096), BF)),
        in_specs=[pl.BlockSpec(memory_space=pltpu.HBM), VMEM],
        out_specs=(VMEM,) * 3,
        scratch_shapes=[pltpu.VMEM((64, 4096), BF), pltpu.SemaphoreType.DMA],
        compiler_params=params(),
        name="pack",
    )(pltpu.with_memory_space_constraint(mine, pltpu.HBM), in_vmem(theirs))


def half_kernel(mine, theirs, wx, wbc, wdt, xo, bco, dto):
    rows = jnp.concatenate([mine[...], theirs[...]], 0)
    xo[...] = jnp.dot(rows, wx[...], preferred_element_type=F32).astype(BF)
    bco[...] = jnp.dot(rows, wbc[...], preferred_element_type=F32).astype(BF)
    dto[...] = dot_nt(rows, wdt[...])


def project_half(mine, theirs, weights, name):
    return pl.pallas_call(
        half_kernel,
        out_shape=(pltpu.VMEM((Q, CH), BF), pltpu.VMEM((Q, BCW), BF), pltpu.VMEM((Q, HH), F32)),
        in_specs=[VMEM] * 5,
        out_specs=(VMEM, VMEM, VMEM),
        compiler_params=params(),
        name=name,
    )(*[in_vmem(v) for v in (mine, theirs, *weights)])


def near_kernel(mine, theirs, wx_far, wbc_far, wdt_far, xo, bco, dto, wx, wbc, wdt, tok, sems):
    c = core()
    pairs = (
        (mine, tok.at[pl.ds(pl.multiple_of(c * 64, 64), 64), :]),
        (wx_far, wx),
        (wdt_far, wdt),
        (wbc_far, wbc),
    )
    copies = [pltpu.make_async_copy(f, t, sems.at[j]) for j, (f, t) in enumerate(pairs)]
    for copy in copies:
        copy.start()
    tok[pl.ds(pl.multiple_of((1 - c) * 64, 64), 64), :] = theirs[...]
    copies[0].wait()
    copies[1].wait()
    rows = tok[...]
    xo[...] = jnp.dot(rows, wx[...], preferred_element_type=F32).astype(BF)
    copies[2].wait()
    dto[...] = dot_nt(rows, wdt[...])
    copies[3].wait()
    bco[...] = jnp.dot(rows, wbc[...], preferred_element_type=F32).astype(BF)


def project_near(mine, theirs, in_x, in_bc, in_dt):
    hbm = pl.BlockSpec(memory_space=pltpu.HBM)
    far = lambda v: pltpu.with_memory_space_constraint(v, pltpu.HBM)
    return pl.pallas_call(
        near_kernel,
        out_shape=(
            pltpu.VMEM((Q, CH), BF),
            pltpu.VMEM((Q, BCW), BF),
            pltpu.VMEM((Q, HH), F32),
            pltpu.VMEM(in_x.shape, BF),
            pltpu.VMEM(in_bc.shape, BF),
            pltpu.VMEM(in_dt.shape, BF),
        ),
        in_specs=[hbm, VMEM, hbm, hbm, hbm],
        out_specs=(VMEM,) * 6,
        scratch_shapes=[pltpu.VMEM((Q, 4096), BF), pltpu.SemaphoreType.DMA((4,))],
        compiler_params=params(),
        name="project_near",
    )(far(mine), in_vmem(theirs), far(in_x), far(in_bc), far(in_dt))


def silu(v):
    return v / (1.0 + jnp.exp(-v))


def softplus(v):
    return jnp.maximum(v, 0.0) + jnp.log1p(jnp.exp(-jnp.abs(v)))


def column(ref):
    row = lax.broadcasted_iota(jnp.int32, (HH, Q), 0)
    v = jnp.full((HH, Q), ref[0], F32)
    for h in range(1, HH):
        v = jnp.where(row == h, ref[h], v)
    return v


def local_kernel(bias, alog, *refs):
    near, one, two = refs[0:3], refs[3:6], refs[6:9]
    far, far_swap, halo, haloswap = refs[9:13]
    wx, wbc, wdt, kx, kbc = refs[13:18]
    (xo, bo, co, cso, dto, eo, do, send) = refs[18:26]
    ext, extb, dtr, tok = refs[26:30]
    y = chip()
    c = core()
    place(tok, far, 0, c)
    place(tok, far_swap, 0, 1 - c)
    edge = halo[...].astype(F32) + haloswap[...].astype(F32)
    tok[Q : Q + 16, :] = jnp.concatenate([edge, edge], 0).astype(BF)
    rows = tok[...]
    x3 = jnp.dot(rows, wx[...], preferred_element_type=F32).astype(BF).astype(F32)
    bc3 = jnp.dot(rows, wbc[...], preferred_element_type=F32).astype(BF).astype(F32)
    dt3 = dot_nt(rows[0:Q], wdt[...])
    ext[0:8, :] = x3[Q : Q + 8]
    extb[0:8, :] = bc3[Q : Q + 8]

    def put(at, n, px, pbc, pdt):
        ext[pl.ds(pl.multiple_of(at + 8, 8), n), :] = px.astype(F32)
        extb[pl.ds(pl.multiple_of(at + 8, 8), n), :] = pbc.astype(F32)
        dtr[pl.ds(pl.multiple_of(at, 8), n), :] = pdt

    put(y * Q, Q, near[0][...], near[1][...], near[2][...])
    put(lax.rem(y + 2, NQ) * Q, Q, x3[0:Q], bc3[0:Q], dt3)
    sides = (lax.rem(y + 3 - 2 * c, NQ), lax.rem(y + 1 + 2 * c, NQ))
    for piece, halves in ((one, (c, 1 - c)), (two, (1 - c, c))):
        for j in range(4):
            at = sides[j // 2] * Q + halves[j // 2] * 32 + (j % 2) * 64
            of = slice(32 * j, 32 * j + 32)
            put(at, 32, piece[0][of, :], piece[1][of, :], piece[2][of, :])
    ones = head_spread()
    lane = lax.broadcasted_iota(jnp.int32, (HH, Q), 1)
    decay = -jnp.exp(column(alog))
    bias_col = column(bias)
    total = jnp.zeros((HH, Q), F32)
    state = jnp.zeros((NS, CH), F32)
    for a in range(NQ):
        dt = softplus(dtr[a * Q : (a + 1) * Q, :].T + bias_col)
        cs = decay * dt
        for s in (1, 2, 4, 8, 16, 32, 64):
            cs = cs + jnp.where(lane >= s, pltpu.roll(cs, s, 1), 0.0)
        end = jnp.broadcast_to(cs[:, Q - 1 : Q], (HH, Q))
        dto[a] = dt
        cso[a] = cs
        total = total + end
        v = kbc[0:1, :] * extb[a * Q + 5 : a * Q + 5 + Q, :]
        for j in range(1, 4):
            v = v + kbc[j : j + 1, :] * extb[a * Q + 5 + j : a * Q + 5 + j + Q, :]
        bc = silu(v).astype(BF)
        b = bc[:, :NS]
        bo[a] = b
        co[a] = bc[:, NS:]
        v = kx[0:1, :] * ext[a * Q + 5 : a * Q + 5 + Q, :]
        for j in range(1, 4):
            v = v + kx[j : j + 1, :] * ext[a * Q + 5 + j : a * Q + 5 + j + Q, :]
        x = silu(v)
        xo[a] = x.astype(BF)
        w = spread(dt * jnp.exp(end - cs), ones)
        e = dot_tn(b, (x * w).astype(BF))
        eo[a] = e
        d = spread(jnp.exp(end), ones)[0:8, :]
        do[a] = d
        state = state * d[0:1, :] + e
    st = state.T
    dec = jnp.exp(total)
    hi = dec.astype(BF).astype(F32)
    mid = (dec - hi).astype(BF).astype(F32)
    low = dec - hi - mid
    row = lax.broadcasted_iota(jnp.int32, (HH, Q), 0)
    for h in range(HH):
        p = lambda t: jnp.broadcast_to(t[h : h + 1, :], (8, Q))
        tail = jnp.where(row == 0, p(hi), jnp.where(row == 1, p(mid), jnp.where(row == 2, p(low), 0.0)))
        for q in range(4):
            d = h * 4 + q
            send[d] = jnp.concatenate([st[16 * d : 16 * d + 16, :], tail], 0).astype(BF)


def local_part(bias, alog, *args):
    s = pltpu.VMEM
    return pl.pallas_call(
        local_kernel,
        out_shape=(
            s((NQ, Q, CH), BF),
            s((NQ, Q, NS), BF),
            s((NQ, Q, NS), BF),
            s((NQ, HH, Q), F32),
            s((NQ, HH, Q), F32),
            s((NQ, NS, CH), F32),
            s((NQ, 8, CH), F32),
            s((32, 24, 128), BF),
        ),
        in_specs=[SMEM] * 2 + [VMEM] * 18,
        out_specs=(VMEM,) * 8,
        scratch_shapes=[
            pltpu.VMEM((8 + NQ * Q, CH), F32),
            pltpu.VMEM((8 + NQ * Q, BCW), F32),
            pltpu.VMEM((NQ * Q, HH), F32),
            pltpu.VMEM((Q + 16, 4096), BF),
        ],
        compiler_params=params(),
        name="local_part",
    )(bias, alog, *[in_vmem(v) for v in args])


def prefix_kernel(r, o):
    s = jnp.zeros((16, 128), F32)
    for j in range(32):
        o[j] = s.astype(BF)
        v = r[j].astype(F32)
        s = s * (v[16:17] + v[17:18] + v[18:19]) + v[0:16]


def prefix(r):
    return pl.pallas_call(
        prefix_kernel,
        out_shape=pltpu.VMEM((32, 16, 128), BF),
        in_specs=[VMEM],
        out_specs=VMEM,
        compiler_params=params(),
        name="prefix",
    )(in_vmem(r))


def diag_kernel(skip, x, b, c, cs, dt, y):
    t = lax.broadcasted_iota(jnp.int32, (Q, Q), 0)
    u = lax.broadcasted_iota(jnp.int32, (Q, Q), 1)
    tri = t >= u
    left = u < HD
    for a in range(NQ):
        scores = dot_nt(c[a], b[a])
        csr = cs[a]
        csc = csr.T
        dtr = dt[a]
        for p in range(HH // 2):
            xp = x[a, :, 128 * p : 128 * p + 128]
            ms = []
            for h in (2 * p, 2 * p + 1):
                diff = csc[:, h : h + 1] - csr[h : h + 1, :]
                m = scores * jnp.exp(jnp.where(tri, diff, -jnp.inf)) * dtr[h : h + 1, :]
                ms.append(m.astype(BF))
            xf = xp.astype(F32)
            xx = jnp.concatenate([jnp.where(left, xf, 0.0), jnp.where(left, 0.0, xf)], 0).astype(BF)
            yy = jnp.dot(jnp.concatenate(ms, 1), xx, preferred_element_type=F32)
            y[a, :, 128 * p : 128 * p + 128] = yy + jnp.where(left, skip[2 * p], skip[2 * p + 1]) * xf


def diag_part(skip, *args):
    return pl.pallas_call(
        diag_kernel,
        out_shape=pltpu.VMEM((NQ, Q, CH), F32),
        in_specs=[SMEM] + [VMEM] * 5,
        out_specs=VMEM,
        compiler_params=params(),
        name="diag_part",
    )(skip, *[in_vmem(v) for v in args])


def norm_kernel(s_in, e, d, c, cs, ydiag, gain, w_far, other, own, rest, w, nb, sem):
    copy = pltpu.make_async_copy(w_far, w, sem)
    copy.start()
    y = chip()
    mine = core()
    ones = head_spread()
    r = lax.broadcasted_iota(jnp.int32, (Q, Q), 0) // HD
    l = lax.broadcasted_iota(jnp.int32, (Q, Q), 1) // HD
    mean = jnp.where(r == l, 1.0 / HD, 0.0).astype(BF)
    state = s_in[...].astype(F32).T
    for a in range(NQ):
        yst = jnp.dot(c[a], state.astype(BF), preferred_element_type=F32)
        g = spread(jnp.exp(cs[a]), ones)
        v = ydiag[a] + g * yst
        if a < NQ - 1:
            state = state * d[a][0:1, :] + e[a]
        hi, lo = two_parts(v * v)
        for p in range(HH // 2):
            at = slice(128 * p, 128 * p + 128)
            ms = jnp.dot(hi[:, at], mean, preferred_element_type=F32)
            ms = ms + jnp.dot(lo[:, at], mean, preferred_element_type=F32)
            nb[a, :, at] = (v[:, at] * lax.rsqrt(ms + 1e-05) * gain[0:1, at]).astype(BF)

    def half(a, h):
        return nb[a, pl.ds(pl.multiple_of(h * 64, 64), 64), :]

    a = lax.rem(y + 2, NQ)
    v = jnp.concatenate([half(a, 1 - mine), half(a, mine)], 0)
    copy.wait()
    v = jnp.dot(v, w[...], preferred_element_type=F32).astype(BF)
    other[...] = v[0:64]
    own[...] = v[64:128]
    side, across = lax.rem(y + 1 + 2 * mine, NQ), lax.rem(y + 3 - 2 * mine, NQ)
    parts = ((across, mine), (across, 1 - mine), (side, 1 - mine), (side, mine), (y, 1 - mine), (y, mine))
    for j, (a, h) in enumerate(parts):
        rest[64 * j : 64 * j + 64, :] = half(a, h)


def norm_part(*args):
    s = pltpu.VMEM
    return pl.pallas_call(
        norm_kernel,
        out_shape=(s((64, 4096), BF), s((64, 4096), BF), s((384, CH), BF), s((CH, 4096), BF)),
        in_specs=[VMEM] * 7 + [pl.BlockSpec(memory_space=pltpu.HBM)],
        out_specs=(VMEM,) * 4,
        scratch_shapes=[pltpu.VMEM((NQ, Q, CH), BF), pltpu.SemaphoreType.DMA],
        compiler_params=params(),
        name="norm_part",
    )(*[in_vmem(v) for v in args[:7]], pltpu.with_memory_space_constraint(args[7], pltpu.HBM))


def out_kernel(n, w, *outs):
    v = jnp.dot(n[...], w[...], preferred_element_type=F32).astype(BF)
    for j, o in enumerate(outs):
        o[...] = v[64 * j : 64 * j + 64]


def out_part(n, w):
    s = pltpu.VMEM
    return pl.pallas_call(
        out_kernel,
        out_shape=(s((64, 4096), BF),) * 6,
        in_specs=[VMEM] * 2,
        out_specs=(VMEM,) * 6,
        compiler_params=params(),
        name="out_part",
    )(in_vmem(n), in_vmem(w))


SWAP = [(y * 2 + c, y * 2 + 1 - c) for y in range(4) for c in range(2)]


AROUND = [(y * 2 + c, ((y + 1 - 2 * c) % 4) * 2 + c) for y in range(4) for c in range(2)]


def around(v):
    return lax.ppermute(v, "tp", AROUND)


def swap(v):
    return lax.ppermute(v, "tp", SWAP)


def per_device(tokens, in_x, in_bc, in_dt, conv_x, conv_bc, dt_bias, a_log, skip_d, norm_gain, out_w):
    after = lax.optimization_barrier
    partner = swap(tokens)
    first, second, last = pack(tokens, partner)
    r1, r2 = around(first), around(second)
    *piece0, wx, wbc, wdt = project_near(tokens, partner, in_x, in_bc, in_dt.T)
    weights = (wx, wbc, wdt)
    r1, wx, last = after((r1, wx, last))
    far = around(r1)
    spans = lax.axis_size("ctx")

    def onward(*route):
        return lax.ppermute(
            last, ("ctx", "tp"), [(i * 8 + f, i * 8 + 8 + t) for i in range(spans - 1) for f, t in route]
        )

    edge_a, edge_b = onward((7, 7), (6, 1)), onward((7, 5), (6, 3))
    s1, r2 = after((swap(r1), r2))
    piece1 = project_half(r1, s1, weights, "project_one")
    far, r2, *piece1 = after((far, r2, *piece1))
    piece2 = project_half(r2, swap(r2), weights, "project_two")
    edge_a, edge_b, far = after((edge_a, edge_b, far))
    edge = edge_a + edge_b
    edges = swap(edge)

    xc, b, c, cs, dt, e, d, send = local_part(
        dt_bias, a_log, *piece0, *piece1, *piece2, far, swap(far), edge, edges, *weights, conv_x, conv_bc
    )
    got = lax.all_to_all(send, "ctx", 0, 0, tiled=True)
    ydiag = diag_part(skip_d, xc, b, c, cs, dt)
    back = lax.all_to_all(prefix(got), "ctx", 0, 0, tiled=True)
    other, own, rest, w = norm_part(back.reshape(CH, NS), e, d, c, cs, ydiag, norm_gain[None, :], out_w)

    def both(mine, theirs):
        return mine.astype(F32) + swap(theirs).astype(F32)

    q2 = both(own, other).astype(BF)
    give_raw, give_sum, keep_raw, keep_sum, give, keep = out_part(rest, w)
    q2, give_raw, give_sum, give = after((q2, give_raw, give_sum, give))
    first = around(q2)
    raw = around(both(keep_raw, give_raw).astype(BF))
    summed = around((both(keep_sum, give_sum) + first.astype(F32)).astype(BF))
    return (both(keep, give) + swap(raw).astype(F32) + summed.astype(F32)).astype(BF)


def solution(mesh):
    return jax.shard_map(
        per_device,
        mesh=mesh,
        in_specs=(
            P(("ctx", "tp"), None),
            P(None, "tp"),
            P(),
            P(None, "tp"),
            P(None, "tp"),
            P(),
            P("tp"),
            P("tp"),
            P("tp"),
            P("tp"),
            P("tp", None),
        ),
        out_specs=P(("ctx", "tp"), None),
        check_vma=False,
    )
```

```python
import functools

import jax
import jax.numpy as jnp
from jax import lax
from jax.experimental import pallas as pl
from jax.experimental.pallas import tpu as pltpu
from jax.sharding import PartitionSpec as P

BF = jnp.bfloat16
F32 = jnp.float32
VMEM = pl.BlockSpec(memory_space=pltpu.VMEM)
SMEM = pl.BlockSpec(memory_space=pltpu.SMEM)
LIMIT = 14 * 1024 * 1024

Q = 128
NQ = 4
HH = 8
HD = 64
NS = 128
CH = 512
BCW = 256


def params():
    return pltpu.CompilerParams(vmem_limit_bytes=LIMIT)


def dot_tn(a, b):
    return lax.dot_general(a, b, (((0,), (0,)), ((), ())), preferred_element_type=F32)


def dot_nt(a, b):
    return lax.dot_general(a, b, (((1,), (1,)), ((), ())), preferred_element_type=F32)


def two_parts(v):
    hi = v.astype(BF)
    return hi, (v - hi.astype(F32)).astype(BF)


def head_spread():
    row = lax.broadcasted_iota(jnp.int32, (2 * HH, CH), 0)
    lane = lax.broadcasted_iota(jnp.int32, (2 * HH, CH), 1)
    return jnp.where(lane // HD == row % HH, 1.0, 0.0).astype(BF)


def spread(v, ones):
    hi, lo = two_parts(v)
    both = jnp.concatenate([hi.astype(F32), lo.astype(F32)], 0).astype(BF)
    return dot_tn(both, ones)


def chip():
    return lax.axis_index("tp") // 2


def core():
    return lax.rem(lax.axis_index("tp"), 2)


def in_vmem(v):
    return pltpu.with_memory_space_constraint(v, pltpu.VMEM)


def pack_kernel(far, theirs, first, second, last, mine, sem):
    c = core()
    copy = pltpu.make_async_copy(far, mine, sem)
    copy.start()
    for part, ref in ((1 - c, theirs), (c, mine)):
        if ref is mine:
            copy.wait()
        at = pl.ds(pl.multiple_of(part * 32, 32), 32)
        first[at, :] = ref[pl.ds(pl.multiple_of(c * 32, 32), 32), :]
        second[at, :] = ref[pl.ds(pl.multiple_of((1 - c) * 32, 32), 32), :]
    end = jnp.where(c == 1, mine[48:64].astype(F32), theirs[48:64].astype(F32))
    last[...] = end[8:16].astype(BF)


def pack(mine, theirs):
    return pl.pallas_call(
        pack_kernel,
        out_shape=(pltpu.VMEM((64, 4096), BF), pltpu.VMEM((64, 4096), BF), pltpu.VMEM((8, 4096), BF)),
        in_specs=[pl.BlockSpec(memory_space=pltpu.HBM), VMEM],
        out_specs=(VMEM,) * 3,
        scratch_shapes=[pltpu.VMEM((64, 4096), BF), pltpu.SemaphoreType.DMA],
        compiler_params=params(),
        name="pack",
    )(pltpu.with_memory_space_constraint(mine, pltpu.HBM), in_vmem(theirs))


def half_kernel(mine, theirs, wx, wbc, wdt, xo, bco, dto):
    rows = jnp.concatenate([mine[...], theirs[...]], 0)
    xo[...] = jnp.dot(rows, wx[...], preferred_element_type=F32).astype(BF)
    bco[...] = jnp.dot(rows, wbc[...], preferred_element_type=F32).astype(BF)
    dto[...] = dot_nt(rows, wdt[...])


def project_half(mine, theirs, weights, name):
    return pl.pallas_call(
        half_kernel,
        out_shape=(pltpu.VMEM((Q, CH), BF), pltpu.VMEM((Q, BCW), BF), pltpu.VMEM((Q, HH), F32)),
        in_specs=[VMEM] * 5,
        out_specs=(VMEM, VMEM, VMEM),
        compiler_params=params(),
        name=name,
    )(*[in_vmem(v) for v in (mine, theirs, *weights)])


def near_kernel(mine, theirs, wx_far, wbc_far, wdt_far, xo, bco, dto, wx, wbc, wdt, tok, sems):
    c = core()
    pairs = (
        (mine, tok.at[pl.ds(pl.multiple_of(c * 64, 64), 64), :]),
        (wx_far, wx),
        (wdt_far, wdt),
        (wbc_far, wbc),
    )
    copies = [pltpu.make_async_copy(f, t, sems.at[j]) for j, (f, t) in enumerate(pairs)]
    for copy in copies:
        copy.start()
    tok[pl.ds(pl.multiple_of((1 - c) * 64, 64), 64), :] = theirs[...]
    copies[0].wait()
    copies[1].wait()
    rows = tok[...]
    xo[...] = jnp.dot(rows, wx[...], preferred_element_type=F32).astype(BF)
    copies[2].wait()
    dto[...] = dot_nt(rows, wdt[...])
    copies[3].wait()
    bco[...] = jnp.dot(rows, wbc[...], preferred_element_type=F32).astype(BF)


def project_near(mine, theirs, in_x, in_bc, in_dt):
    hbm = pl.BlockSpec(memory_space=pltpu.HBM)
    far = lambda v: pltpu.with_memory_space_constraint(v, pltpu.HBM)
    return pl.pallas_call(
        near_kernel,
        out_shape=(
            pltpu.VMEM((Q, CH), BF),
            pltpu.VMEM((Q, BCW), BF),
            pltpu.VMEM((Q, HH), F32),
            pltpu.VMEM(in_x.shape, BF),
            pltpu.VMEM(in_bc.shape, BF),
            pltpu.VMEM(in_dt.shape, BF),
        ),
        in_specs=[hbm, VMEM, hbm, hbm, hbm],
        out_specs=(VMEM,) * 6,
        scratch_shapes=[pltpu.VMEM((Q, 4096), BF), pltpu.SemaphoreType.DMA((4,))],
        compiler_params=params(),
        name="project_near",
    )(far(mine), in_vmem(theirs), far(in_x), far(in_bc), far(in_dt))


def silu(v):
    return v / (1.0 + jnp.exp(-v))


def softplus(v):
    return jnp.maximum(v, 0.0) + jnp.log1p(jnp.exp(-jnp.abs(v)))


def column(ref):
    row = lax.broadcasted_iota(jnp.int32, (HH, Q), 0)
    v = jnp.full((HH, Q), ref[0], F32)
    for h in range(1, HH):
        v = jnp.where(row == h, ref[h], v)
    return v


def local_kernel(bias, alog, *refs):
    near, one, two = refs[0:3], refs[3:6], refs[6:9]
    far, far_swap, halo, haloswap = refs[9:13]
    wx, wbc, wdt, kx, kbc = refs[13:18]
    (xo, bo, co, cso, dto, eo, do, send) = refs[18:26]
    ext, extb, dtr = refs[26:29]
    y = chip()
    c = core()
    edge = halo[...].astype(F32) + haloswap[...].astype(F32)
    rows = jnp.concatenate([far[...], far_swap[...], jnp.concatenate([edge, edge], 0).astype(BF)], 0)
    x3 = jnp.dot(rows, wx[...], preferred_element_type=F32).astype(BF).astype(F32)
    bc3 = jnp.dot(rows, wbc[...], preferred_element_type=F32).astype(BF).astype(F32)
    dt3 = dot_nt(rows[0:Q], wdt[...])
    ext[0:8, :] = x3[Q : Q + 8]
    extb[0:8, :] = bc3[Q : Q + 8]

    def put(at, n, px, pbc, pdt):
        ext[pl.ds(pl.multiple_of(at + 8, 8), n), :] = px.astype(F32)
        extb[pl.ds(pl.multiple_of(at + 8, 8), n), :] = pbc.astype(F32)
        dtr[pl.ds(pl.multiple_of(at, 8), n), :] = pdt

    put(y * Q, Q, near[0][...], near[1][...], near[2][...])
    for j in range(4):
        at = lax.rem(y + 2, NQ) * Q + (c, 1 - c)[j // 2] * 32 + (j % 2) * 64
        of = slice(32 * j, 32 * j + 32)
        put(at, 32, x3[of], bc3[of], dt3[of])
    sides = (lax.rem(y + 3 - 2 * c, NQ), lax.rem(y + 1 + 2 * c, NQ))
    for piece, halves in ((one, (c, 1 - c)), (two, (1 - c, c))):
        for j in range(4):
            at = sides[j // 2] * Q + halves[j // 2] * 32 + (j % 2) * 64
            of = slice(32 * j, 32 * j + 32)
            put(at, 32, piece[0][of, :], piece[1][of, :], piece[2][of, :])
    ones = head_spread()
    lane = lax.broadcasted_iota(jnp.int32, (HH, Q), 1)
    decay = -jnp.exp(column(alog))
    bias_col = column(bias)
    total = jnp.zeros((HH, Q), F32)
    state = jnp.zeros((NS, CH), F32)
    for a in range(NQ):
        dt = softplus(dtr[a * Q : (a + 1) * Q, :].T + bias_col)
        cs = decay * dt
        for s in (1, 2, 4, 8, 16, 32, 64):
            cs = cs + jnp.where(lane >= s, pltpu.roll(cs, s, 1), 0.0)
        end = jnp.broadcast_to(cs[:, Q - 1 : Q], (HH, Q))
        dto[a] = dt
        cso[a] = cs
        total = total + end
        v = kbc[0:1, :] * extb[a * Q + 5 : a * Q + 5 + Q, :]
        for j in range(1, 4):
            v = v + kbc[j : j + 1, :] * extb[a * Q + 5 + j : a * Q + 5 + j + Q, :]
        bc = silu(v).astype(BF)
        b = bc[:, :NS]
        bo[a] = b
        co[a] = bc[:, NS:]
        v = kx[0:1, :] * ext[a * Q + 5 : a * Q + 5 + Q, :]
        for j in range(1, 4):
            v = v + kx[j : j + 1, :] * ext[a * Q + 5 + j : a * Q + 5 + j + Q, :]
        x = silu(v)
        xo[a] = x.astype(BF)
        w = spread(dt * jnp.exp(end - cs), ones)
        e = dot_tn(b, (x * w).astype(BF))
        eo[a] = e
        d = spread(jnp.exp(end), ones)[0:8, :]
        do[a] = d
        state = state * d[0:1, :] + e
    st = state.T
    dec = jnp.exp(total)
    hi = dec.astype(BF).astype(F32)
    mid = (dec - hi).astype(BF).astype(F32)
    low = dec - hi - mid
    row = lax.broadcasted_iota(jnp.int32, (HH, Q), 0)
    for h in range(HH):
        p = lambda t: jnp.broadcast_to(t[h : h + 1, :], (8, Q))
        tail = jnp.where(row == 0, p(hi), jnp.where(row == 1, p(mid), jnp.where(row == 2, p(low), 0.0)))
        for q in range(4):
            d = h * 4 + q
            send[d] = jnp.concatenate([st[16 * d : 16 * d + 16, :], tail], 0).astype(BF)


def local_part(bias, alog, *args):
    s = pltpu.VMEM
    return pl.pallas_call(
        local_kernel,
        out_shape=(
            s((NQ, Q, CH), BF),
            s((NQ, Q, NS), BF),
            s((NQ, Q, NS), BF),
            s((NQ, HH, Q), F32),
            s((NQ, HH, Q), F32),
            s((NQ, NS, CH), F32),
            s((NQ, 8, CH), F32),
            s((32, 24, 128), BF),
        ),
        in_specs=[SMEM] * 2 + [VMEM] * 18,
        out_specs=(VMEM,) * 8,
        scratch_shapes=[
            pltpu.VMEM((8 + NQ * Q, CH), F32),
            pltpu.VMEM((8 + NQ * Q, BCW), F32),
            pltpu.VMEM((NQ * Q, HH), F32),
        ],
        compiler_params=params(),
        name="local_part",
    )(bias, alog, *[in_vmem(v) for v in args])


def prefix_kernel(r, o):
    s = jnp.zeros((16, 128), F32)
    for j in range(32):
        o[j] = s.astype(BF)
        v = r[j].astype(F32)
        s = s * (v[16:17] + v[17:18] + v[18:19]) + v[0:16]


def prefix(r):
    return pl.pallas_call(
        prefix_kernel,
        out_shape=pltpu.VMEM((32, 16, 128), BF),
        in_specs=[VMEM],
        out_specs=VMEM,
        compiler_params=params(),
        name="prefix",
    )(in_vmem(r))


def diag_kernel(skip, x, b, c, cs, dt, y):
    t = lax.broadcasted_iota(jnp.int32, (Q, Q), 0)
    u = lax.broadcasted_iota(jnp.int32, (Q, Q), 1)
    tri = t >= u
    left = u < HD
    for a in range(NQ):
        scores = dot_nt(c[a], b[a])
        csr = cs[a]
        csc = csr.T
        dtr = dt[a]
        for p in range(HH // 2):
            xp = x[a, :, 128 * p : 128 * p + 128]
            ms = []
            for h in (2 * p, 2 * p + 1):
                diff = csc[:, h : h + 1] - csr[h : h + 1, :]
                m = scores * jnp.exp(jnp.where(tri, diff, -jnp.inf)) * dtr[h : h + 1, :]
                ms.append(m.astype(BF))
            xf = xp.astype(F32)
            xx = jnp.concatenate([jnp.where(left, xf, 0.0), jnp.where(left, 0.0, xf)], 0).astype(BF)
            yy = jnp.dot(jnp.concatenate(ms, 1), xx, preferred_element_type=F32)
            y[a, :, 128 * p : 128 * p + 128] = yy + jnp.where(left, skip[2 * p], skip[2 * p + 1]) * xf


def diag_part(skip, *args):
    return pl.pallas_call(
        diag_kernel,
        out_shape=pltpu.VMEM((NQ, Q, CH), F32),
        in_specs=[SMEM] + [VMEM] * 5,
        out_specs=VMEM,
        compiler_params=params(),
        name="diag_part",
    )(skip, *[in_vmem(v) for v in args])


def norm_kernel(s_in, e, d, c, cs, ydiag, gain, w_far, other, own, rest, w, nb, sem):
    copy = pltpu.make_async_copy(w_far, w, sem)
    copy.start()
    y = chip()
    mine = core()
    ones = head_spread()
    r = lax.broadcasted_iota(jnp.int32, (Q, Q), 0) // HD
    l = lax.broadcasted_iota(jnp.int32, (Q, Q), 1) // HD
    mean = jnp.where(r == l, 1.0 / HD, 0.0).astype(BF)
    state = s_in[...].astype(F32).T
    for a in range(NQ):
        yst = jnp.dot(c[a], state.astype(BF), preferred_element_type=F32)
        g = spread(jnp.exp(cs[a]), ones)
        v = ydiag[a] + g * yst
        if a < NQ - 1:
            state = state * d[a][0:1, :] + e[a]
        hi, lo = two_parts(v * v)
        for p in range(HH // 2):
            at = slice(128 * p, 128 * p + 128)
            ms = jnp.dot(hi[:, at], mean, preferred_element_type=F32)
            ms = ms + jnp.dot(lo[:, at], mean, preferred_element_type=F32)
            nb[a, :, at] = (v[:, at] * lax.rsqrt(ms + 1e-05) * gain[0:1, at]).astype(BF)

    def half(a, h):
        return nb[a, pl.ds(pl.multiple_of(h * 64, 64), 64), :]

    a = lax.rem(y + 2, NQ)
    v = jnp.concatenate([half(a, 1 - mine), half(a, mine)], 0)
    copy.wait()
    v = jnp.dot(v, w[...], preferred_element_type=F32).astype(BF)
    other[...] = v[0:64]
    own[...] = v[64:128]
    side, across = lax.rem(y + 1 + 2 * mine, NQ), lax.rem(y + 3 - 2 * mine, NQ)
    parts = ((across, mine), (across, 1 - mine), (side, 1 - mine), (side, mine), (y, 1 - mine), (y, mine))
    for j, (a, h) in enumerate(parts):
        rest[64 * j : 64 * j + 64, :] = half(a, h)


def norm_part(*args):
    s = pltpu.VMEM
    return pl.pallas_call(
        norm_kernel,
        out_shape=(s((64, 4096), BF), s((64, 4096), BF), s((384, CH), BF), s((CH, 4096), BF)),
        in_specs=[VMEM] * 7 + [pl.BlockSpec(memory_space=pltpu.HBM)],
        out_specs=(VMEM,) * 4,
        scratch_shapes=[pltpu.VMEM((NQ, Q, CH), BF), pltpu.SemaphoreType.DMA],
        compiler_params=params(),
        name="norm_part",
    )(*[in_vmem(v) for v in args[:7]], pltpu.with_memory_space_constraint(args[7], pltpu.HBM))


def out_kernel(n, w, *outs):
    v = jnp.dot(n[...], w[...], preferred_element_type=F32).astype(BF)
    for j, o in enumerate(outs):
        o[...] = v[64 * j : 64 * j + 64]


def out_part(n, w):
    s = pltpu.VMEM
    return pl.pallas_call(
        out_kernel,
        out_shape=(s((64, 4096), BF),) * 6,
        in_specs=[VMEM] * 2,
        out_specs=(VMEM,) * 6,
        compiler_params=params(),
        name="out_part",
    )(in_vmem(n), in_vmem(w))


SWAP = [(y * 2 + c, y * 2 + 1 - c) for y in range(4) for c in range(2)]


AROUND = [(y * 2 + c, ((y + 1 - 2 * c) % 4) * 2 + c) for y in range(4) for c in range(2)]


def around(v):
    return lax.ppermute(v, "tp", AROUND)


def swap(v):
    return lax.ppermute(v, "tp", SWAP)


def per_device(tokens, in_x, in_bc, in_dt, conv_x, conv_bc, dt_bias, a_log, skip_d, norm_gain, out_w):
    after = lax.optimization_barrier
    partner = swap(tokens)
    first, second, last = pack(tokens, partner)
    r1, r2 = around(first), around(second)
    *piece0, wx, wbc, wdt = project_near(tokens, partner, in_x, in_bc, in_dt.T)
    weights = (wx, wbc, wdt)
    r1, wx, last = after((r1, wx, last))
    far = around(r1)
    spans = lax.axis_size("ctx")

    def onward(*route):
        return lax.ppermute(
            last, ("ctx", "tp"), [(i * 8 + f, i * 8 + 8 + t) for i in range(spans - 1) for f, t in route]
        )

    edge_a, edge_b = onward((7, 7), (6, 1)), onward((7, 5), (6, 3))
    s1, r2 = after((swap(r1), r2))
    piece1 = project_half(r1, s1, weights, "project_one")
    far, r2, *piece1 = after((far, r2, *piece1))
    piece2 = project_half(r2, swap(r2), weights, "project_two")
    edge_a, edge_b, far = after((edge_a, edge_b, far))
    edge = edge_a + edge_b
    edges = swap(edge)

    xc, b, c, cs, dt, e, d, send = local_part(
        dt_bias, a_log, *piece0, *piece1, *piece2, far, swap(far), edge, edges, *weights, conv_x, conv_bc
    )
    got = lax.all_to_all(send, "ctx", 0, 0, tiled=True)
    ydiag = diag_part(skip_d, xc, b, c, cs, dt)
    back = lax.all_to_all(prefix(got), "ctx", 0, 0, tiled=True)
    other, own, rest, w = norm_part(back.reshape(CH, NS), e, d, c, cs, ydiag, norm_gain[None, :], out_w)

    def both(mine, theirs):
        return mine.astype(F32) + swap(theirs).astype(F32)

    q2 = both(own, other).astype(BF)
    give_raw, give_sum, keep_raw, keep_sum, give, keep = out_part(rest, w)
    q2, give_raw, give_sum, give = after((q2, give_raw, give_sum, give))
    first = around(q2)
    raw = around(both(keep_raw, give_raw).astype(BF))
    summed = around((both(keep_sum, give_sum) + first.astype(F32)).astype(BF))
    return (both(keep, give) + swap(raw).astype(F32) + summed.astype(F32)).astype(BF)


def solution(mesh):
    return jax.shard_map(
        per_device,
        mesh=mesh,
        in_specs=(
            P(("ctx", "tp"), None),
            P(None, "tp"),
            P(),
            P(None, "tp"),
            P(None, "tp"),
            P(),
            P("tp"),
            P("tp"),
            P("tp"),
            P("tp"),
            P("tp", None),
        ),
        out_specs=P(("ctx", "tp"), None),
        check_vma=False,
    )
```

```python
import functools

import jax
import jax.numpy as jnp
from jax import lax
from jax.experimental import pallas as pl
from jax.experimental.pallas import tpu as pltpu
from jax.sharding import PartitionSpec as P

BF = jnp.bfloat16
F32 = jnp.float32
VMEM = pl.BlockSpec(memory_space=pltpu.VMEM)
SMEM = pl.BlockSpec(memory_space=pltpu.SMEM)
LIMIT = 14 * 1024 * 1024

Q = 128
NQ = 4
HH = 8
HD = 64
NS = 128
CH = 512
BCW = 256


def params():
    return pltpu.CompilerParams(vmem_limit_bytes=LIMIT)


def dot_tn(a, b):
    return lax.dot_general(a, b, (((0,), (0,)), ((), ())), preferred_element_type=F32)


def dot_nt(a, b):
    return lax.dot_general(a, b, (((1,), (1,)), ((), ())), preferred_element_type=F32)


def two_parts(v):
    hi = v.astype(BF)
    return hi, (v - hi.astype(F32)).astype(BF)


def head_spread():
    row = lax.broadcasted_iota(jnp.int32, (2 * HH, CH), 0)
    lane = lax.broadcasted_iota(jnp.int32, (2 * HH, CH), 1)
    return jnp.where(lane // HD == row % HH, 1.0, 0.0).astype(BF)


def spread(v, ones):
    hi, lo = two_parts(v)
    both = jnp.concatenate([hi.astype(F32), lo.astype(F32)], 0).astype(BF)
    return dot_tn(both, ones)


def chip():
    return lax.axis_index("tp") // 2


def core():
    return lax.rem(lax.axis_index("tp"), 2)


def in_vmem(v):
    return pltpu.with_memory_space_constraint(v, pltpu.VMEM)


def pack_kernel(far, theirs, first, second, last, mine, sem):
    c = core()
    copy = pltpu.make_async_copy(far, mine, sem)
    copy.start()
    for part, ref in ((1 - c, theirs), (c, mine)):
        if ref is mine:
            copy.wait()
        at = pl.ds(pl.multiple_of(part * 32, 32), 32)
        first[at, :] = ref[pl.ds(pl.multiple_of(c * 32, 32), 32), :]
        second[at, :] = ref[pl.ds(pl.multiple_of((1 - c) * 32, 32), 32), :]
    end = jnp.where(c == 1, mine[48:64].astype(F32), theirs[48:64].astype(F32))
    last[...] = end[8:16].astype(BF)


def pack(mine, theirs):
    return pl.pallas_call(
        pack_kernel,
        out_shape=(pltpu.VMEM((64, 4096), BF), pltpu.VMEM((64, 4096), BF), pltpu.VMEM((8, 4096), BF)),
        in_specs=[pl.BlockSpec(memory_space=pltpu.HBM), VMEM],
        out_specs=(VMEM,) * 3,
        scratch_shapes=[pltpu.VMEM((64, 4096), BF), pltpu.SemaphoreType.DMA],
        compiler_params=params(),
        name="pack",
    )(pltpu.with_memory_space_constraint(mine, pltpu.HBM), in_vmem(theirs))


def half_kernel(mine, theirs, wx, wbc, wdt, xo, bco, dto):
    rows = jnp.concatenate([mine[...], theirs[...]], 0)
    xo[...] = jnp.dot(rows, wx[...], preferred_element_type=F32).astype(BF)
    bco[...] = jnp.dot(rows, wbc[...], preferred_element_type=F32).astype(BF)
    dto[...] = dot_nt(rows, wdt[...])


def project_half(mine, theirs, weights, name):
    return pl.pallas_call(
        half_kernel,
        out_shape=(pltpu.VMEM((Q, CH), BF), pltpu.VMEM((Q, BCW), BF), pltpu.VMEM((Q, HH), F32)),
        in_specs=[VMEM] * 5,
        out_specs=(VMEM, VMEM, VMEM),
        compiler_params=params(),
        name=name,
    )(*[in_vmem(v) for v in (mine, theirs, *weights)])


def near_kernel(mine, theirs, wx_far, wbc_far, wdt_far, xo, bco, dto, wx, wbc, wdt, tok, sems):
    c = core()
    pairs = (
        (mine, tok.at[pl.ds(pl.multiple_of(c * 64, 64), 64), :]),
        (wx_far, wx),
        (wdt_far, wdt),
        (wbc_far, wbc),
    )
    copies = [pltpu.make_async_copy(f, t, sems.at[j]) for j, (f, t) in enumerate(pairs)]
    for copy in copies:
        copy.start()
    tok[pl.ds(pl.multiple_of((1 - c) * 64, 64), 64), :] = theirs[...]
    copies[0].wait()
    copies[1].wait()
    rows = tok[...]
    xo[...] = jnp.dot(rows, wx[...], preferred_element_type=F32).astype(BF)
    copies[2].wait()
    dto[...] = dot_nt(rows, wdt[...])
    copies[3].wait()
    bco[...] = jnp.dot(rows, wbc[...], preferred_element_type=F32).astype(BF)


def project_near(mine, theirs, in_x, in_bc, in_dt):
    hbm = pl.BlockSpec(memory_space=pltpu.HBM)
    far = lambda v: pltpu.with_memory_space_constraint(v, pltpu.HBM)
    return pl.pallas_call(
        near_kernel,
        out_shape=(
            pltpu.VMEM((Q, CH), BF),
            pltpu.VMEM((Q, BCW), BF),
            pltpu.VMEM((Q, HH), F32),
            pltpu.VMEM(in_x.shape, BF),
            pltpu.VMEM(in_bc.shape, BF),
            pltpu.VMEM(in_dt.shape, BF),
        ),
        in_specs=[hbm, VMEM, hbm, hbm, hbm],
        out_specs=(VMEM,) * 6,
        scratch_shapes=[pltpu.VMEM((Q, 4096), BF), pltpu.SemaphoreType.DMA((4,))],
        compiler_params=params(),
        name="project_near",
    )(far(mine), in_vmem(theirs), far(in_x), far(in_bc), far(in_dt))


def silu(v):
    return v / (1.0 + jnp.exp(-v))


def softplus(v):
    return jnp.maximum(v, 0.0) + jnp.log1p(jnp.exp(-jnp.abs(v)))


def column(ref):
    row = lax.broadcasted_iota(jnp.int32, (HH, Q), 0)
    v = jnp.full((HH, Q), ref[0], F32)
    for h in range(1, HH):
        v = jnp.where(row == h, ref[h], v)
    return v


def local_kernel(bias, alog, *refs):
    near, one, two = refs[0:3], refs[3:6], refs[6:9]
    far, far_swap, halo, haloswap = refs[9:13]
    wx, wbc, wdt, kx, kbc = refs[13:18]
    (xo, bo, co, cso, dto, eo, do, send) = refs[18:26]
    ext, extb, dtr = refs[26:29]
    y = chip()
    c = core()
    edge = halo[...].astype(F32) + haloswap[...].astype(F32)
    rows = jnp.concatenate([far[...], far_swap[...], jnp.concatenate([edge, edge], 0).astype(BF)], 0)
    x3 = jnp.dot(rows, wx[...], preferred_element_type=F32).astype(BF).astype(F32)
    bc3 = jnp.dot(rows, wbc[...], preferred_element_type=F32).astype(BF).astype(F32)
    dt3 = dot_nt(rows[0:Q], wdt[...])
    ext[0:8, :] = x3[Q : Q + 8]
    extb[0:8, :] = bc3[Q : Q + 8]

    def put(at, n, px, pbc, pdt):
        ext[pl.ds(pl.multiple_of(at + 8, 8), n), :] = px.astype(F32)
        extb[pl.ds(pl.multiple_of(at + 8, 8), n), :] = pbc.astype(F32)
        dtr[pl.ds(pl.multiple_of(at, 8), n), :] = pdt

    put(y * Q, Q, near[0][...], near[1][...], near[2][...])
    for j in range(4):
        at = lax.rem(y + 2, NQ) * Q + (c, 1 - c)[j // 2] * 32 + (j % 2) * 64
        of = slice(32 * j, 32 * j + 32)
        put(at, 32, x3[of], bc3[of], dt3[of])
    sides = (lax.rem(y + 3 - 2 * c, NQ), lax.rem(y + 1 + 2 * c, NQ))
    for piece, halves in ((one, (c, 1 - c)), (two, (1 - c, c))):
        for j in range(4):
            at = sides[j // 2] * Q + halves[j // 2] * 32 + (j % 2) * 64
            of = slice(32 * j, 32 * j + 32)
            put(at, 32, piece[0][of, :], piece[1][of, :], piece[2][of, :])
    ones = head_spread()
    lane = lax.broadcasted_iota(jnp.int32, (HH, Q), 1)
    decay = -jnp.exp(column(alog))
    bias_col = column(bias)
    total = jnp.zeros((HH, Q), F32)
    state = jnp.zeros((NS, CH), F32)
    for a in range(NQ):
        dt = softplus(dtr[a * Q : (a + 1) * Q, :].T + bias_col)
        cs = decay * dt
        for s in (1, 2, 4, 8, 16, 32, 64):
            cs = cs + jnp.where(lane >= s, pltpu.roll(cs, s, 1), 0.0)
        end = jnp.broadcast_to(cs[:, Q - 1 : Q], (HH, Q))
        dto[a] = dt
        cso[a] = cs
        total = total + end
        v = kbc[0:1, :] * extb[a * Q + 5 : a * Q + 5 + Q, :]
        for j in range(1, 4):
            v = v + kbc[j : j + 1, :] * extb[a * Q + 5 + j : a * Q + 5 + j + Q, :]
        bc = silu(v).astype(BF)
        b = bc[:, :NS]
        bo[a] = b
        co[a] = bc[:, NS:]
        v = kx[0:1, :] * ext[a * Q + 5 : a * Q + 5 + Q, :]
        for j in range(1, 4):
            v = v + kx[j : j + 1, :] * ext[a * Q + 5 + j : a * Q + 5 + j + Q, :]
        x = silu(v)
        xo[a] = x.astype(BF)
        w = spread(dt * jnp.exp(end - cs), ones)
        e = dot_tn(b, (x * w).astype(BF))
        eo[a] = e
        d = spread(jnp.exp(end), ones)[0:8, :]
        do[a] = d
        state = state * d[0:1, :] + e
    st = state.T
    dec = jnp.exp(total)
    hi = dec.astype(BF).astype(F32)
    mid = (dec - hi).astype(BF).astype(F32)
    low = dec - hi - mid
    row = lax.broadcasted_iota(jnp.int32, (HH, Q), 0)
    for h in range(HH):
        p = lambda t: jnp.broadcast_to(t[h : h + 1, :], (8, Q))
        tail = jnp.where(row == 0, p(hi), jnp.where(row == 1, p(mid), jnp.where(row == 2, p(low), 0.0)))
        for q in range(4):
            d = h * 4 + q
            send[d] = jnp.concatenate([st[16 * d : 16 * d + 16, :], tail], 0).astype(BF)


def local_part(bias, alog, *args):
    s = pltpu.VMEM
    return pl.pallas_call(
        local_kernel,
        out_shape=(
            s((NQ, Q, CH), BF),
            s((NQ, Q, NS), BF),
            s((NQ, Q, NS), BF),
            s((NQ, HH, Q), F32),
            s((NQ, HH, Q), F32),
            s((NQ, NS, CH), F32),
            s((NQ, 8, CH), F32),
            s((32, 24, 128), BF),
        ),
        in_specs=[SMEM] * 2 + [VMEM] * 18,
        out_specs=(VMEM,) * 8,
        scratch_shapes=[
            pltpu.VMEM((8 + NQ * Q, CH), F32),
            pltpu.VMEM((8 + NQ * Q, BCW), F32),
            pltpu.VMEM((NQ * Q, HH), F32),
        ],
        compiler_params=params(),
        name="local_part",
    )(bias, alog, *[in_vmem(v) for v in args])


def prefix_kernel(r, o):
    s = jnp.zeros((16, 128), F32)
    for j in range(32):
        o[j] = s.astype(BF)
        v = r[j].astype(F32)
        s = s * (v[16:17] + v[17:18] + v[18:19]) + v[0:16]


def prefix(r):
    return pl.pallas_call(
        prefix_kernel,
        out_shape=pltpu.VMEM((32, 16, 128), BF),
        in_specs=[VMEM],
        out_specs=VMEM,
        compiler_params=params(),
        name="prefix",
    )(in_vmem(r))


def diag_kernel(skip, x, b, c, cs, dt, y):
    t = lax.broadcasted_iota(jnp.int32, (Q, Q), 0)
    u = lax.broadcasted_iota(jnp.int32, (Q, Q), 1)
    tri = t >= u
    left = u < HD
    for a in range(NQ):
        scores = dot_nt(c[a], b[a])
        csr = cs[a]
        csc = csr.T
        dtr = dt[a]
        for p in range(HH // 2):
            xp = x[a, :, 128 * p : 128 * p + 128]
            ms = []
            for h in (2 * p, 2 * p + 1):
                diff = csc[:, h : h + 1] - csr[h : h + 1, :]
                m = scores * jnp.exp(jnp.where(tri, diff, -jnp.inf)) * dtr[h : h + 1, :]
                ms.append(m.astype(BF))
            xf = xp.astype(F32)
            xx = jnp.concatenate([jnp.where(left, xf, 0.0), jnp.where(left, 0.0, xf)], 0).astype(BF)
            yy = jnp.dot(jnp.concatenate(ms, 1), xx, preferred_element_type=F32)
            y[a, :, 128 * p : 128 * p + 128] = yy + jnp.where(left, skip[2 * p], skip[2 * p + 1]) * xf


def diag_part(skip, *args):
    return pl.pallas_call(
        diag_kernel,
        out_shape=pltpu.VMEM((NQ, Q, CH), F32),
        in_specs=[SMEM] + [VMEM] * 5,
        out_specs=VMEM,
        compiler_params=params(),
        name="diag_part",
    )(skip, *[in_vmem(v) for v in args])


def norm_kernel(s_in, e, d, c, cs, ydiag, gain, w_far, other, own, rest, w, nb, sem):
    copy = pltpu.make_async_copy(w_far, w, sem)
    copy.start()
    y = chip()
    mine = core()
    ones = head_spread()
    r = lax.broadcasted_iota(jnp.int32, (Q, Q), 0) // HD
    l = lax.broadcasted_iota(jnp.int32, (Q, Q), 1) // HD
    mean = jnp.where(r == l, 1.0 / HD, 0.0).astype(BF)
    state = s_in[...].astype(F32).T
    for a in range(NQ):
        yst = jnp.dot(c[a], state.astype(BF), preferred_element_type=F32)
        g = spread(jnp.exp(cs[a]), ones)
        v = ydiag[a] + g * yst
        if a < NQ - 1:
            state = state * d[a][0:1, :] + e[a]
        hi, lo = two_parts(v * v)
        for p in range(HH // 2):
            at = slice(128 * p, 128 * p + 128)
            ms = jnp.dot(hi[:, at], mean, preferred_element_type=F32)
            ms = ms + jnp.dot(lo[:, at], mean, preferred_element_type=F32)
            nb[a, :, at] = (v[:, at] * lax.rsqrt(ms + 1e-05) * gain[0:1, at]).astype(BF)

    def half(a, h):
        return nb[a, pl.ds(pl.multiple_of(h * 64, 64), 64), :]

    a = lax.rem(y + 2, NQ)
    v = jnp.concatenate([half(a, 1 - mine), half(a, mine)], 0)
    copy.wait()
    v = jnp.dot(v, w[...], preferred_element_type=F32).astype(BF)
    other[...] = v[0:64]
    own[...] = v[64:128]
    side, across = lax.rem(y + 1 + 2 * mine, NQ), lax.rem(y + 3 - 2 * mine, NQ)
    parts = ((across, mine), (across, 1 - mine), (side, 1 - mine), (side, mine), (y, 1 - mine), (y, mine))
    for j, (a, h) in enumerate(parts):
        rest[64 * j : 64 * j + 64, :] = half(a, h)


def norm_part(*args):
    s = pltpu.VMEM
    return pl.pallas_call(
        norm_kernel,
        out_shape=(s((64, 4096), BF), s((64, 4096), BF), s((384, CH), BF), s((CH, 4096), BF)),
        in_specs=[VMEM] * 7 + [pl.BlockSpec(memory_space=pltpu.HBM)],
        out_specs=(VMEM,) * 4,
        scratch_shapes=[pltpu.VMEM((NQ, Q, CH), BF), pltpu.SemaphoreType.DMA],
        compiler_params=params(),
        name="norm_part",
    )(*[in_vmem(v) for v in args[:7]], pltpu.with_memory_space_constraint(args[7], pltpu.HBM))


def out_kernel(n, w, *outs):
    v = jnp.dot(n[...], w[...], preferred_element_type=F32).astype(BF)
    for j, o in enumerate(outs):
        o[...] = v[64 * j : 64 * j + 64]


def out_part(n, w):
    s = pltpu.VMEM
    return pl.pallas_call(
        out_kernel,
        out_shape=(s((64, 4096), BF),) * 6,
        in_specs=[VMEM] * 2,
        out_specs=(VMEM,) * 6,
        compiler_params=params(),
        name="out_part",
    )(in_vmem(n), in_vmem(w))


SWAP = [(y * 2 + c, y * 2 + 1 - c) for y in range(4) for c in range(2)]


AROUND = [(y * 2 + c, ((y + 1 - 2 * c) % 4) * 2 + c) for y in range(4) for c in range(2)]


def around(v):
    return lax.ppermute(v, "tp", AROUND)


def swap(v):
    return lax.ppermute(v, "tp", SWAP)


def per_device(tokens, in_x, in_bc, in_dt, conv_x, conv_bc, dt_bias, a_log, skip_d, norm_gain, out_w):
    after = lax.optimization_barrier
    partner = swap(tokens)
    first, second, last = pack(tokens, partner)
    r1, r2 = around(first), around(second)
    *piece0, wx, wbc, wdt = project_near(tokens, partner, in_x, in_bc, in_dt.T)
    weights = (wx, wbc, wdt)
    r1, wx, last = after((r1, wx, last))
    far = around(r1)
    spans = lax.axis_size("ctx")

    def onward(*route):
        return lax.ppermute(
            last, ("ctx", "tp"), [(i * 8 + f, i * 8 + 8 + t) for i in range(spans - 1) for f, t in route]
        )

    edge_a, edge_b = onward((7, 7), (6, 1)), onward((7, 5), (6, 3))
    s1, r2 = after((swap(r1), r2))
    piece1 = project_half(r1, s1, weights, "project_one")
    r2, edge_a, edge_b, *piece1 = after((r2, edge_a, edge_b, *piece1))
    far, s2 = after((far, swap(r2)))
    piece2 = project_half(r2, s2, weights, "project_two")
    edge = edge_a + edge_b
    edges = swap(edge)

    xc, b, c, cs, dt, e, d, send = local_part(
        dt_bias, a_log, *piece0, *piece1, *piece2, far, swap(far), edge, edges, *weights, conv_x, conv_bc
    )
    got = lax.all_to_all(send, "ctx", 0, 0, tiled=True)
    ydiag = diag_part(skip_d, xc, b, c, cs, dt)
    back = lax.all_to_all(prefix(got), "ctx", 0, 0, tiled=True)
    other, own, rest, w = norm_part(back.reshape(CH, NS), e, d, c, cs, ydiag, norm_gain[None, :], out_w)

    def both(mine, theirs):
        return mine.astype(F32) + swap(theirs).astype(F32)

    q2 = both(own, other).astype(BF)
    give_raw, give_sum, keep_raw, keep_sum, give, keep = out_part(rest, w)
    q2, give_raw, give_sum, give = after((q2, give_raw, give_sum, give))
    first = around(q2)
    raw = around(both(keep_raw, give_raw).astype(BF))
    summed = around((both(keep_sum, give_sum) + first.astype(F32)).astype(BF))
    return (both(keep, give) + swap(raw).astype(F32) + summed.astype(F32)).astype(BF)


def solution(mesh):
    return jax.shard_map(
        per_device,
        mesh=mesh,
        in_specs=(
            P(("ctx", "tp"), None),
            P(None, "tp"),
            P(),
            P(None, "tp"),
            P(None, "tp"),
            P(),
            P("tp"),
            P("tp"),
            P("tp"),
            P("tp"),
            P("tp", None),
        ),
        out_specs=P(("ctx", "tp"), None),
        check_vma=False,
    )
```
